32 devices in a mesh: band: 8 (over z, y), lon: 4 (over x, core).
Axes of the slice: x: 2, y: 2, z: 4, core: 2. Of those that a mesh axis runs over, the one named last changes fastest.
Arguments:
- source: bfloat16 [4096, 8, 128], P(('band', 'lon')), may hold values from -6 to 6
- routes: int32 [4096, 2], P(('band', 'lon')), may hold values from 0 to 11, as said below
- slot_weights: bfloat16 [32, 12, 32, 128, 128], P(('band', 'lon')), may hold values from -0.5 to 0.5
- window: int32 [32, 12, 32], P(('band', 'lon')), may hold values from 0 to 255
- stem_weight: bfloat16 [9, 8, 128], replicated, may hold values from -0.75 to 0.75
- stem_bias: float32 [128], replicated, may hold values from -3 to 3
- mix_weight: bfloat16 [9, 128, 128], replicated, may hold values from -0.1875 to 0.1875
- mix_bias: float32 [128], replicated, may hold values from -3 to 3
Outputs:
- features: bfloat16 [512, 2048, 128], P('band', 'lon')
The draws below stay inside these ranges and needn't reach their ends.
Inputs may be any that keep to these rules, and one draw needn't show every extreme that they name: `routes`: each cell block names 2 different codes, never a band outside the grid. Among one device's blocks no code is named more than 32 times, and the device's own tile (code 4) exactly 32 times except in the first and last band. A device of another band names only longitude offsets 0, 1 and 3. A device of the first band names each code of band offsets 0 and +1 exactly 32 times; one of the last band each code of band offsets -1 and 0 exactly 32 times.
All inputs are finite; a program needn't handle non-finite values.
Results may differ from the reference program's by a relative error of at most 0.0056.
Values may be sent and summed in bfloat16 or wider, within the bound.
No kernel may reach another device: no remote copies, remote signals or barrier semaphores. Data moves between devices by JAX's collectives and lax.ppermute only.
A program may use at most 128 MiB of HBM per device.

```python
import jax
import jax.numpy as jnp
from jax import lax

F = 8
CH = 128
CB = 128
PIX = 128
TOP = 2
ROWS_DEV = 64
COLS_DEV = 512
NBR = 12
BLK_DEV = 128
CAP = 32
NWIN = 256
TOTAL_BLK = 4096
LAT = 512
LONG = 2048
N_BAND = 8
N_LON = 4
DEVICES = 32


def draw_routes(key, part):
    devices = DEVICES
    n_band = devices // N_LON
    nbr = 3 * N_LON
    entries = BLK_DEV * TOP
    key_picks = jax.random.fold_in(key, 11)
    key_flip = jax.random.fold_in(key, 12)
    key_order = jax.random.fold_in(key, 13)
    device_ids = jnp.arange(devices, dtype=jnp.int32)
    band = device_ids // N_LON
    code = jnp.arange(nbr, dtype=jnp.int32)
    offset_band = code // N_LON - 1
    offset_lon = code % N_LON
    near = (offset_lon == 0) | (offset_lon == 1) | (offset_lon == N_LON - 1)
    others = near & (code != N_LON)
    other_index = jnp.cumsum(others.astype(jnp.int32)) - 1
    picks = jax.random.randint(key_picks, (devices, CAP), 0, 8, dtype=jnp.int32)
    matches = (picks[:, :, None] == other_index[None, None, :]) & others[None, None, :]
    taken = jnp.sum(matches.astype(jnp.int32), axis=1)
    interior = jnp.where(near, CAP, 0).astype(jnp.int32)[None, :] - taken
    first_band = jnp.where(offset_band >= 0, CAP, 0).astype(jnp.int32)
    last_band = jnp.where(offset_band <= 0, CAP, 0).astype(jnp.int32)
    counts = jnp.where((band == 0)[:, None], first_band[None, :], jnp.where((band == n_band - 1)[:, None], last_band[None, :], interior))
    bounds = jnp.cumsum(counts, axis=1)
    entry = jnp.arange(entries, dtype=jnp.int32)
    ordered = jnp.sum((bounds[:, None, :] <= entry[None, :, None]).astype(jnp.int32), axis=2)
    paired = jnp.stack([ordered[:, :BLK_DEV], ordered[:, BLK_DEV:]], axis=2)
    flip = jax.random.randint(key_flip, (devices, BLK_DEV), 0, 2, dtype=jnp.int32)
    paired = jnp.where((flip == 1)[:, :, None], paired[:, :, ::-1], paired)
    scores = jax.random.randint(key_order, (devices, BLK_DEV), 0, 1 << 20, dtype=jnp.int32) * BLK_DEV + jnp.arange(BLK_DEV, dtype=jnp.int32)[None, :]
    order = jnp.argsort(scores, axis=1)
    paired = jnp.take_along_axis(paired, order[:, :, None], axis=1)
    return paired.reshape(devices * BLK_DEV, TOP).astype(jnp.int32)


def touch_ends(values, own_key, low, high):
    extent = values.shape
    spot = [jax.random.randint(jax.random.fold_in(own_key, axis), (), 0, extent[axis]) for axis in range(len(extent))]
    values = values.at[tuple(spot)].set(low)
    longest = extent.index(max(extent))
    spot[longest] = (spot[longest] + 1) % extent[longest]
    return values.at[tuple(spot)].set(high)


def steps_of(rng, shape, split, low, high):
    def one(position, parts):
        heights = jax.random.uniform(jax.random.fold_in(jax.random.fold_in(rng, 6), position), (parts,), jnp.float32, low / len(split), high / len(split))
        return jnp.repeat(jnp.exp(heights), shape[position] // parts).reshape((-1,) + (1,) * (len(shape) - position - 1))

    level = one(*split[0])
    for cut in split[1:]:
        level = level * one(*cut)
    return level


def bell_draw(own_key, extent, scale, most, split=(), held_as=jnp.bfloat16):
    drawn = jax.random.normal(own_key, extent, jnp.float32) * scale
    if len(split) > 0:
        drawn = steps_of(own_key, extent, split, -0.22, 0.18) * drawn
    return jnp.clip(drawn, min=-most, max=most).astype(held_as)


def setup_inputs(seed: int = 0) -> dict:
    streams_of = jax.random.split(jax.random.key(seed), 9)
    source = bell_draw(streams_of[0], (TOTAL_BLK, F, CB), 1.0, 6.0, ((0, 32),))
    routes = draw_routes(jax.random.fold_in(streams_of[8], 71), 0)
    slot_weights = bell_draw(streams_of[2], (DEVICES, NBR, CAP, CB, PIX), CB ** -0.5, 0.5, ((0, 32),))
    window = touch_ends(jax.random.randint(streams_of[3], (DEVICES, NBR, CAP), 0, NWIN), jax.random.fold_in(streams_of[3], 1), 0, NWIN - 1).astype(jnp.int32)
    stem_weight = bell_draw(streams_of[4], (9, F, CH), (9 * F) ** -0.5, 0.75)
    stem_bias = bell_draw(streams_of[5], (CH,), 0.5, 3.0, (), jnp.float32)
    mix_weight = bell_draw(streams_of[6], (9, CH, CH), (9 * CH) ** -0.5, 0.1875)
    mix_bias = bell_draw(streams_of[7], (CH,), 0.5, 3.0, (), jnp.float32)
    return dict(source=source, routes=routes, slot_weights=slot_weights, window=window, stem_weight=stem_weight, stem_bias=stem_bias, mix_weight=mix_weight, mix_bias=mix_bias)


def reference(source, routes, slot_weights, window, stem_weight, stem_bias, mix_weight, mix_bias):
    devices = N_BAND * N_LON
    nbr = 3 * N_LON
    entries = BLK_DEV * TOP
    blocks = source.reshape(devices, BLK_DEV, F * CB)
    codes = routes.reshape(devices, entries)

    def pack(pair):
        dest, blk = pair
        onehot = (dest[:, None] == jnp.arange(nbr, dtype=jnp.int32)[None, :]).astype(jnp.int32)
        before = jnp.cumsum(onehot, axis=0) - onehot
        rank = jnp.sum(before * onehot, axis=1)
        slot = dest * CAP + rank
        select = (jnp.arange(nbr * CAP, dtype=jnp.int32)[:, None] == slot[None, :]).astype(jnp.bfloat16)
        repeated = jnp.repeat(blk, TOP, axis=0)
        return jnp.dot(select, repeated, preferred_element_type=jnp.float32).astype(jnp.bfloat16)

    outgoing = lax.map(pack, (codes, blocks)).reshape(devices, nbr, CAP, F * CB)

    def one_tile(target):
        band_t = target // N_LON
        lon_t = target % N_LON
        code = jnp.arange(nbr, dtype=jnp.int32)
        src_band = band_t - (code // N_LON - 1)
        src_lon = (lon_t - code % N_LON) % N_LON
        valid = (src_band >= 0) & (src_band < N_BAND)
        src = (jnp.clip(src_band, 0, N_BAND - 1) * N_LON + src_lon).astype(jnp.int32)
        incoming = outgoing[src, code]
        incoming = jnp.where(valid[:, None, None], incoming, jnp.zeros_like(incoming))
        incoming = incoming.reshape(nbr, CAP, F, CB).astype(jnp.float32)
        weights = slot_weights[target].astype(jnp.float32)
        contrib = jnp.einsum('qcfk,qckp->qcfp', incoming, weights).astype(jnp.bfloat16)
        place = (jnp.arange(NWIN, dtype=jnp.int32)[:, None] == window[target].reshape(-1)[None, :]).astype(jnp.bfloat16)
        summed = jnp.dot(place, contrib.reshape(nbr * CAP, F * PIX), preferred_element_type=jnp.float32)
        tile = summed.reshape(ROWS_DEV, COLS_DEV // PIX, F, PIX).transpose(2, 0, 1, 3)
        return tile.reshape(F, ROWS_DEV, COLS_DEV).astype(jnp.bfloat16)

    tiles = lax.map(one_tile, jnp.arange(devices, dtype=jnp.int32))
    field = tiles.reshape(N_BAND, N_LON, F, ROWS_DEV, COLS_DEV).transpose(2, 0, 3, 1, 4).reshape(F, LAT, LONG)
    padded = jnp.pad(field, ((0, 0), (2, 2), (0, 0)))
    padded = jnp.concatenate([padded[:, :, -2:], padded, padded[:, :, :2]], axis=2)
    stem_f = stem_weight.astype(jnp.float32)

    def one_band(band_index):
        piece = lax.dynamic_slice_in_dim(padded, band_index * ROWS_DEV, ROWS_DEV + 4, axis=1).astype(jnp.float32)
        total = jnp.zeros((ROWS_DEV + 2, LONG + 2, CH), jnp.float32)
        for tap in range(9):
            a, b = tap // 3, tap % 3
            total = total + jnp.einsum('fhw,fc->hwc', piece[:, a:a + ROWS_DEV + 2, b:b + LONG + 2], stem_f[tap])
        hidden = jax.nn.silu(total + stem_bias)
        rows = band_index * ROWS_DEV - 1 + jnp.arange(ROWS_DEV + 2, dtype=jnp.int32)
        valid = (rows >= 0) & (rows < LAT)
        hidden = jnp.where(valid[:, None, None], hidden, 0.0).astype(jnp.bfloat16)
        result = jnp.zeros((ROWS_DEV, LONG, CH), jnp.float32)
        for tap in range(9):
            a, b = tap // 3, tap % 3
            result = result + jnp.dot(hidden[a:a + ROWS_DEV, b:b + LONG], mix_weight[tap], preferred_element_type=jnp.float32)
        return (result + mix_bias).astype(jnp.bfloat16)

    bands = lax.map(one_band, jnp.arange(N_BAND, dtype=jnp.int32))
    return bands.reshape(LAT, LONG, CH)
```

```python
import functools

import jax
import jax.numpy as jnp
from jax import lax
from jax.experimental import pallas as pl
from jax.experimental.pallas import tpu as pltpu
from jax.sharding import PartitionSpec as P

ROWS = 64
COLS = 512
PAIRS = COLS // 2
HROWS = 264
LANES = 384
STEP = 6
BLOCKS = (ROWS + 2) // STEP
SCALE = 1.0 / 2.0
BF = jnp.bfloat16
F32 = jnp.float32
VM = pl.BlockSpec(memory_space=pltpu.VMEM)
SM = pl.BlockSpec(memory_space=pltpu.SMEM)
ANY = pl.BlockSpec(memory_space=pl.ANY)


def params(mib):
    return pltpu.CompilerParams(vmem_limit_bytes=mib << 20)


def cost(flops, size):
    return pl.CostEstimate(flops=flops, bytes_accessed=size, transcendentals=0)


def swap_core(n_band, n_lon):
    return [(b * n_lon + l, b * n_lon + (l ^ 1)) for b in range(n_band) for l in range(n_lon)]


def swap_x(n_band, n_lon):
    return [(b * n_lon + l, b * n_lon + n_lon - 1 - l) for b in range(n_band) for l in range(n_lon)]


def swap_a(n_band, n_lon):
    return [(b * n_lon + l, (b ^ 1) * n_lon + l) for b in range(n_band) for l in range(n_lon)]


def swap_b(n_band, n_lon, across):
    pairs = []
    for b in range(n_band):
        partner = b + 1 if b % 2 else b - 1
        for l in range(n_lon):
            if 0 <= partner < n_band:
                pairs.append((b * n_lon + l, partner * n_lon + l))
            elif across:
                pairs.append((b * n_lon + l, b * n_lon + (l + 2) % n_lon))
    return pairs


def swap_far(n_band, n_lon):
    pairs = []
    for b, c in ((0, 1), (1, 0), (n_band - 1, n_band - 2), (n_band - 2, n_band - 1)):
        pairs += [(b * n_lon + l, c * n_lon + (l + 2) % n_lon) for l in range(n_lon)]
    return pairs


def pack_kernel(pos_ref, routes_ref, src_ref, own_ref, core_ref, x_ref, far_ref, buf, table, count):
    band = pos_ref[0]
    lon = pos_ref[1]
    a_dir = 1 - 2 * (band % 2)
    core_dl = 1 + 2 * (lon % 2)
    for q in range(12):
        db, dl = q // 4 - 1, q % 4
        if db == 0:
            way = 1
        else:
            way = jnp.where(a_dir == db, 0, 2)
        if dl == 0:
            group = way
        elif dl == 2:
            group = 2 if db == 0 else 9
        else:
            group = jnp.where(core_dl == dl, 3, 6) + way
        table[q] = group * 32
        count[q] = 0
    buf[...] = jnp.zeros_like(buf)

    def one(j, carry):
        block = src_ref[j]
        for t in range(2):
            q = routes_ref[t, j]
            rank = count[q]
            count[q] = rank + 1
            buf[table[q] + rank] = block
        return carry

    lax.fori_loop(0, src_ref.shape[0], one, 0, unroll=8)
    own_ref[...] = buf[0:96]
    core_ref[...] = buf[96:192]
    x_ref[...] = buf[192:288]
    far_ref[...] = buf[288:320]


def pack(pos, routes, source):
    fields, cells = source.shape[1:]
    shape = lambda n: jax.ShapeDtypeStruct((n, fields, cells), BF)
    return pl.pallas_call(
        pack_kernel,
        in_specs=[SM, SM, VM],
        out_specs=[VM] * 4,
        out_shape=[shape(96), shape(96), shape(96), shape(32)],
        scratch_shapes=[
            pltpu.VMEM((320, fields, cells), BF),
            pltpu.SMEM((12,), jnp.int32),
            pltpu.SMEM((12,), jnp.int32),
        ],
        compiler_params=params(16),
        cost_estimate=cost(0, 1 << 20),
        name="pack",
    )(pos, routes, source)


def prep_kernel(stem_ref, mix_ref, ws_ref, wm_ref):
    zero8 = jnp.zeros((8, 128), F32)
    taps = [stem_ref[t].astype(F32) * SCALE for t in range(9)]
    for i in range(STEP):
        for par in range(2):
            rows = []
            for d in range(4):
                for row in range(8):
                    a, b = row - i, d - par
                    rows.append(taps[3 * a + b] if 0 <= a < 3 and 0 <= b < 3 else zero8)
            lane = (2 * i + par) * 128
            ws_ref[:, lane : lane + 128] = jnp.concatenate(rows, axis=0).astype(BF)
    zero = jnp.zeros((128, 128), BF)
    for a in range(3):
        for par in range(2):
            for d in range(4):
                b = d - par
                wm_ref[a, d * 128 : d * 128 + 128, par * 128 : par * 128 + 128] = (
                    mix_ref[3 * a + b] if 0 <= b < 3 else zero
                )


def prep(stem_weight, mix_weight):
    return pl.pallas_call(
        prep_kernel,
        in_specs=[VM] * 2,
        out_specs=[VM] * 2,
        out_shape=[
            jax.ShapeDtypeStruct((256, STEP * 256), BF),
            jax.ShapeDtypeStruct((3, 512, 256), BF),
        ],
        compiler_params=params(16),
        cost_estimate=cost(0, 2 << 20),
        name="prep",
    )(stem_weight, mix_weight)


def contrib_kernel(pieces, first, codes_ref, win_ref, *refs):
    arrays = refs[: len(pieces)]
    refs = refs[len(pieces) :]
    if first:
        w_ref, out_ref, inc, acc = refs
    else:
        w_ref, start_ref, pos_ref, fld_ref, a_ref, b_ref, inc, acc = refs
    g = pl.program_id(0)

    @pl.when(g == 0)
    def _():
        if first:
            acc[...] = jnp.zeros_like(acc)
        else:
            acc[...] = start_ref[...]

    number = 0
    for array, groups in zip(arrays, pieces):
        for i in groups:

            @pl.when(g == number)
            def _(array=array, i=i):
                inc[...] = array[i * 32 : i * 32 + 32]

            number += 1
    q = codes_ref[g]
    for s in range(32):
        part = jnp.dot(inc[s], w_ref[0, 0, s], preferred_element_type=F32).astype(BF).astype(F32)
        w = win_ref[q, s]
        place = (w % 4) * ROWS + w // 4
        acc[place] = acc[place] + part

    @pl.when(g == number - 1)
    def _():
        if first:
            out_ref[...] = acc[...]
        else:
            for cb in range(4):
                rows = acc[cb * ROWS : (cb + 1) * ROWS].reshape(ROWS * 8, 128)
                fld_ref[:, cb * 128 : cb * 128 + 128] = rows.astype(BF)
            even = pos_ref[0] % 2 == 0
            top, bottom = fld_ref[0:16], fld_ref[ROWS * 8 - 16 : ROWS * 8]
            a_ref[...] = jnp.where(even, bottom, top)
            b_ref[...] = jnp.where(even, top, bottom)


def contrib(first, codes, win, arrays, pieces, weights, extra=()):
    groups = sum(len(p) for p in pieces)
    whole = lambda a: pl.BlockSpec(a.shape, lambda g, *_: (0,) * a.ndim)
    if first:
        out_shape = jax.ShapeDtypeStruct((ROWS * 4, 8, 128), F32)
        out_specs = pl.BlockSpec((ROWS * 4, 8, 128), lambda g, *_: (0, 0, 0))
        extra_specs = []
    else:
        out_shape = [
            jax.ShapeDtypeStruct((ROWS * 8, COLS), BF),
            jax.ShapeDtypeStruct((16, COLS), BF),
            jax.ShapeDtypeStruct((16, COLS), BF),
        ]
        out_specs = [pl.BlockSpec(o.shape, lambda g, *_: (0, 0)) for o in out_shape]
        extra_specs = [whole(extra[0]), SM]
    spec = pltpu.PrefetchScalarGridSpec(
        num_scalar_prefetch=2,
        grid=(groups,),
        in_specs=[whole(a) for a in arrays]
        + [pl.BlockSpec((1, 1, 32, 128, 128), lambda g, codes, win: (0, codes[g], 0, 0, 0))]
        + extra_specs,
        out_specs=out_specs,
        scratch_shapes=[pltpu.VMEM((32, 8, 128), BF), pltpu.VMEM((ROWS * 4, 8, 128), F32)],
    )
    return pl.pallas_call(
        functools.partial(contrib_kernel, pieces, first),
        grid_spec=spec,
        out_shape=out_shape,
        compiler_params=params(24),
        cost_estimate=cost(groups * 32 * 2 * 8 * 128 * 128, groups << 20),
        name="contrib_near" if first else "contrib_far",
    )(codes, win, *arrays, weights, *extra)


def tall(fld_ref, a, b, even):
    north = jnp.where(even, b, a)
    south = jnp.where(even, a, b)
    return jnp.concatenate([north, fld_ref[...], south], axis=0)


def edge_kernel(pos_ref, fld_ref, a_ref, b_ref, edge_ref):
    even = pos_ref[0] % 2 == 0
    whole = tall(fld_ref, a_ref[...], b_ref[...], even)
    rank = lax.broadcasted_iota(jnp.int32, (16, COLS), 0)
    col = lax.broadcasted_iota(jnp.int32, (16, COLS), 1)
    pick = ((rank < 2) & (col == rank)) | ((rank >= 2) & (rank < 4) & (col == COLS - 4 + rank))
    pick = jnp.where(pick, 1.0, 0.0).astype(BF)
    edge_ref[...] = lax.dot_general(
        pick, whole, (((1,), (1,)), ((), ())), preferred_element_type=F32
    ).astype(BF)


def edges(pos, fld, a, b):
    return pl.pallas_call(
        edge_kernel,
        in_specs=[SM, VM, VM, VM],
        out_specs=VM,
        out_shape=jax.ShapeDtypeStruct((16, (ROWS + 4) * 8), BF),
        compiler_params=params(8),
        cost_estimate=cost(0, 1 << 20),
        name="edges",
    )(pos, fld, a, b)


def build(pos_ref, fld_ref, a_ref, b_ref, core_ref, x_ref, g):
    whole = tall(fld_ref, a_ref[...], b_ref[...], pos_ref[0] % 2 == 0)
    even = pos_ref[1] % 2 == 0
    core, x = core_ref[...].astype(F32), x_ref[...].astype(F32)
    right, left = jnp.where(even, core, x), jnp.where(even, x, core)
    c = lax.broadcasted_iota(jnp.int32, (256, 256), 0)
    lane = lax.broadcasted_iota(jnp.int32, (256, 256), 1)
    j, d = lane % 128, lane // 128
    hr = lax.broadcasted_iota(jnp.int32, (16, 256), 0)
    hl = lax.broadcasted_iota(jnp.int32, (16, 256), 1)

    def halo(side, base):
        hot = ((hl % 128) == 0) & (hr == hl // 128 + base)
        return lax.dot_general(
            side.astype(BF),
            jnp.where(hot, 1.0, 0.0).astype(BF),
            (((0,), (0,)), ((), ())),
            preferred_element_type=F32,
        )

    def moved(half, shift):
        hot = jnp.where(c == 2 * j + d + shift, 1.0, 0.0).astype(BF)
        return jnp.dot(whole[:, half * 256 : half * 256 + 256], hot, preferred_element_type=F32)

    tiles = {
        (0, 0): moved(0, -2) + halo(left, 2),
        (0, 1): moved(0, 254) + moved(1, -2),
        (0, 2): moved(1, 254),
        (1, 0): moved(0, 0),
        (1, 1): moved(1, 0),
        (1, 2): halo(right, 0),
    }
    for (pair, tile), value in tiles.items():
        value = value.astype(BF)
        for half in range(2):
            d0 = (2 * pair + half) * 64
            part = value[:, half * 128 : half * 128 + 128]
            for m in range(BLOCKS):
                g[m, d0 : d0 + 64, tile * 128 : tile * 128 + 128] = part[48 * m : 48 * m + 64]


def conv_kernel(
    last,
    pos_ref,
    fld_ref,
    a_ref,
    b_ref,
    core_ref,
    x_ref,
    ws_ref,
    bs_ref,
    wm_ref,
    bm_ref,
    out_ref,
    g,
    hs,
    vs,
    ys,
    yb,
    sem,
):
    s = pl.program_id(0)

    @pl.when(s == 0)
    def _():
        build(pos_ref, fld_ref, a_ref, b_ref, core_ref, x_ref, g)

    band = pos_ref[0]
    keep_first = jnp.where((s == 0) & (band == 0), 0.0, 1.0)
    keep_last = jnp.where((s == BLOCKS - 1) & (band == last), 0.0, 1.0)
    x = g[s][:, :HROWS]
    for i in range(STEP):
        t = lax.dot_general(
            x,
            ws_ref[:, i * 256 : i * 256 + 256],
            (((0,), (0,)), ((), ())),
            preferred_element_type=F32,
        )
        t = t + bs_ref[...]
        h = t + t * jnp.tanh(t)
        if i == 0:
            h = h * keep_first
        if i == STEP - 1:
            h = h * keep_last
        hs[6 * s + 2 + i, 0] = h[:, :128]
        hs[6 * s + 2 + i, 1] = h[:, 128:]
    parts = [(0, 0), (1, 0), (0, 1), (1, 1)]
    for r in range(STEP + 2):
        for k, (par, shift) in enumerate(parts):
            vs[r, :, k * 128 : k * 128 + 128] = hs[6 * s + r, par, shift : shift + PAIRS, :].astype(BF)
    slot = s % 2

    def copy(at, slot):
        return pltpu.make_async_copy(
            yb.at[slot], out_ref.at[pl.ds(6 * at - 2, 6)], sem.at[slot]
        )

    first = pltpu.make_async_copy(yb.at[0, pl.ds(2, 4)], out_ref.at[pl.ds(0, 4)], sem.at[0])

    @pl.when(s == 2)
    def _():
        first.wait()

    @pl.when(s > 2)
    def _():
        copy(s - 2, slot).wait()

    for h in range(STEP):
        lhs = jnp.concatenate([vs[h + a] for a in range(3)], axis=1)
        y = jnp.dot(lhs, wm_ref[...].reshape(1536, 256), preferred_element_type=F32)
        for par in range(2):
            ys[h, pl.ds(par, PAIRS, stride=2), :] = y[:, par * 128 : par * 128 + 128] + bm_ref[...]
        yb[slot, h] = ys[h].astype(BF)

    @pl.when(s == 0)
    def _():
        first.start()

    @pl.when(s > 0)
    def _():
        copy(s, slot).start()

    @pl.when(s == BLOCKS - 1)
    def _():
        copy(s - 1, 1 - slot).wait()
        copy(s, slot).wait()


def conv(n_band, pos, fld, a, b, core, x, ws, bs, wm, bm):
    channels = bm.shape[-1]
    return pl.pallas_call(
        functools.partial(conv_kernel, n_band - 1),
        grid=(BLOCKS,),
        in_specs=[SM] + [VM] * 9,
        out_specs=ANY,
        out_shape=jax.ShapeDtypeStruct((ROWS, COLS, channels), BF),
        scratch_shapes=[
            pltpu.VMEM((BLOCKS, 256, LANES), BF),
            pltpu.VMEM((ROWS + 4, 2, HROWS, 128), F32),
            pltpu.VMEM((STEP + 2, PAIRS, 512), BF),
            pltpu.VMEM((STEP, COLS, channels), F32),
            pltpu.VMEM((2, STEP, COLS, channels), BF),
            pltpu.SemaphoreType.DMA((2,)),
        ],
        compiler_params=params(56),
        cost_estimate=cost(2 * ROWS * COLS * 9 * 128 * 128, 12 << 20),
        name="conv",
    )(pos, fld, a, b, core, x, ws, bs, wm, bm)


def on_device(source, routes, slot_weights, window, stem_weight, stem_bias, mix_weight, mix_bias):
    n_band = lax.axis_size("band")
    n_lon = lax.axis_size("lon")
    axes = ("band", "lon")
    band = lax.axis_index("band")
    lon = lax.axis_index("lon")

    def move(value, pairs):
        return lax.ppermute(value, axes, pairs)

    pos = jnp.stack([band, lon]).astype(jnp.int32)
    core_dl = jnp.where(lon % 2 == 0, 3, 1)
    x_dl = 4 - core_dl
    a_base = jnp.where(band % 2 == 0, 0, 8)
    b_base = 8 - a_base
    rim = (band == 0) | (band == n_band - 1)
    far_code = jnp.where(band < n_band // 2, 10, 2)
    near_codes = jnp.stack([4 + 0 * lon, 4 + core_dl, 4 + x_dl]).astype(jnp.int32)
    far_codes = jnp.stack(
        [
            a_base,
            a_base + core_dl,
            a_base + x_dl,
            jnp.where(rim, 6, b_base),
            b_base + core_dl,
            b_base + x_dl,
            far_code,
        ]
    ).astype(jnp.int32)

    own, to_core, to_x, to_far = pack(pos, routes.T, source)
    core = move(to_core, swap_core(n_band, n_lon))
    x = move(to_x, swap_x(n_band, n_lon))
    far = move(to_far, swap_far(n_band, n_lon))
    a_out = jnp.concatenate([own[0:32], core[0:32], x[0:32]], axis=0)
    b_out = jnp.concatenate([own[64:96], core[64:96], x[64:96]], axis=0)
    a_in = move(a_out, swap_a(n_band, n_lon))
    b_in = move(b_out, swap_b(n_band, n_lon, True))
    ws, wm = prep(stem_weight, mix_weight)
    win = window[0]
    near = contrib(True, near_codes, win, [own, core, x], [(1,)] * 3, slot_weights)
    fld, a_row, b_row = contrib(
        False,
        far_codes,
        win,
        [a_in, b_in, far],
        [(0, 1, 2), (0, 1, 2), (0,)],
        slot_weights,
        (near, pos),
    )
    a_halo = move(a_row, swap_a(n_band, n_lon))
    b_halo = move(b_row, swap_b(n_band, n_lon, False))
    edge = edges(pos, fld, a_halo, b_halo)
    core_edge = move(edge, swap_core(n_band, n_lon))
    x_edge = move(edge, swap_x(n_band, n_lon))
    bs = SCALE * jnp.concatenate([stem_bias, stem_bias])[None]
    return conv(n_band, pos, fld, a_halo, b_halo, core_edge, x_edge, ws, bs, wm, mix_bias[None])


def solution(mesh):
    both = ("band", "lon")
    in_specs = (
        P(both, None, None),
        P(both, None),
        P(both, None, None, None, None),
        P(both, None, None),
        P(),
        P(),
        P(),
        P(),
    )
    return jax.shard_map(
        on_device, mesh=mesh, in_specs=in_specs, out_specs=P("band", "lon", None), check_vma=False
    )
```

```python
import functools

import jax
import jax.numpy as jnp
from jax import lax
from jax.experimental import pallas as pl
from jax.experimental.pallas import tpu as pltpu
from jax.sharding import PartitionSpec as P

ROWS = 64
COLS = 512
PAIRS = COLS // 2
SUB = 16
HROWS = PAIRS + SUB
PITCH = 2 * SUB + 1
LANES = 384
CHUNK = 256
STEP = 6
BLOCKS = (ROWS + 2) // STEP
SCALE = 1.0 / 2.0
BF = jnp.bfloat16
F32 = jnp.float32
VM = pl.BlockSpec(memory_space=pltpu.VMEM)
SM = pl.BlockSpec(memory_space=pltpu.SMEM)
ANY = pl.BlockSpec(memory_space=pl.ANY)
HBM = pl.BlockSpec(memory_space=pltpu.HBM)


def params(mib):
    return pltpu.CompilerParams(vmem_limit_bytes=mib << 20)


def cost(flops, size):
    return pl.CostEstimate(flops=flops, bytes_accessed=size, transcendentals=0)


def swap_core(n_band, n_lon):
    return [(b * n_lon + l, b * n_lon + (l ^ 1)) for b in range(n_band) for l in range(n_lon)]


def swap_x(n_band, n_lon):
    return [(b * n_lon + l, b * n_lon + n_lon - 1 - l) for b in range(n_band) for l in range(n_lon)]


def swap_a(n_band, n_lon):
    return [(b * n_lon + l, (b ^ 1) * n_lon + l) for b in range(n_band) for l in range(n_lon)]


def swap_b(n_band, n_lon):
    pairs = []
    for b in range(n_band):
        partner = b + 1 if b % 2 else b - 1
        for l in range(n_lon):
            if 0 <= partner < n_band:
                pairs.append((b * n_lon + l, partner * n_lon + l))
            else:
                pairs.append((b * n_lon + l, b * n_lon + (l + 2) % n_lon))
    return pairs


def swap_diagonal(n_band, n_lon):
    return [
        (b * n_lon + l, (b ^ 1) * n_lon + (l + 2) % n_lon) for b in range(n_band) for l in range(n_lon)
    ]


def in_hbm(*arrays):
    return [pltpu.with_memory_space_constraint(a, pltpu.HBM) for a in arrays]


def pack_kernel(
    pos_ref, routes_hbm, src_hbm, own_ref, core_ref, x_ref, far_ref, routes_ref, src_ref, buf, table, count, sem
):
    copies = [
        pltpu.make_async_copy(routes_hbm, routes_ref, sem.at[0]),
        pltpu.make_async_copy(src_hbm, src_ref, sem.at[1]),
    ]
    for copy in copies:
        copy.start()
    band = pos_ref[0]
    lon = pos_ref[1]
    a_dir = 1 - 2 * (band % 2)
    core_dl = 1 + 2 * (lon % 2)
    for q in range(12):
        db, dl = q // 4 - 1, q % 4
        if db == 0:
            way = 1
        else:
            way = jnp.where(a_dir == db, 0, 2)
        if dl == 0:
            group = way
        elif dl == 2:
            group = 2 if db == 0 else 9
        else:
            group = jnp.where(core_dl == dl, 3, 6) + way
        table[q] = group * 32
        count[q] = 0
    buf[...] = jnp.zeros_like(buf)
    for copy in copies:
        copy.wait()

    def one(j, carry):
        block = src_ref[j]
        for t in range(2):
            q = routes_ref[t, j]
            rank = count[q]
            count[q] = rank + 1
            buf[table[q] + rank] = block
        return carry

    lax.fori_loop(0, src_ref.shape[0], one, 0, unroll=8)
    own_ref[...] = buf[0:96]
    core_ref[...] = buf[96:192]
    x_ref[...] = buf[192:288]
    far_ref[...] = buf[288:320]


def pack(pos, routes, source):
    fields, cells = source.shape[1:]
    shape = lambda n: jax.ShapeDtypeStruct((n, fields, cells), BF)
    return pl.pallas_call(
        pack_kernel,
        in_specs=[SM, HBM, HBM],
        out_specs=[VM] * 4,
        out_shape=[shape(96), shape(96), shape(96), shape(32)],
        scratch_shapes=[
            pltpu.SMEM(routes.shape, jnp.int32),
            pltpu.VMEM(source.shape, BF),
            pltpu.VMEM((320, fields, cells), BF),
            pltpu.SMEM((12,), jnp.int32),
            pltpu.SMEM((12,), jnp.int32),
            pltpu.SemaphoreType.DMA((2,)),
        ],
        compiler_params=params(16),
        cost_estimate=cost(0, 1 << 20),
        name="pack",
    )(pos, *in_hbm(routes, source))


def prep_kernel(stem_ref, bias_ref, mix_ref, ws_ref, bs_ref, wm_ref, hot_ref):
    for par in range(2):
        bs_ref[:, par * 128 : par * 128 + 128] = bias_ref[...] * SCALE
    c = lax.broadcasted_iota(jnp.int32, (COLS, 256), 0)
    lane = lax.broadcasted_iota(jnp.int32, (COLS, 256), 1)
    for tile in range(3):
        n = lane % 128 + tile * 128
        j = jnp.where(n < PAIRS, SUB * (n % SUB) + n // SUB, SUB * (n - PAIRS + 1))
        gap = jnp.where(n < HROWS, c - 2 * j - lane // 128, -COLS)
        for pair in range(2):
            hot = jnp.where(gap == 2 * pair - 2, 1.0, 0.0)
            hot_ref[:, (2 * tile + pair) * 256 : (2 * tile + pair) * 256 + 256] = hot.astype(BF)
    zero8 = jnp.zeros((8, 128), F32)
    taps = [stem_ref[t].astype(F32) * SCALE for t in range(9)]
    for i in range(STEP):
        for par in range(2):
            rows = []
            for d in range(4):
                for row in range(8):
                    a, b = row - i, d - par
                    rows.append(taps[3 * a + b] if 0 <= a < 3 and 0 <= b < 3 else zero8)
            lane = (2 * i + par) * 128
            ws_ref[:, lane : lane + 128] = jnp.concatenate(rows, axis=0).astype(BF)
    zero = jnp.zeros((128, 128), BF)
    for b in range(3):
        w = [mix_ref[3 * a + b].astype(F32) for a in range(3)]
        mean = 0.5 * (w[0] + w[2])
        forms = [w[0], mean + 0.5 * w[1], mean - 0.5 * w[1], w[2]]
        for k in range(4):
            for par in range(2):
                d = b + par
                wm_ref[k, d * 128 : d * 128 + 128, par * 128 : par * 128 + 128] = forms[k].astype(BF)
    for k in range(4):
        wm_ref[k, 0:128, 128:256] = zero
        wm_ref[k, 384:512, 0:128] = zero


def prep(stem_weight, stem_bias, mix_weight):
    return pl.pallas_call(
        prep_kernel,
        in_specs=[VM] * 3,
        out_specs=[VM] * 4,
        out_shape=[
            jax.ShapeDtypeStruct((256, STEP * 256), BF),
            jax.ShapeDtypeStruct((1, 256), F32),
            jax.ShapeDtypeStruct((4, 512, 256), BF),
            jax.ShapeDtypeStruct((COLS, 6 * 256), BF),
        ],
        compiler_params=params(12),
        cost_estimate=cost(0, 2 << 20),
        name="prep",
    )(stem_weight, stem_bias[None], mix_weight)


def add_groups(codes_ref, win_ref, w_hbm, w_ref, sem, acc, arrays, number):
    first = number
    copies = [
        pltpu.make_async_copy(w_hbm.at[0, codes_ref[first + g]], w_ref.at[g], sem.at[g])
        for g in range(w_ref.shape[0])
    ]
    for copy in copies:
        copy.start()
    for array, begin, groups in arrays:
        for i in range(groups):
            copies[number - first].wait()
            q = codes_ref[number]
            for s in range(32):
                block = array[(begin + i) * 32 + s]
                part = jnp.dot(block, w_ref[number - first, s], preferred_element_type=F32)
                w = win_ref[0, q, s]
                place = (w % 4) * ROWS + w // 4
                acc[place] = acc[place] + part.astype(BF).astype(F32)
            number += 1


def near_kernel(codes_ref, win_ref, own_ref, core_ref, x_ref, w_hbm, acc, w_ref, sem):
    acc[...] = jnp.zeros_like(acc)
    arrays = [(own_ref, 1, 1), (core_ref, 1, 1), (x_ref, 1, 1)]
    add_groups(codes_ref, win_ref, w_hbm, w_ref, sem, acc, arrays, 0)


def far_kernel(
    codes_ref, win_ref, pos_ref, a_in, b_in, far_in, near_ref, w_hbm, fld_ref, a_ref, b_ref, acc, w_ref, sem
):
    acc[...] = near_ref[...]
    arrays = [(a_in, 0, 3), (b_in, 0, 3), (far_in, 0, 1)]
    add_groups(codes_ref, win_ref, w_hbm, w_ref, sem, acc, arrays, 3)
    for cb in range(4):
        rows = acc[cb * ROWS : (cb + 1) * ROWS].reshape(ROWS * 8, 128)
        fld_ref[:, cb * 128 : cb * 128 + 128] = rows.astype(BF)
    even = pos_ref[0] % 2 == 0
    top, bottom = fld_ref[0:16], fld_ref[ROWS * 8 - 16 : ROWS * 8]
    a_ref[...] = jnp.where(even, bottom, top)
    b_ref[...] = jnp.where(even, top, bottom)


def near_part(codes, win, own, core, x, weights):
    return pl.pallas_call(
        near_kernel,
        in_specs=[SM, SM] + [VM] * 3 + [HBM],
        out_specs=VM,
        out_shape=jax.ShapeDtypeStruct((ROWS * 4, 8, 128), F32),
        scratch_shapes=[
            pltpu.VMEM((3,) + weights.shape[2:], BF),
            pltpu.SemaphoreType.DMA((3,)),
        ],
        compiler_params=params(12),
        cost_estimate=cost(96 * 2 * 8 * 128 * 128, 4 << 20),
        name="near",
    )(codes, win, own, core, x, *in_hbm(weights))


def far_part(codes, win, pos, a, b, far, near, weights):
    return pl.pallas_call(
        far_kernel,
        in_specs=[SM, SM, SM] + [VM] * 4 + [HBM],
        out_specs=[VM] * 3,
        out_shape=[
            jax.ShapeDtypeStruct((ROWS * 8, COLS), BF),
            jax.ShapeDtypeStruct((16, COLS), BF),
            jax.ShapeDtypeStruct((16, COLS), BF),
        ],
        scratch_shapes=[
            pltpu.VMEM((ROWS * 4, 8, 128), F32),
            pltpu.VMEM((7,) + weights.shape[2:], BF),
            pltpu.SemaphoreType.DMA((7,)),
        ],
        compiler_params=params(16),
        cost_estimate=cost(224 * 2 * 8 * 128 * 128, 8 << 20),
        name="far",
    )(codes, win, pos, a, b, far, near, *in_hbm(weights))


def tall(fld_ref, a, b, band, last):
    even = band % 2 == 0
    b = jnp.where((band == 0) | (band == last), jnp.zeros_like(b), b)
    north = jnp.where(even, b, a)
    south = jnp.where(even, a, b)
    return jnp.concatenate([north, fld_ref[...], south], axis=0)


def edge_kernel(last, pos_ref, fld_ref, a_ref, b_ref, edge_ref):
    whole = tall(fld_ref, a_ref[...], b_ref[...], pos_ref[0], last)
    rank = lax.broadcasted_iota(jnp.int32, (16, COLS), 0)
    col = lax.broadcasted_iota(jnp.int32, (16, COLS), 1)
    pick = ((rank < 2) & (col == rank)) | ((rank >= 2) & (rank < 4) & (col == COLS - 4 + rank))
    pick = jnp.where(pick, 1.0, 0.0).astype(BF)
    edge_ref[...] = lax.dot_general(
        pick, whole, (((1,), (1,)), ((), ())), preferred_element_type=F32
    ).astype(BF)


def edges(n_band, pos, fld, a, b):
    return pl.pallas_call(
        functools.partial(edge_kernel, n_band - 1),
        in_specs=[SM, VM, VM, VM],
        out_specs=VM,
        out_shape=jax.ShapeDtypeStruct((16, (ROWS + 4) * 8), BF),
        compiler_params=params(8),
        cost_estimate=cost(0, 1 << 20),
        name="edges",
    )(pos, fld, a, b)


def build(last, pos_ref, fld_ref, a_ref, b_ref, core_ref, x_ref, hot_ref, g):
    whole = tall(fld_ref, a_ref[...], b_ref[...], pos_ref[0], last)
    even = pos_ref[1] % 2 == 0
    core, x = core_ref[...].astype(F32), x_ref[...].astype(F32)
    right, left = jnp.where(even, core, x), jnp.where(even, x, core)
    hr = lax.broadcasted_iota(jnp.int32, (16, 256), 0)
    hl = lax.broadcasted_iota(jnp.int32, (16, 256), 1)

    def halo(side, base, at):
        hot = ((hl % 128) == at) & (hr == hl // 128 + base)
        return lax.dot_general(
            side.astype(BF),
            jnp.where(hot, 1.0, 0.0).astype(BF),
            (((0,), (0,)), ((), ())),
            preferred_element_type=F32,
        )

    def moved(pair, tile):
        at = (2 * tile + pair) * 256
        return jnp.dot(whole, hot_ref[:, at : at + 256], preferred_element_type=F32)

    tiles = {(pair, tile): moved(pair, tile) for pair in range(2) for tile in range(3)}
    tiles[0, 0] = tiles[0, 0] + halo(left, 2, 0)
    tiles[1, 2] = tiles[1, 2] + halo(right, 0, SUB - 1)
    for (pair, tile), value in tiles.items():
        value = value.astype(BF)
        for half in range(2):
            d0 = (2 * pair + half) * 64
            part = value[:, half * 128 : half * 128 + 128]
            for m in range(BLOCKS):
                g[m, d0 : d0 + 64, tile * 128 : tile * 128 + 128] = part[48 * m : 48 * m + 64]


def conv_kernel(
    last,
    pos_ref,
    fld_ref,
    a_ref,
    b_ref,
    core_ref,
    x_ref,
    ws_ref,
    bs_ref,
    wm_ref,
    bm_ref,
    hot_ref,
    out_ref,
    g,
    hs,
    ys,
    yb,
    sem,
):
    s = pl.program_id(0)
    band = pos_ref[0]

    def stem(block, which, low, high):
        x = g[jnp.minimum(block, BLOCKS - 1)][:, :HROWS]
        for i in which:
            t = lax.dot_general(
                x,
                ws_ref[:, i * 256 : i * 256 + 256],
                (((0,), (0,)), ((), ())),
                preferred_element_type=F32,
            )
            t = t + bs_ref[...]
            h = t + t * jnp.tanh(t)
            if i == 0 and low is not None:
                h = h * low
            if i == STEP - 1 and high is not None:
                h = h * high
            hs[block % 2, i] = h.astype(BF)

    @pl.when(s == 0)
    def _():
        build(last, pos_ref, fld_ref, a_ref, b_ref, core_ref, x_ref, hot_ref, g)
        stem(0, range(STEP), jnp.where(band == 0, 0.0, 1.0), None)

    slot = s % 2

    def copy(at, slot):
        return pltpu.make_async_copy(
            yb.at[slot], out_ref.at[pl.ds(6 * at - 2, 6)], sem.at[slot]
        )

    first = pltpu.make_async_copy(yb.at[0, pl.ds(2, 4)], out_ref.at[pl.ds(0, 4)], sem.at[0])

    @pl.when(s == 2)
    def _():
        first.wait()

    @pl.when(s > 2)
    def _():
        copy(s - 2, slot).wait()

    rows = [(1 - slot, 4), (1 - slot, 5)] + [(slot, i) for i in range(STEP)]
    keep_last = jnp.where((s == BLOCKS - 2) & (band == last), 0.0, 1.0)

    def mix(t):
        for c in range(PAIRS // CHUNK):
            row0 = c * CHUNK

            def both(r):
                return jnp.concatenate(
                    [hs[rows[2 * t + r]][row0 + k * SUB : row0 + k * SUB + CHUNK] for k in range(2)],
                    axis=1,
                )

            h = [both(r) for r in range(4)]
            v = [h[0] - h[2], h[1] + h[2], h[2] - h[1], h[1] - h[3]]
            m = [jnp.dot(v[k], wm_ref[k], preferred_element_type=F32) for k in range(4)]
            plus, minus = m[1] + m[2], m[1] - m[2]
            for q, y in enumerate([plus + m[0], minus - m[3]]):
                row = 2 * t + q
                for par in range(2):
                    part = y[:, par * 128 : par * 128 + 128] + bm_ref[...]
                    for k in range(CHUNK // SUB):
                        to = pl.ds(2 * (c * CHUNK // SUB + k) + par, SUB, stride=PITCH)
                        ys[row, to, :] = part[k * SUB : k * SUB + SUB]
        for q in range(2):
            for a in range(SUB):
                yb[slot, 2 * t + q, 2 * SUB * a : 2 * SUB * a + 2 * SUB] = ys[
                    2 * t + q, PITCH * a : PITCH * a + 2 * SUB
                ].astype(BF)

    for t in range(STEP // 2):
        mix(t)
    stem(s + 1, range(STEP), None, keep_last)

    @pl.when(s == 0)
    def _():
        first.start()

    @pl.when(s > 0)
    def _():
        copy(s, slot).start()

    @pl.when(s == BLOCKS - 1)
    def _():
        copy(s - 1, 1 - slot).wait()
        copy(s, slot).wait()


def conv(n_band, pos, fld, a, b, core, x, ws, bs, wm, bm, hot):
    channels = bm.shape[-1]
    return pl.pallas_call(
        functools.partial(conv_kernel, n_band - 1),
        grid=(BLOCKS,),
        in_specs=[SM] + [VM] * 10,
        out_specs=ANY,
        out_shape=jax.ShapeDtypeStruct((ROWS, COLS, channels), BF),
        scratch_shapes=[
            pltpu.VMEM((BLOCKS, 256, LANES), BF),
            pltpu.VMEM((2, STEP, HROWS, 256), BF),
            pltpu.VMEM((STEP, SUB * PITCH, channels), F32),
            pltpu.VMEM((2, STEP, COLS, channels), BF),
            pltpu.SemaphoreType.DMA((2,)),
        ],
        compiler_params=params(20),
        cost_estimate=cost(2 * ROWS * COLS * 9 * 128 * 128, 12 << 20),
        name="conv",
    )(pos, fld, a, b, core, x, ws, bs, wm, bm, hot)


def on_device(source, routes, slot_weights, window, stem_weight, stem_bias, mix_weight, mix_bias):
    n_band = lax.axis_size("band")
    n_lon = lax.axis_size("lon")
    axes = ("band", "lon")
    band = lax.axis_index("band")
    lon = lax.axis_index("lon")

    def move(value, pairs):
        return lax.ppermute(value, axes, pairs)

    pos = jnp.stack([band, lon]).astype(jnp.int32)
    core_dl = jnp.where(lon % 2 == 0, 3, 1)
    x_dl = 4 - core_dl
    a_base = jnp.where(band % 2 == 0, 0, 8)
    b_base = 8 - a_base
    rim = (band == 0) | (band == n_band - 1)
    far_code = jnp.where(band < n_band // 2, 10, 2)
    near = [4 + 0 * lon, 4 + core_dl, 4 + x_dl]
    along_a = [a_base, a_base + core_dl, a_base + x_dl]
    along_b = [jnp.where(rim, 6, b_base), b_base + core_dl, b_base + x_dl]
    codes = jnp.stack(near + along_a + along_b + [far_code]).astype(jnp.int32)

    own, to_core, to_x, to_far = pack(pos, routes.T, source)
    core = move(to_core, swap_core(n_band, n_lon))
    x = move(to_x, swap_x(n_band, n_lon))
    far = move(to_far, swap_diagonal(n_band, n_lon))
    ws, bs, wm, hot = prep(stem_weight, stem_bias, mix_weight)
    core, x, far, ws, bs, wm, hot = lax.optimization_barrier((core, x, far, ws, bs, wm, hot))
    a_out = jnp.concatenate([own[0:32], core[0:32], x[0:32]], axis=0)
    b_out = jnp.concatenate([own[64:96], core[64:96], x[64:96]], axis=0)
    a_in = move(a_out, swap_a(n_band, n_lon))
    b_in = move(b_out, swap_b(n_band, n_lon))
    near = near_part(codes, window, own, core, x, slot_weights)
    a_in, b_in, near = lax.optimization_barrier((a_in, b_in, near))
    fld, a_row, b_row = far_part(codes, window, pos, a_in, b_in, far, near, slot_weights)
    a_halo = move(a_row, swap_a(n_band, n_lon))
    b_halo = move(b_row, swap_b(n_band, n_lon))
    edge = edges(n_band, pos, fld, a_halo, b_halo)
    core_edge = move(edge, swap_core(n_band, n_lon))
    x_edge = move(edge, swap_x(n_band, n_lon))
    return conv(
        n_band, pos, fld, a_halo, b_halo, core_edge, x_edge, ws, bs, wm, mix_bias[None], hot
    )


def solution(mesh):
    both = ("band", "lon")
    in_specs = (
        P(both, None, None),
        P(both, None),
        P(both, None, None, None, None),
        P(both, None, None),
        P(),
        P(),
        P(),
        P(),
    )
    return jax.shard_map(
        on_device, mesh=mesh, in_specs=in_specs, out_specs=P("band", "lon", None), check_vma=False
    )
```

```python
import functools

import jax
import jax.numpy as jnp
from jax import lax
from jax.experimental import pallas as pl
from jax.experimental.pallas import tpu as pltpu
from jax.sharding import PartitionSpec as P

ROWS = 64
COLS = 512
PAIRS = COLS // 2
SUB = 16
HROWS = PAIRS + SUB
PITCH = 2 * SUB + 1
LANES = 384
CHUNK = 256
STEP = 6
BLOCKS = (ROWS + 2) // STEP
SCALE = 1.0 / 2.0
BF = jnp.bfloat16
F32 = jnp.float32
VM = pl.BlockSpec(memory_space=pltpu.VMEM)
SM = pl.BlockSpec(memory_space=pltpu.SMEM)
ANY = pl.BlockSpec(memory_space=pl.ANY)
HBM = pl.BlockSpec(memory_space=pltpu.HBM)


def params(mib):
    return pltpu.CompilerParams(vmem_limit_bytes=mib << 20)


def cost(flops, size):
    return pl.CostEstimate(flops=flops, bytes_accessed=size, transcendentals=0)


def swap(n_band, n_lon, way, turn):
    pairs = []
    for b in range(n_band):
        if way == "a":
            partner = b ^ 1
        elif way == "b":
            partner = b + 1 if b % 2 else b - 1
        else:
            partner = b
        for l in range(n_lon):
            target = {"stay": l, "core": l ^ 1, "x": n_lon - 1 - l, "across": (l + 2) % n_lon}[turn]
            if not 0 <= partner < n_band:
                pairs.append((b * n_lon + l, b * n_lon + (l + 2) % n_lon))
            else:
                pairs.append((b * n_lon + l, partner * n_lon + target))
    return pairs


def in_hbm(*arrays):
    return [pltpu.with_memory_space_constraint(a, pltpu.HBM) for a in arrays]


def pack_kernel(
    pos_ref, routes_hbm, src_hbm, *refs
):
    outs, (routes_ref, src_ref, buf, table, count, sem) = refs[:10], refs[10:]
    copies = [
        pltpu.make_async_copy(routes_hbm, routes_ref, sem.at[0]),
        pltpu.make_async_copy(src_hbm, src_ref, sem.at[1]),
    ]
    for copy in copies:
        copy.start()
    band = pos_ref[0]
    lon = pos_ref[1]
    a_dir = 1 - 2 * (band % 2)
    core_dl = 1 + 2 * (lon % 2)
    for q in range(12):
        db, dl = q // 4 - 1, q % 4
        if db == 0:
            way = 0
        else:
            way = jnp.where(a_dir == db, 3, 6)
        if dl == 0:
            group = way
        elif dl == 2:
            group = 6 if db == 0 else 9
        else:
            group = jnp.where(core_dl == dl, 1, 2) + way
        table[q] = group * 32
        count[q] = 0
    buf[...] = jnp.zeros_like(buf)
    for copy in copies:
        copy.wait()

    def one(j, carry):
        block = src_ref[j]
        for t in range(2):
            q = routes_ref[t, j]
            rank = count[q]
            count[q] = rank + 1
            buf[table[q] + rank] = block
        return carry

    lax.fori_loop(0, src_ref.shape[0], one, 0, unroll=8)
    for group, out in enumerate(outs):
        out[...] = buf[group * 32 : group * 32 + 32]


def pack(pos, routes, source):
    fields, cells = source.shape[1:]
    shape = lambda n: jax.ShapeDtypeStruct((n, fields, cells), BF)
    return pl.pallas_call(
        pack_kernel,
        in_specs=[SM, HBM, HBM],
        out_specs=[VM] * 10,
        out_shape=[shape(32)] * 10,
        scratch_shapes=[
            pltpu.SMEM(routes.shape, jnp.int32),
            pltpu.VMEM(source.shape, BF),
            pltpu.VMEM((320, fields, cells), BF),
            pltpu.SMEM((12,), jnp.int32),
            pltpu.SMEM((12,), jnp.int32),
            pltpu.SemaphoreType.DMA((2,)),
        ],
        compiler_params=params(16),
        cost_estimate=cost(0, 1 << 20),
        name="pack",
    )(pos, *in_hbm(routes, source))


def prep_kernel(stem_ref, bias_ref, mix_ref, ws_ref, bs_ref, wm_ref):
    for par in range(2):
        bs_ref[:, par * 128 : par * 128 + 128] = bias_ref[...] * SCALE
    zero8 = jnp.zeros((8, 128), F32)
    taps = [stem_ref[t].astype(F32) * SCALE for t in range(9)]
    for i in range(STEP):
        for par in range(2):
            rows = []
            for d in range(4):
                for row in range(8):
                    a, b = row - i, d - par
                    rows.append(taps[3 * a + b] if 0 <= a < 3 and 0 <= b < 3 else zero8)
            lane = (2 * i + par) * 128
            ws_ref[:, lane : lane + 128] = jnp.concatenate(rows, axis=0).astype(BF)
    zero = jnp.zeros((128, 128), BF)
    for b in range(3):
        w = [mix_ref[3 * a + b].astype(F32) for a in range(3)]
        mean = 0.5 * (w[0] + w[2])
        forms = [w[0], mean + 0.5 * w[1], mean - 0.5 * w[1], w[2]]
        for k in range(4):
            for par in range(2):
                d = b + par
                wm_ref[k, d * 128 : d * 128 + 128, par * 128 : par * 128 + 128] = forms[k].astype(BF)
    for k in range(4):
        wm_ref[k, 0:128, 128:256] = zero
        wm_ref[k, 384:512, 0:128] = zero


def prep(stem_weight, stem_bias, mix_weight):
    return pl.pallas_call(
        prep_kernel,
        in_specs=[VM] * 3,
        out_specs=[VM] * 3,
        out_shape=[
            jax.ShapeDtypeStruct((256, STEP * 256), BF),
            jax.ShapeDtypeStruct((1, 256), F32),
            jax.ShapeDtypeStruct((4, 512, 256), BF),
        ],
        compiler_params=params(12),
        cost_estimate=cost(0, 2 << 20),
        name="prep",
    )(*in_hbm(stem_weight, stem_bias[None], mix_weight))


def add_groups(codes_ref, win_ref, w_hbm, w_ref, sem, inc, acc, arrays, first):
    def copy(g):
        return pltpu.make_async_copy(w_hbm.at[0, codes_ref[first + g]], w_ref.at[g], sem.at[g])

    for g in range(len(arrays)):
        copy(g).start()
    for g, array in enumerate(arrays):
        inc[g] = array[...]

    def group(g, carry):
        copy(g).wait()
        q = codes_ref[first + g]
        for s in range(0, 32, 2):
            pair = jnp.dot(
                inc[g, s : s + 2].reshape(16, 128),
                jnp.concatenate([w_ref[g, s], w_ref[g, s + 1]], axis=1),
                preferred_element_type=F32,
            )
            for i in range(2):
                part = pair[8 * i : 8 * i + 8, 128 * i : 128 * i + 128]
                w = win_ref[0, q, s + i]
                place = (w % 4) * ROWS + w // 4
                acc[place] = acc[place] + part.astype(BF).astype(F32)
        return carry

    lax.fori_loop(0, len(arrays), group, 0)


def near_kernel(codes_ref, win_ref, own_ref, core_ref, x_ref, w_hbm, acc, w_ref, inc, sem):
    acc[...] = jnp.zeros_like(acc)
    add_groups(codes_ref, win_ref, w_hbm, w_ref, sem, inc, acc, [own_ref, core_ref, x_ref], 0)


def far_kernel(codes_ref, win_ref, pos_ref, *refs):
    arrays, (near_ref, w_hbm, fld_ref, a_ref, b_ref, acc, w_ref, inc, sem) = refs[:7], refs[7:]
    acc[...] = near_ref[...]
    add_groups(codes_ref, win_ref, w_hbm, w_ref, sem, inc, acc, arrays, 3)
    for cb in range(4):
        rows = acc[cb * ROWS : (cb + 1) * ROWS].reshape(ROWS * 8, 128)
        fld_ref[:, cb * 128 : cb * 128 + 128] = rows.astype(BF)
    even = pos_ref[0] % 2 == 0
    top, bottom = fld_ref[0:16], fld_ref[ROWS * 8 - 16 : ROWS * 8]
    a_ref[...] = jnp.where(even, bottom, top)
    b_ref[...] = jnp.where(even, top, bottom)


def near_part(codes, win, own, core, x, weights):
    return pl.pallas_call(
        near_kernel,
        in_specs=[SM, SM] + [VM] * 3 + [HBM],
        out_specs=VM,
        out_shape=jax.ShapeDtypeStruct((ROWS * 4, 8, 128), F32),
        scratch_shapes=[
            pltpu.VMEM((3,) + weights.shape[2:], BF),
            pltpu.VMEM((3, 32, 8, 128), BF),
            pltpu.SemaphoreType.DMA((3,)),
        ],
        compiler_params=params(12),
        cost_estimate=cost(96 * 2 * 8 * 128 * 128, 4 << 20),
        name="near",
    )(codes, win, own, core, x, *in_hbm(weights))


def far_part(codes, win, pos, arrays, near, weights):
    return pl.pallas_call(
        far_kernel,
        in_specs=[SM, SM, SM] + [VM] * 8 + [HBM],
        out_specs=[VM] * 3,
        out_shape=[
            jax.ShapeDtypeStruct((ROWS * 8, COLS), BF),
            jax.ShapeDtypeStruct((16, COLS), BF),
            jax.ShapeDtypeStruct((16, COLS), BF),
        ],
        scratch_shapes=[
            pltpu.VMEM((ROWS * 4, 8, 128), F32),
            pltpu.VMEM((7,) + weights.shape[2:], BF),
            pltpu.VMEM((7, 32, 8, 128), BF),
            pltpu.SemaphoreType.DMA((7,)),
        ],
        compiler_params=params(16),
        cost_estimate=cost(224 * 2 * 8 * 128 * 128, 8 << 20),
        name="far",
    )(codes, win, pos, *arrays, near, *in_hbm(weights))


def tall(fld_ref, a, b, band, last):
    even = band % 2 == 0
    b = jnp.where((band == 0) | (band == last), jnp.zeros_like(b), b)
    north = jnp.where(even, b, a)
    south = jnp.where(even, a, b)
    return jnp.concatenate([north, fld_ref[...], south], axis=0)


def edge_kernel(last, pos_ref, fld_ref, a_ref, b_ref, edge_ref):
    whole = tall(fld_ref, a_ref[...], b_ref[...], pos_ref[0], last)
    rank = lax.broadcasted_iota(jnp.int32, (16, COLS), 0)
    col = lax.broadcasted_iota(jnp.int32, (16, COLS), 1)
    pick = ((rank < 2) & (col == rank)) | ((rank >= 2) & (rank < 4) & (col == COLS - 4 + rank))
    pick = jnp.where(pick, 1.0, 0.0).astype(BF)
    edge_ref[...] = lax.dot_general(
        pick, whole, (((1,), (1,)), ((), ())), preferred_element_type=F32
    ).astype(BF)


def edges(n_band, pos, fld, a, b):
    return pl.pallas_call(
        functools.partial(edge_kernel, n_band - 1),
        in_specs=[SM, VM, VM, VM],
        out_specs=VM,
        out_shape=jax.ShapeDtypeStruct((16, (ROWS + 4) * 8), BF),
        compiler_params=params(8),
        cost_estimate=cost(0, 1 << 20),
        name="edges",
    )(pos, fld, a, b)


def spread_kernel(fld_ref, g_ref, hot_ref):
    c = lax.broadcasted_iota(jnp.int32, (COLS, 256), 0)
    lane = lax.broadcasted_iota(jnp.int32, (COLS, 256), 1)
    for tile in range(3):
        n = lane % 128 + tile * 128
        j = jnp.where(n < PAIRS, SUB * (n % SUB) + n // SUB, SUB * (n - PAIRS + 1))
        gap = jnp.where(n < HROWS, c - 2 * j - lane // 128, -COLS)
        for pair in range(2):
            hot = jnp.where(gap == 2 * pair - 2, 1.0, 0.0)
            hot_ref[:, (2 * tile + pair) * 256 : (2 * tile + pair) * 256 + 256] = hot.astype(BF)
    zero = jnp.zeros((16, 256), BF)
    for pair in range(2):
        for tile in range(3):
            at = (2 * tile + pair) * 256
            value = jnp.dot(fld_ref[...], hot_ref[:, at : at + 256], preferred_element_type=F32)
            value = jnp.concatenate([zero, value.astype(BF), zero], axis=0)
            for half in range(2):
                d0 = (2 * pair + half) * 64
                for m in range(BLOCKS):
                    g_ref[m, d0 : d0 + 64, tile * 128 : tile * 128 + 128] = value[
                        48 * m : 48 * m + 64, half * 128 : half * 128 + 128
                    ]


def spread(fld):
    return pl.pallas_call(
        spread_kernel,
        in_specs=[VM],
        out_specs=[VM] * 2,
        out_shape=[
            jax.ShapeDtypeStruct((BLOCKS, 256, LANES), BF),
            jax.ShapeDtypeStruct((COLS, 6 * 256), BF),
        ],
        compiler_params=params(12),
        cost_estimate=cost(2 * 512 * 512 * 1536, 4 << 20),
        name="spread",
    )(fld)


def halos(last, pos_ref, a_ref, b_ref, core_ref, x_ref, hot_ref, rim, left_ref, right_ref):
    band = pos_ref[0]
    a, b = a_ref[...], b_ref[...]
    b = jnp.where((band == 0) | (band == last), jnp.zeros_like(b), b)
    even = band % 2 == 0
    rows = jnp.concatenate([jnp.where(even, b, a), jnp.where(even, a, b)], axis=0)
    rim[...] = jnp.zeros_like(rim)
    for pair in range(2):
        for tile in range(3):
            at = (2 * tile + pair) * 256
            value = jnp.dot(rows, hot_ref[:, at : at + 256], preferred_element_type=F32).astype(BF)
            for half in range(2):
                d0 = (2 * pair + half) * 64
                lanes = slice(tile * 128, tile * 128 + 128)
                part = value[:, half * 128 : half * 128 + 128]
                rim[0, d0 : d0 + 16, lanes] = part[0:16]
                rim[1, d0 + 48 : d0 + 64, lanes] = part[16:32]
    even = pos_ref[1] % 2 == 0
    core, x = core_ref[...].astype(F32), x_ref[...].astype(F32)
    right, left = jnp.where(even, core, x), jnp.where(even, x, core)
    hr = lax.broadcasted_iota(jnp.int32, (16, 256), 0)
    hl = lax.broadcasted_iota(jnp.int32, (16, 256), 1)
    for side, base, at, out in ((left, 2, 0, left_ref), (right, 0, SUB - 1, right_ref)):
        hot = ((hl % 128) == at) & (hr == hl // 128 + base)
        value = lax.dot_general(
            side.astype(BF),
            jnp.where(hot, 1.0, 0.0).astype(BF),
            (((0,), (0,)), ((), ())),
            preferred_element_type=F32,
        ).astype(BF)
        for m in range(BLOCKS):
            for half in range(2):
                out[m, half * 64 : half * 64 + 64] = value[
                    48 * m : 48 * m + 64, half * 128 : half * 128 + 128
                ]


def conv_kernel(
    last,
    pos_ref,
    g_ref,
    a_ref,
    b_ref,
    core_ref,
    x_ref,
    ws_ref,
    bs_ref,
    wm_ref,
    bm_ref,
    hot_ref,
    out_ref,
    rim,
    left_ref,
    right_ref,
    hs,
    ys,
    yb,
    sem,
):
    band = pos_ref[0]

    def stem(block, which, low, high):
        block_in = jnp.minimum(block, BLOCKS - 1)
        edge = jnp.where(block_in == 0, 0, jnp.where(block_in == BLOCKS - 1, 1, 2))
        x = g_ref[block_in] + rim[edge]
        first = jnp.concatenate([x[:128, :128] + left_ref[block_in], x[128:, :128]], axis=0)
        final = jnp.concatenate([x[:128, 256:], x[128:, 256:] + right_ref[block_in]], axis=0)
        x = jnp.concatenate([first, x[:, 128:256], final], axis=1)[:, :HROWS]
        for i in which:
            t = lax.dot_general(
                x,
                ws_ref[:, i * 256 : i * 256 + 256],
                (((0,), (0,)), ((), ())),
                preferred_element_type=F32,
            )
            t = t + bs_ref[...]
            h = t + t * jnp.tanh(t)
            if i == 0 and low is not None:
                h = h * low
            if i == STEP - 1 and high is not None:
                h = h * high
            hs[block % 2, i] = h.astype(BF)

    halos(last, pos_ref, a_ref, b_ref, core_ref, x_ref, hot_ref, rim, left_ref, right_ref)
    stem(0, range(STEP), jnp.where(band == 0, 0.0, 1.0), None)

    def copy(at, slot):
        return pltpu.make_async_copy(
            yb.at[slot], out_ref.at[pl.ds(6 * at - 2, 6)], sem.at[slot]
        )

    first = pltpu.make_async_copy(yb.at[0, pl.ds(2, 4)], out_ref.at[pl.ds(0, 4)], sem.at[0])

    def step(s, carry):
        slot = s % 2

        @pl.when(s == 2)
        def _():
            first.wait()

        @pl.when(s > 2)
        def _():
            copy(s - 2, slot).wait()

        rows = [(1 - slot, 4), (1 - slot, 5)] + [(slot, i) for i in range(STEP)]
        keep_last = jnp.where((s == BLOCKS - 2) & (band == last), 0.0, 1.0)

        def mix(t):
            for c in range(PAIRS // CHUNK):
                row0 = c * CHUNK

                def both(r):
                    return jnp.concatenate(
                        [hs[rows[2 * t + r]][row0 + k * SUB : row0 + k * SUB + CHUNK] for k in range(2)],
                        axis=1,
                    )

                h = [both(r) for r in range(4)]
                v = [h[0] - h[2], h[1] + h[2], h[2] - h[1], h[1] - h[3]]
                m = [jnp.dot(v[k], wm_ref[k], preferred_element_type=F32) for k in range(4)]
                plus, minus = m[1] + m[2], m[1] - m[2]
                for q, y in enumerate([plus + m[0], minus - m[3]]):
                    row = 2 * t + q
                    for par in range(2):
                        part = y[:, par * 128 : par * 128 + 128] + bm_ref[...]
                        for k in range(CHUNK // SUB):
                            to = pl.ds(2 * (c * CHUNK // SUB + k) + par, SUB, stride=PITCH)
                            ys[row, to, :] = part[k * SUB : k * SUB + SUB]
            for q in range(2):
                for a in range(SUB):
                    yb[slot, 2 * t + q, 2 * SUB * a : 2 * SUB * a + 2 * SUB] = ys[
                        2 * t + q, PITCH * a : PITCH * a + 2 * SUB
                    ].astype(BF)

        for t in range(STEP // 2):
            mix(t)
        stem(s + 1, range(STEP), None, keep_last)

        @pl.when(s == 0)
        def _():
            first.start()

        @pl.when(s > 0)
        def _():
            copy(s, slot).start()
        return carry

    lax.fori_loop(0, BLOCKS, step, 0)
    copy(BLOCKS - 2, (BLOCKS - 2) % 2).wait()
    copy(BLOCKS - 1, (BLOCKS - 1) % 2).wait()


def conv(n_band, pos, g, a, b, core, x, ws, bs, wm, bm, hot):
    channels = bm.shape[-1]
    return pl.pallas_call(
        functools.partial(conv_kernel, n_band - 1),
        in_specs=[SM] + [VM] * 10,
        out_specs=ANY,
        out_shape=jax.ShapeDtypeStruct((ROWS, COLS, channels), BF),
        scratch_shapes=[
            pltpu.VMEM((3, 256, LANES), BF),
            pltpu.VMEM((BLOCKS, 128, 128), BF),
            pltpu.VMEM((BLOCKS, 128, 128), BF),
            pltpu.VMEM((2, STEP, HROWS, 256), BF),
            pltpu.VMEM((STEP, SUB * PITCH, channels), F32),
            pltpu.VMEM((2, STEP, COLS, channels), BF),
            pltpu.SemaphoreType.DMA((2,)),
        ],
        compiler_params=params(20),
        cost_estimate=cost(2 * ROWS * COLS * 9 * 128 * 128, 12 << 20),
        name="conv",
    )(pos, g, a, b, core, x, ws, bs, wm, bm, hot)


def on_device(source, routes, slot_weights, window, stem_weight, stem_bias, mix_weight, mix_bias):
    n_band = lax.axis_size("band")
    n_lon = lax.axis_size("lon")
    axes = ("band", "lon")
    band = lax.axis_index("band")
    lon = lax.axis_index("lon")

    def move(value, way, turn):
        return lax.ppermute(value, axes, swap(n_band, n_lon, way, turn))

    pos = jnp.stack([band, lon]).astype(jnp.int32)
    core_dl = jnp.where(lon % 2 == 0, 3, 1)
    x_dl = 4 - core_dl
    a_base = jnp.where(band % 2 == 0, 0, 8)
    b_base = 8 - a_base
    rim = (band == 0) | (band == n_band - 1)
    far_code = jnp.where(band < n_band // 2, 10, 2)
    near = [4 + 0 * lon, 4 + core_dl, 4 + x_dl]
    along_a = [a_base, a_base + core_dl, a_base + x_dl]
    along_b = [jnp.where(rim, 6, b_base), b_base + core_dl, b_base + x_dl]
    codes = jnp.stack(near + along_a + along_b + [far_code]).astype(jnp.int32)

    turns = ("stay", "core", "x")
    out = pack(pos, routes.T, source)
    arrays = [move(out[3 + i], "a", turn) for i, turn in enumerate(turns)]
    arrays += [move(out[6 + i], "b", turn) for i, turn in enumerate(turns)]
    arrays.append(move(out[9], "a", "across"))
    core, x = move(out[1], "", "core"), move(out[2], "", "x")
    near = near_part(codes, window, out[0], core, x, slot_weights)
    fld, a_row, b_row = far_part(codes, window, pos, arrays, near, slot_weights)
    a_halo = move(a_row, "a", "stay")
    b_halo = move(b_row, "b", "stay")
    g, hot = spread(fld)
    a_halo, b_halo, g, hot = lax.optimization_barrier((a_halo, b_halo, g, hot))
    edge = edges(n_band, pos, fld, a_halo, b_halo)
    core_edge = move(edge, "", "core")
    x_edge = move(edge, "", "x")
    ws, bs, wm = prep(stem_weight, stem_bias, mix_weight)
    return conv(
        n_band, pos, g, a_halo, b_halo, core_edge, x_edge, ws, bs, wm, mix_bias[None], hot
    )


def solution(mesh):
    both = ("band", "lon")
    in_specs = (
        P(both, None, None),
        P(both, None),
        P(both, None, None, None, None),
        P(both, None, None),
        P(),
        P(),
        P(),
        P(),
    )
    return jax.shard_map(
        on_device, mesh=mesh, in_specs=in_specs, out_specs=P("band", "lon", None), check_vma=False
    )
```

```python
import functools

import jax
import jax.numpy as jnp
from jax import lax
from jax.experimental import pallas as pl
from jax.experimental.pallas import tpu as pltpu
from jax.sharding import PartitionSpec as P

ROWS = 64
COLS = 512
PAIRS = COLS // 2
SUB = 16
HROWS = PAIRS + SUB
PITCH = 2 * SUB + 1
LANES = 384
CHUNK = 256
NEAR, FAR = 3, 7
EARLY = 4
STEP = 6
BLOCKS = (ROWS + 2) // STEP
SCALE = 1.0 / 2.0
BF = jnp.bfloat16
F32 = jnp.float32
VM = pl.BlockSpec(memory_space=pltpu.VMEM)
SM = pl.BlockSpec(memory_space=pltpu.SMEM)
ANY = pl.BlockSpec(memory_space=pl.ANY)
HBM = pl.BlockSpec(memory_space=pltpu.HBM)


def params(mib):
    return pltpu.CompilerParams(vmem_limit_bytes=mib << 20)


def cost(flops, size):
    return pl.CostEstimate(flops=flops, bytes_accessed=size, transcendentals=0)


def swap(n_band, n_lon, way, turn):
    pairs = []
    for b in range(n_band):
        if way == "a":
            partner = b ^ 1
        elif way == "b":
            partner = b + 1 if b % 2 else b - 1
        else:
            partner = b
        for l in range(n_lon):
            target = {"stay": l, "core": l ^ 1, "x": n_lon - 1 - l, "across": (l + 2) % n_lon}[turn]
            if not 0 <= partner < n_band:
                spare = (l + 2) % n_lon if turn == "stay" else l ^ 1
                pairs.append((b * n_lon + l, b * n_lon + spare))
            else:
                pairs.append((b * n_lon + l, partner * n_lon + target))
    return pairs


def in_hbm(*arrays):
    return [pltpu.with_memory_space_constraint(a, pltpu.HBM) for a in arrays]


def pack_kernel(routes_hbm, src_hbm, *refs):
    outs, (routes_ref, src_ref, buf, place, sem) = refs[:10], refs[10:]
    copies = [
        pltpu.make_async_copy(routes_hbm, routes_ref, sem.at[0]),
        pltpu.make_async_copy(src_hbm, src_ref, sem.at[1]),
    ]
    for copy in copies:
        copy.start()
    band, lon = lax.axis_index("band"), lax.axis_index("lon")
    a_dir = 1 - 2 * (band % 2)
    core_dl = 1 + 2 * (lon % 2)
    for q in range(12):
        db, dl = q // 4 - 1, q % 4
        if db == 0:
            way = 0
        else:
            way = jnp.where(a_dir == db, 3, 6)
        if dl == 0:
            group = way
        elif dl == 2:
            group = 6 if db == 0 else 9
        else:
            group = jnp.where(core_dl == dl, 1, 2) + way
        place[q] = group * 32
    buf[...] = jnp.zeros_like(buf)
    for copy in copies:
        copy.wait()

    def one(j, carry):
        block = src_ref[j]
        for t in range(2):
            q = routes_ref[t, j]
            at = place[q]
            place[q] = at + 1
            buf[at] = block
        return carry

    lax.fori_loop(0, src_ref.shape[0], one, 0, unroll=8)
    for group, out in enumerate(outs):
        out[...] = buf[group * 32 : group * 32 + 32]


def pack(routes, source):
    fields, cells = source.shape[1:]
    shape = lambda n: jax.ShapeDtypeStruct((n, fields, cells), BF)
    return pl.pallas_call(
        pack_kernel,
        in_specs=[HBM, HBM],
        out_specs=[VM] * 10,
        out_shape=[shape(32)] * 10,
        scratch_shapes=[
            pltpu.SMEM(routes.shape, jnp.int32),
            pltpu.VMEM(source.shape, BF),
            pltpu.VMEM((320, fields, cells), BF),
            pltpu.SMEM((12,), jnp.int32),
            pltpu.SemaphoreType.DMA((2,)),
        ],
        compiler_params=params(16),
        cost_estimate=cost(0, 1 << 20),
        name="pack",
    )(*in_hbm(routes, source))


def prep_kernel(stem_ref, bias_ref, mix_ref, ws_ref, bs_ref, wm_ref):
    for par in range(2):
        bs_ref[:, par * 128 : par * 128 + 128] = bias_ref[...] * SCALE
    zero8 = jnp.zeros((8, 128), F32)
    taps = [stem_ref[t].astype(F32) * SCALE for t in range(9)]
    for i in range(STEP):
        for par in range(2):
            rows = []
            for d in range(4):
                for row in range(8):
                    a, b = row - i, d - par
                    rows.append(taps[3 * a + b] if 0 <= a < 3 and 0 <= b < 3 else zero8)
            lane = (2 * i + par) * 128
            ws_ref[:, lane : lane + 128] = jnp.concatenate(rows, axis=0).astype(BF)
    zero = jnp.zeros((128, 128), BF)
    for b in range(3):
        w = [mix_ref[3 * a + b].astype(F32) for a in range(3)]
        mean = 0.5 * (w[0] + w[2])
        forms = [w[0], mean + 0.5 * w[1], mean - 0.5 * w[1], w[2]]
        for k in range(4):
            for par in range(2):
                d = b + par
                wm_ref[k, d * 128 : d * 128 + 128, par * 128 : par * 128 + 128] = forms[k].astype(BF)
    for k in range(4):
        wm_ref[k, 0:128, 128:256] = zero
        wm_ref[k, 384:512, 0:128] = zero


def prep(stem_weight, stem_bias, mix_weight):
    return pl.pallas_call(
        prep_kernel,
        in_specs=[VM] * 3,
        out_specs=[VM] * 3,
        out_shape=[
            jax.ShapeDtypeStruct((256, STEP * 256), BF),
            jax.ShapeDtypeStruct((1, 256), F32),
            jax.ShapeDtypeStruct((4, 512, 256), BF),
        ],
        compiler_params=params(12),
        cost_estimate=cost(0, 2 << 20),
        name="prep",
    )(*in_hbm(stem_weight, stem_bias[None], mix_weight))


def group_codes(last, codes_ref):
    band, lon = lax.axis_index("band"), lax.axis_index("lon")
    core_dl = jnp.where(lon % 2 == 0, 3, 1)
    x_dl = 4 - core_dl
    a_base = jnp.where(band % 2 == 0, 0, 8)
    b_base = 8 - a_base
    rim = (band == 0) | (band == last)
    codes = [4, 4 + core_dl, 4 + x_dl]
    codes += [a_base, a_base + core_dl, a_base + x_dl]
    codes += [jnp.where(rim, 6, b_base), b_base + core_dl, b_base + x_dl]
    codes.append(jnp.where(band < (last + 1) // 2, 10, 2))
    for g, code in enumerate(codes):
        codes_ref[g] = jnp.int32(code)


def add_groups(codes_ref, win_ref, w_ref, inc, acc, first, begin, count, ready=None):
    def group(i, carry):
        if ready is not None:
            ready(i)
        q = codes_ref[first + begin + i]
        for s in range(0, 32, 2):
            pair = jnp.dot(
                inc[begin + i, s : s + 2].reshape(16, 128),
                jnp.concatenate([w_ref[i, s], w_ref[i, s + 1]], axis=1),
                preferred_element_type=F32,
            )
            for k in range(2):
                part = pair[8 * k : 8 * k + 8, 128 * k : 128 * k + 128]
                w = win_ref[q, 0, s + k]
                place = (w % 4) * ROWS + w // 4
                acc[place] = acc[place] + part.astype(BF).astype(F32)
        return carry

    lax.fori_loop(0, count, group, 0)


def near_kernel(last, win_hbm, own_ref, core_ref, x_ref, w_hbm, acc, early_ref, w_ref, inc, codes_ref, win_ref, sem, early_sem, win_sem):
    group_codes(last, codes_ref)
    window = pltpu.make_async_copy(win_hbm, win_ref, win_sem)
    window.start()

    def copy(g):
        return pltpu.make_async_copy(w_hbm.at[0, codes_ref[g]], w_ref.at[g], sem.at[g])

    early = [
        pltpu.make_async_copy(w_hbm.at[0, codes_ref[NEAR + g]], early_ref.at[g], early_sem.at[g])
        for g in range(EARLY)
    ]
    for g in range(NEAR):
        copy(g).start()
    for transfer in early:
        transfer.start()
    acc[...] = jnp.zeros_like(acc)
    for g, array in enumerate((own_ref, core_ref, x_ref)):
        inc[g] = array[...]
    window.wait()
    add_groups(codes_ref, win_ref, w_ref, inc, acc, 0, 0, NEAR, lambda g: copy(g).wait())
    for transfer in early:
        transfer.wait()


def far_kernel(last, win_hbm, *refs):
    arrays, (near_ref, early_ref, w_hbm, fld_ref, a_ref, b_ref) = refs[:7], refs[7:13]
    acc, w_ref, inc, codes_ref, win_ref, sem, win_sem = refs[13:]
    group_codes(last, codes_ref)
    window = pltpu.make_async_copy(win_hbm, win_ref, win_sem)
    window.start()

    def copy(g):
        return pltpu.make_async_copy(
            w_hbm.at[0, codes_ref[NEAR + EARLY + g]], w_ref.at[g], sem.at[g]
        )

    for g in range(FAR - EARLY):
        copy(g).start()
    acc[...] = near_ref[...]
    for g, array in enumerate(arrays):
        inc[g] = array[...]
    window.wait()
    add_groups(codes_ref, win_ref, early_ref, inc, acc, NEAR, 0, EARLY)
    add_groups(
        codes_ref, win_ref, w_ref, inc, acc, NEAR, EARLY, FAR - EARLY, lambda g: copy(g).wait()
    )
    for cb in range(4):
        rows = acc[cb * ROWS : (cb + 1) * ROWS].reshape(ROWS * 8, 128)
        fld_ref[:, cb * 128 : cb * 128 + 128] = rows.astype(BF)
    even = lax.axis_index("band") % 2 == 0
    top, bottom = fld_ref[0:16], fld_ref[ROWS * 8 - 16 : ROWS * 8]
    a_ref[...] = jnp.where(even, bottom, top)
    b_ref[...] = jnp.where(even, top, bottom)


def near_part(n_band, win, own, core, x, weights):
    group = weights.shape[2:]
    return pl.pallas_call(
        functools.partial(near_kernel, n_band - 1),
        in_specs=[HBM] + [VM] * 3 + [HBM],
        out_specs=[VM] * 2,
        out_shape=[
            jax.ShapeDtypeStruct((ROWS * 4, 8, 128), F32),
            jax.ShapeDtypeStruct((EARLY,) + group, BF),
        ],
        scratch_shapes=[
            pltpu.VMEM((NEAR,) + group, BF),
            pltpu.VMEM((NEAR, 32, 8, 128), BF),
            pltpu.SMEM((NEAR + FAR,), jnp.int32),
            pltpu.SMEM(win.shape, jnp.int32),
            pltpu.SemaphoreType.DMA((NEAR,)),
            pltpu.SemaphoreType.DMA((EARLY,)),
            pltpu.SemaphoreType.DMA,
        ],
        compiler_params=params(14),
        cost_estimate=cost(96 * 2 * 8 * 128 * 128, 12 << 20),
        name="near",
    )(*in_hbm(win), own, core, x, *in_hbm(weights))


def far_part(n_band, win, arrays, near, early, weights):
    group = weights.shape[2:]
    return pl.pallas_call(
        functools.partial(far_kernel, n_band - 1),
        in_specs=[HBM] + [VM] * 9 + [HBM],
        out_specs=[VM] * 3,
        out_shape=[
            jax.ShapeDtypeStruct((ROWS * 8, COLS), BF),
            jax.ShapeDtypeStruct((16, COLS), BF),
            jax.ShapeDtypeStruct((16, COLS), BF),
        ],
        scratch_shapes=[
            pltpu.VMEM((ROWS * 4, 8, 128), F32),
            pltpu.VMEM((FAR - EARLY,) + group, BF),
            pltpu.VMEM((FAR, 32, 8, 128), BF),
            pltpu.SMEM((NEAR + FAR,), jnp.int32),
            pltpu.SMEM(win.shape, jnp.int32),
            pltpu.SemaphoreType.DMA((FAR - EARLY,)),
            pltpu.SemaphoreType.DMA,
        ],
        compiler_params=params(14),
        cost_estimate=cost(224 * 2 * 8 * 128 * 128, 8 << 20),
        name="far",
    )(*in_hbm(win), *arrays, near, early, *in_hbm(weights))


def edge_kernel(last, fld_ref, a_ref, b_ref, edge_ref):
    band = lax.axis_index("band")
    a, b = a_ref[...], b_ref[...]
    b = jnp.where((band == 0) | (band == last), jnp.zeros_like(b), b)
    even = band % 2 == 0
    north, south = jnp.where(even, b, a), jnp.where(even, a, b)
    ends = []
    for lanes in (slice(0, 128), slice(COLS - 128, COLS)):
        ends.append(jnp.concatenate([north[:, lanes], fld_ref[:, lanes], south[:, lanes]], axis=0))
    rank = lax.broadcasted_iota(jnp.int32, (16, 256), 0)
    col = lax.broadcasted_iota(jnp.int32, (16, 256), 1)
    pick = ((rank < 2) & (col == rank)) | ((rank >= 2) & (rank < 4) & (col == 252 + rank))
    edge_ref[...] = lax.dot_general(
        jnp.where(pick, 1.0, 0.0).astype(BF),
        jnp.concatenate(ends, axis=1),
        (((1,), (1,)), ((), ())),
        preferred_element_type=F32,
    ).astype(BF)


def edges(n_band, fld, a, b):
    return pl.pallas_call(
        functools.partial(edge_kernel, n_band - 1),
        in_specs=[VM, VM, VM],
        out_specs=VM,
        out_shape=jax.ShapeDtypeStruct((16, (ROWS + 4) * 8), BF),
        compiler_params=params(8),
        cost_estimate=cost(0, 1 << 20),
        name="edges",
    )(fld, a, b)


def spread_kernel(fld_ref, g_ref, hot_ref):
    c = lax.broadcasted_iota(jnp.int32, (COLS, 256), 0)
    lane = lax.broadcasted_iota(jnp.int32, (COLS, 256), 1)
    for tile in range(3):
        n = lane % 128 + tile * 128
        j = jnp.where(n < PAIRS, SUB * (n % SUB) + n // SUB, SUB * (n - PAIRS + 1))
        gap = jnp.where(n < HROWS, c - 2 * j - lane // 128, -COLS)
        for pair in range(2):
            hot = jnp.where(gap == 2 * pair - 2, 1.0, 0.0)
            hot_ref[:, (2 * tile + pair) * 256 : (2 * tile + pair) * 256 + 256] = hot.astype(BF)
    zero = jnp.zeros((16, 256), BF)
    for pair in range(2):
        for tile in range(3):
            at = (2 * tile + pair) * 256
            value = jnp.dot(fld_ref[...], hot_ref[:, at : at + 256], preferred_element_type=F32)
            value = jnp.concatenate([zero, value.astype(BF), zero], axis=0)
            for half in range(2):
                d0 = (2 * pair + half) * 64
                for m in range(BLOCKS):
                    g_ref[m, d0 : d0 + 64, tile * 128 : tile * 128 + 128] = value[
                        48 * m : 48 * m + 64, half * 128 : half * 128 + 128
                    ]


def spread(fld):
    return pl.pallas_call(
        spread_kernel,
        in_specs=[VM],
        out_specs=[VM] * 2,
        out_shape=[
            jax.ShapeDtypeStruct((BLOCKS, 256, LANES), BF),
            jax.ShapeDtypeStruct((COLS, 6 * 256), BF),
        ],
        compiler_params=params(12),
        cost_estimate=cost(2 * 512 * 512 * 1536, 4 << 20),
        name="spread",
    )(fld)


def halos(last, a_ref, b_ref, core_ref, x_ref, hot_ref, rim, left_ref, right_ref):
    band = lax.axis_index("band")
    a, b = a_ref[...], b_ref[...]
    b = jnp.where((band == 0) | (band == last), jnp.zeros_like(b), b)
    even = band % 2 == 0
    rows = jnp.concatenate([jnp.where(even, b, a), jnp.where(even, a, b)], axis=0)
    rim[...] = jnp.zeros_like(rim)
    for pair in range(2):
        for tile in range(3):
            at = (2 * tile + pair) * 256
            value = jnp.dot(rows, hot_ref[:, at : at + 256], preferred_element_type=F32).astype(BF)
            for half in range(2):
                d0 = (2 * pair + half) * 64
                lanes = slice(tile * 128, tile * 128 + 128)
                part = value[:, half * 128 : half * 128 + 128]
                rim[0, d0 : d0 + 16, lanes] = part[0:16]
                rim[1, d0 + 48 : d0 + 64, lanes] = part[16:32]
    even = lax.axis_index("lon") % 2 == 0
    core, x = core_ref[...].astype(F32), x_ref[...].astype(F32)
    right, left = jnp.where(even, core, x), jnp.where(even, x, core)
    hr = lax.broadcasted_iota(jnp.int32, (16, 256), 0)
    hl = lax.broadcasted_iota(jnp.int32, (16, 256), 1)
    for side, base, at, out in ((left, 2, 0, left_ref), (right, 0, SUB - 1, right_ref)):
        hot = ((hl % 128) == at) & (hr == hl // 128 + base)
        value = lax.dot_general(
            side.astype(BF),
            jnp.where(hot, 1.0, 0.0).astype(BF),
            (((0,), (0,)), ((), ())),
            preferred_element_type=F32,
        ).astype(BF)
        for m in range(BLOCKS):
            for half in range(2):
                out[m, half * 64 : half * 64 + 64] = value[
                    48 * m : 48 * m + 64, half * 128 : half * 128 + 128
                ]


def conv_kernel(
    last,
    g_ref,
    a_ref,
    b_ref,
    core_ref,
    x_ref,
    ws_ref,
    bs_ref,
    wm_ref,
    bm_ref,
    hot_ref,
    out_ref,
    rim,
    left_ref,
    right_ref,
    hs,
    ys,
    yb,
    sem,
):
    band = lax.axis_index("band")

    def stem(block, which, low, high):
        block_in = jnp.minimum(block, BLOCKS - 1)
        edge = jnp.where(block_in == 0, 0, jnp.where(block_in == BLOCKS - 1, 1, 2))
        x = g_ref[block_in] + rim[edge]
        first = jnp.concatenate([x[:128, :128] + left_ref[block_in], x[128:, :128]], axis=0)
        final = jnp.concatenate([x[:128, 256:], x[128:, 256:] + right_ref[block_in]], axis=0)
        x = jnp.concatenate([first, x[:, 128:256], final], axis=1)[:, :HROWS]
        for i in which:
            t = lax.dot_general(
                x,
                ws_ref[:, i * 256 : i * 256 + 256],
                (((0,), (0,)), ((), ())),
                preferred_element_type=F32,
            )
            t = t + bs_ref[...]
            h = t + t * jnp.tanh(t)
            if i == 0 and low is not None:
                h = h * low
            if i == STEP - 1 and high is not None:
                h = h * high
            hs[block % 2, i] = h.astype(BF)

    halos(last, a_ref, b_ref, core_ref, x_ref, hot_ref, rim, left_ref, right_ref)
    stem(0, range(STEP), jnp.where(band == 0, 0.0, 1.0), None)

    def copy(at, slot):
        return pltpu.make_async_copy(
            yb.at[slot], out_ref.at[pl.ds(6 * at - 2, 6)], sem.at[slot]
        )

    first = pltpu.make_async_copy(yb.at[0, pl.ds(2, 4)], out_ref.at[pl.ds(0, 4)], sem.at[0])

    def step(s, carry):
        slot = s % 2

        @pl.when(s == 2)
        def _():
            first.wait()

        @pl.when(s > 2)
        def _():
            copy(s - 2, slot).wait()

        rows = [(1 - slot, 4), (1 - slot, 5)] + [(slot, i) for i in range(STEP)]
        keep_last = jnp.where((s == BLOCKS - 2) & (band == last), 0.0, 1.0)

        def mix(t):
            for c in range(PAIRS // CHUNK):
                row0 = c * CHUNK

                def both(r):
                    return jnp.concatenate(
                        [hs[rows[2 * t + r]][row0 + k * SUB : row0 + k * SUB + CHUNK] for k in range(2)],
                        axis=1,
                    )

                h = [both(r) for r in range(4)]
                v = [h[0] - h[2], h[1] + h[2], h[2] - h[1], h[1] - h[3]]
                m = [jnp.dot(v[k], wm_ref[k], preferred_element_type=F32) for k in range(4)]
                plus, minus = m[1] + m[2], m[1] - m[2]
                for q, y in enumerate([plus + m[0], minus - m[3]]):
                    row = 2 * t + q
                    for par in range(2):
                        part = y[:, par * 128 : par * 128 + 128] + bm_ref[...]
                        for k in range(CHUNK // SUB):
                            to = pl.ds(2 * (c * CHUNK // SUB + k) + par, SUB, stride=PITCH)
                            ys[row, to, :] = part[k * SUB : k * SUB + SUB]
            for q in range(2):
                for a in range(SUB):
                    yb[slot, 2 * t + q, 2 * SUB * a : 2 * SUB * a + 2 * SUB] = ys[
                        2 * t + q, PITCH * a : PITCH * a + 2 * SUB
                    ].astype(BF)

        for t in range(STEP // 2):
            mix(t)
        stem(s + 1, range(STEP), None, keep_last)

        @pl.when(s == 0)
        def _():
            first.start()

        @pl.when(s > 0)
        def _():
            copy(s, slot).start()
        return carry

    lax.fori_loop(0, BLOCKS, step, 0)
    copy(BLOCKS - 2, (BLOCKS - 2) % 2).wait()
    copy(BLOCKS - 1, (BLOCKS - 1) % 2).wait()


def conv(n_band, g, a, b, core, x, ws, bs, wm, bm, hot):
    channels = bm.shape[-1]
    return pl.pallas_call(
        functools.partial(conv_kernel, n_band - 1),
        in_specs=[VM] * 10,
        out_specs=ANY,
        out_shape=jax.ShapeDtypeStruct((ROWS, COLS, channels), BF),
        scratch_shapes=[
            pltpu.VMEM((3, 256, LANES), BF),
            pltpu.VMEM((BLOCKS, 128, 128), BF),
            pltpu.VMEM((BLOCKS, 128, 128), BF),
            pltpu.VMEM((2, STEP, HROWS, 256), BF),
            pltpu.VMEM((STEP, SUB * PITCH, channels), F32),
            pltpu.VMEM((2, STEP, COLS, channels), BF),
            pltpu.SemaphoreType.DMA((2,)),
        ],
        compiler_params=params(20),
        cost_estimate=cost(2 * ROWS * COLS * 9 * 128 * 128, 12 << 20),
        name="conv",
    )(g, a, b, core, x, ws, bs, wm, bm, hot)


def on_device(source, routes, slot_weights, window, stem_weight, stem_bias, mix_weight, mix_bias):
    n_band = lax.axis_size("band")
    n_lon = lax.axis_size("lon")
    axes = ("band", "lon")

    def move(value, way, turn):
        return lax.ppermute(value, axes, swap(n_band, n_lon, way, turn))

    turns = ("stay", "core", "x")
    out = pack(routes.T, source)
    win = window.transpose(1, 0, 2)
    arrays = [move(out[3 + i], "a", turn) for i, turn in enumerate(turns)]
    arrays += [move(out[6 + i], "b", turn) for i, turn in enumerate(turns)]
    arrays.append(move(out[9], "a", "across"))
    core, x = move(out[1], "", "core"), move(out[2], "", "x")
    near, early = near_part(n_band, win, out[0], core, x, slot_weights)
    fld, a_row, b_row = far_part(n_band, win, arrays, near, early, slot_weights)
    a_halo = move(a_row, "a", "stay")
    b_halo = move(b_row, "b", "stay")
    g, hot = spread(fld)
    a_halo, b_halo, g, hot = lax.optimization_barrier((a_halo, b_halo, g, hot))
    edge = edges(n_band, fld, a_halo, b_halo)
    core_edge = move(edge, "", "core")
    x_edge = move(edge, "", "x")
    ws, bs, wm = prep(stem_weight, stem_bias, mix_weight)
    return conv(
        n_band, g, a_halo, b_halo, core_edge, x_edge, ws, bs, wm, mix_bias[None], hot
    )


def solution(mesh):
    both = ("band", "lon")
    in_specs = (
        P(both, None, None),
        P(both, None),
        P(both, None, None, None, None),
        P(both, None, None),
        P(),
        P(),
        P(),
        P(),
    )
    return jax.shard_map(
        on_device, mesh=mesh, in_specs=in_specs, out_specs=P("band", "lon", None), check_vma=False
    )
```

```python
import functools

import jax
import jax.numpy as jnp
from jax import lax
from jax.experimental import pallas as pl
from jax.experimental.pallas import tpu as pltpu
from jax.sharding import PartitionSpec as P

ROWS = 64
COLS = 512
PAIRS = COLS // 2
SUB = 16
HROWS = PAIRS + SUB
PITCH = 2 * SUB + 1
LANES = 384
CHUNK = 256
NEAR, FAR = 3, 7
EARLY = 2
STEP = 6
BLOCKS = (ROWS + 2) // STEP
SCALE = 1.0 / 2.0
BF = jnp.bfloat16
F32 = jnp.float32
VM = pl.BlockSpec(memory_space=pltpu.VMEM)
SM = pl.BlockSpec(memory_space=pltpu.SMEM)
ANY = pl.BlockSpec(memory_space=pl.ANY)
HBM = pl.BlockSpec(memory_space=pltpu.HBM)


def params(mib):
    return pltpu.CompilerParams(vmem_limit_bytes=mib << 20)


def cost(flops, size):
    return pl.CostEstimate(flops=flops, bytes_accessed=size, transcendentals=0)


def swap(n_band, n_lon, way, turn):
    pairs = []
    for b in range(n_band):
        if way == "a":
            partner = b ^ 1
        elif way == "b":
            partner = b + 1 if b % 2 else b - 1
        else:
            partner = b
        for l in range(n_lon):
            target = {"stay": l, "core": l ^ 1, "x": n_lon - 1 - l, "x_rim": n_lon - 1 - l}[turn]
            if not 0 <= partner < n_band or (turn == "x_rim" and 2 <= b < n_band - 2):
                pairs.append((b * n_lon + l, b * n_lon + (l ^ 1)))
            else:
                pairs.append((b * n_lon + l, partner * n_lon + target))
    return pairs


def in_hbm(*arrays):
    return [pltpu.with_memory_space_constraint(a, pltpu.HBM) for a in arrays]


PARTS = ((0, 1), (1, 5), (6, 1), (7, 1), (8, 1), (9, 1), (10, 1))


def pack_kernel(routes_hbm, src_hbm, *refs):
    outs, (routes_ref, src_ref, buf, place, sem) = refs[:7], refs[7:]
    copies = [
        pltpu.make_async_copy(routes_hbm, routes_ref, sem.at[0]),
        pltpu.make_async_copy(src_hbm, src_ref, sem.at[1]),
    ]
    for copy in copies:
        copy.start()
    band, lon = lax.axis_index("band"), lax.axis_index("lon")
    a_dir = 1 - 2 * (band % 2)
    core_dl = 1 + 2 * (lon % 2)
    for q in range(12):
        db, dl = q // 4 - 1, q % 4
        if dl == 2:
            group = 5 if db == 0 else 4
        elif db == 0:
            group = 0 if dl == 0 else jnp.where(core_dl == dl, 1, 6)
        elif dl == 0:
            group = jnp.where(a_dir == db, 7, 9)
        else:
            group = jnp.where(core_dl == dl, jnp.where(a_dir == db, 2, 3), jnp.where(a_dir == db, 8, 10))
        place[q] = group * 32
    buf[...] = jnp.zeros_like(buf)
    for copy in copies:
        copy.wait()

    def one(j, carry):
        block = src_ref[j]
        for t in range(2):
            q = routes_ref[t, j]
            at = place[q]
            place[q] = at + 1
            buf[at] = block
        return carry

    lax.fori_loop(0, src_ref.shape[0], one, 0, unroll=8)
    for out, (begin, groups) in zip(outs, PARTS):
        out[...] = buf[begin * 32 : (begin + groups) * 32]


def pack(routes, source):
    fields, cells = source.shape[1:]
    shape = lambda n: jax.ShapeDtypeStruct((n, fields, cells), BF)
    return pl.pallas_call(
        pack_kernel,
        in_specs=[HBM, HBM],
        out_specs=[VM] * 7,
        out_shape=[shape(32 * groups) for _, groups in PARTS],
        scratch_shapes=[
            pltpu.SMEM(routes.shape, jnp.int32),
            pltpu.VMEM(source.shape, BF),
            pltpu.VMEM((352, fields, cells), BF),
            pltpu.SMEM((12,), jnp.int32),
            pltpu.SemaphoreType.DMA((2,)),
        ],
        compiler_params=params(16),
        cost_estimate=cost(0, 1 << 20),
        name="pack",
    )(*in_hbm(routes, source))


def merge_kernel(core_ref, x_ref, a_ref, b_ref, x_out, a_out, b_out, far_out):
    for out, mine, group in ((x_out, x_ref, 4), (a_out, a_ref, 1), (b_out, b_ref, 2)):
        out[0:32] = mine[...]
        out[32:64] = core_ref[group * 32 : group * 32 + 32]
    far_out[...] = core_ref[96:128]


def merge(core, x, a, b):
    shape = lambda n: jax.ShapeDtypeStruct((n,) + a.shape[1:], BF)
    return pl.pallas_call(
        merge_kernel,
        in_specs=[VM] * 4,
        out_specs=[VM] * 4,
        out_shape=[shape(64), shape(64), shape(64), shape(32)],
        compiler_params=params(8),
        cost_estimate=cost(0, 1 << 20),
        name="merge",
    )(core, x, a, b)


def prep_kernel(stem_ref, bias_ref, mix_ref, ws_ref, bs_ref, wm_ref):
    for par in range(2):
        bs_ref[:, par * 128 : par * 128 + 128] = bias_ref[...] * SCALE
    zero8 = jnp.zeros((8, 128), F32)
    taps = [stem_ref[t].astype(F32) * SCALE for t in range(9)]
    for i in range(STEP):
        for par in range(2):
            rows = []
            for d in range(4):
                for row in range(8):
                    a, b = row - i, d - par
                    rows.append(taps[3 * a + b] if 0 <= a < 3 and 0 <= b < 3 else zero8)
            lane = (2 * i + par) * 128
            ws_ref[:, lane : lane + 128] = jnp.concatenate(rows, axis=0).astype(BF)
    zero = jnp.zeros((128, 128), BF)
    for b in range(3):
        w = [mix_ref[3 * a + b].astype(F32) for a in range(3)]
        mean = 0.5 * (w[0] + w[2])
        forms = [w[0], mean + 0.5 * w[1], mean - 0.5 * w[1], w[2]]
        for k in range(4):
            for par in range(2):
                d = b + par
                wm_ref[k, d * 128 : d * 128 + 128, par * 128 : par * 128 + 128] = forms[k].astype(BF)
    for k in range(4):
        wm_ref[k, 0:128, 128:256] = zero
        wm_ref[k, 384:512, 0:128] = zero


def prep(stem_weight, stem_bias, mix_weight):
    return pl.pallas_call(
        prep_kernel,
        in_specs=[VM] * 3,
        out_specs=[VM] * 3,
        out_shape=[
            jax.ShapeDtypeStruct((256, STEP * 256), BF),
            jax.ShapeDtypeStruct((1, 256), F32),
            jax.ShapeDtypeStruct((4, 512, 256), BF),
        ],
        compiler_params=params(12),
        cost_estimate=cost(0, 2 << 20),
        name="prep",
    )(*in_hbm(stem_weight, stem_bias[None], mix_weight))


def group_codes(last, codes_ref):
    band, lon = lax.axis_index("band"), lax.axis_index("lon")
    core_dl = jnp.where(lon % 2 == 0, 3, 1)
    x_dl = 4 - core_dl
    a_base = jnp.where(band % 2 == 0, 0, 8)
    b_base = 8 - a_base
    rim = (band == 0) | (band == last)
    codes = [4, 4 + core_dl, 4 + x_dl]
    codes += [a_base, a_base + core_dl]
    codes += [a_base + x_dl, jnp.where(band < (last + 1) // 2, 10, 2)]
    codes += [jnp.where(rim, 6, b_base), b_base + core_dl, b_base + x_dl]
    for g, code in enumerate(codes):
        codes_ref[g] = jnp.int32(code)


def add_groups(codes_ref, win_ref, w_ref, inc, acc, first, begin, count, ready=None):
    def group(i, carry):
        if ready is not None:
            ready(i)
        q = codes_ref[first + begin + i]
        for s in range(0, 32, 2):
            pair = jnp.dot(
                inc[begin + i, s : s + 2].reshape(16, 128),
                jnp.concatenate([w_ref[i, s], w_ref[i, s + 1]], axis=1),
                preferred_element_type=F32,
            )
            for k in range(2):
                part = pair[8 * k : 8 * k + 8, 128 * k : 128 * k + 128]
                w = win_ref[q, 0, s + k]
                place = (w % 4) * ROWS + w // 4
                acc[place] = acc[place] + part.astype(BF).astype(F32)
        return carry

    lax.fori_loop(0, count, group, 0)


def near_kernel(last, win_hbm, own_ref, core_ref, x_ref, w_hbm, acc, early_ref, w_ref, inc, codes_ref, win_ref, sem, early_sem, win_sem):
    group_codes(last, codes_ref)
    window = pltpu.make_async_copy(win_hbm, win_ref, win_sem)
    window.start()

    def copy(g):
        return pltpu.make_async_copy(w_hbm.at[0, codes_ref[g]], w_ref.at[g], sem.at[g])

    early = [
        pltpu.make_async_copy(w_hbm.at[0, codes_ref[NEAR + g]], early_ref.at[g], early_sem.at[g])
        for g in range(EARLY)
    ]
    for g in range(NEAR):
        copy(g).start()
    for transfer in early:
        transfer.start()
    acc[...] = jnp.zeros_like(acc)
    for g, array in enumerate((own_ref, core_ref, x_ref)):
        inc[g] = array[0:32]
    window.wait()
    add_groups(codes_ref, win_ref, w_ref, inc, acc, 0, 0, NEAR, lambda g: copy(g).wait())
    for transfer in early:
        transfer.wait()


def far_kernel(last, win_hbm, *refs):
    (x_in, a_in, ax_in, far_in, b_in, bx_in), refs = refs[:6], refs[6:]
    near_ref, early_ref, w_hbm, fld_ref, a_ref, b_ref = refs[:6]
    acc, w_ref, inc, codes_ref, win_ref, sem, win_sem = refs[6:]
    group_codes(last, codes_ref)
    window = pltpu.make_async_copy(win_hbm, win_ref, win_sem)
    window.start()

    def copy(g):
        return pltpu.make_async_copy(
            w_hbm.at[0, codes_ref[NEAR + EARLY + g]], w_ref.at[g], sem.at[g]
        )

    for g in range(FAR - EARLY):
        copy(g).start()
    acc[...] = near_ref[...]
    band = lax.axis_index("band")
    rim = (band == 0) | (band == last)
    blocks = [a_in[0:32], a_in[32:64], ax_in[...], far_in[...]]
    blocks += [jnp.where(rim, x_in[32:64], b_in[0:32]), b_in[32:64], bx_in[...]]
    for g, value in enumerate(blocks):
        inc[g] = value
    window.wait()
    add_groups(codes_ref, win_ref, early_ref, inc, acc, NEAR, 0, EARLY)
    add_groups(
        codes_ref, win_ref, w_ref, inc, acc, NEAR, EARLY, FAR - EARLY, lambda g: copy(g).wait()
    )
    for cb in range(4):
        rows = acc[cb * ROWS : (cb + 1) * ROWS].reshape(ROWS * 8, 128)
        fld_ref[:, cb * 128 : cb * 128 + 128] = rows.astype(BF)
    even = lax.axis_index("band") % 2 == 0
    top, bottom = fld_ref[0:16], fld_ref[ROWS * 8 - 16 : ROWS * 8]
    a_ref[...] = jnp.where(even, bottom, top)
    b_ref[...] = jnp.where(even, top, bottom)


def near_part(n_band, win, own, core, x, weights):
    group = weights.shape[2:]
    return pl.pallas_call(
        functools.partial(near_kernel, n_band - 1),
        in_specs=[HBM] + [VM] * 3 + [HBM],
        out_specs=[VM] * 2,
        out_shape=[
            jax.ShapeDtypeStruct((ROWS * 4, 8, 128), F32),
            jax.ShapeDtypeStruct((EARLY,) + group, BF),
        ],
        scratch_shapes=[
            pltpu.VMEM((NEAR,) + group, BF),
            pltpu.VMEM((NEAR, 32, 8, 128), BF),
            pltpu.SMEM((NEAR + FAR,), jnp.int32),
            pltpu.SMEM(win.shape, jnp.int32),
            pltpu.SemaphoreType.DMA((NEAR,)),
            pltpu.SemaphoreType.DMA((EARLY,)),
            pltpu.SemaphoreType.DMA,
        ],
        compiler_params=params(14),
        cost_estimate=cost(96 * 2 * 8 * 128 * 128, 12 << 20),
        name="near",
    )(*in_hbm(win), own, core, x, *in_hbm(weights))


def far_part(n_band, win, arrays, near, early, weights):
    group = weights.shape[2:]
    return pl.pallas_call(
        functools.partial(far_kernel, n_band - 1),
        in_specs=[HBM] + [VM] * 8 + [HBM],
        out_specs=[VM] * 3,
        out_shape=[
            jax.ShapeDtypeStruct((ROWS * 8, COLS), BF),
            jax.ShapeDtypeStruct((16, COLS), BF),
            jax.ShapeDtypeStruct((16, COLS), BF),
        ],
        scratch_shapes=[
            pltpu.VMEM((ROWS * 4, 8, 128), F32),
            pltpu.VMEM((FAR - EARLY,) + group, BF),
            pltpu.VMEM((FAR, 32, 8, 128), BF),
            pltpu.SMEM((NEAR + FAR,), jnp.int32),
            pltpu.SMEM(win.shape, jnp.int32),
            pltpu.SemaphoreType.DMA((FAR - EARLY,)),
            pltpu.SemaphoreType.DMA,
        ],
        compiler_params=params(14),
        cost_estimate=cost(224 * 2 * 8 * 128 * 128, 8 << 20),
        name="far",
    )(*in_hbm(win), *arrays, near, early, *in_hbm(weights))


def edge_kernel(last, fld_ref, a_ref, b_ref, edge_ref):
    band = lax.axis_index("band")
    a, b = a_ref[...], b_ref[...]
    b = jnp.where((band == 0) | (band == last), jnp.zeros_like(b), b)
    even = band % 2 == 0
    north, south = jnp.where(even, b, a), jnp.where(even, a, b)
    ends = []
    for lanes in (slice(0, 128), slice(COLS - 128, COLS)):
        ends.append(jnp.concatenate([north[:, lanes], fld_ref[:, lanes], south[:, lanes]], axis=0))
    rank = lax.broadcasted_iota(jnp.int32, (16, 256), 0)
    col = lax.broadcasted_iota(jnp.int32, (16, 256), 1)
    pick = ((rank < 2) & (col == rank)) | ((rank >= 2) & (rank < 4) & (col == 252 + rank))
    edge_ref[...] = lax.dot_general(
        jnp.where(pick, 1.0, 0.0).astype(BF),
        jnp.concatenate(ends, axis=1),
        (((1,), (1,)), ((), ())),
        preferred_element_type=F32,
    ).astype(BF)


def edges(n_band, fld, a, b):
    return pl.pallas_call(
        functools.partial(edge_kernel, n_band - 1),
        in_specs=[VM, VM, VM],
        out_specs=VM,
        out_shape=jax.ShapeDtypeStruct((16, (ROWS + 4) * 8), BF),
        compiler_params=params(8),
        cost_estimate=cost(0, 1 << 20),
        name="edges",
    )(fld, a, b)


def spread_kernel(fld_ref, g_ref, hot_ref):
    c = lax.broadcasted_iota(jnp.int32, (COLS, 256), 0)
    lane = lax.broadcasted_iota(jnp.int32, (COLS, 256), 1)
    for tile in range(3):
        n = lane % 128 + tile * 128
        j = jnp.where(n < PAIRS, SUB * (n % SUB) + n // SUB, SUB * (n - PAIRS + 1))
        gap = jnp.where(n < HROWS, c - 2 * j - lane // 128, -COLS)
        for pair in range(2):
            hot = jnp.where(gap == 2 * pair - 2, 1.0, 0.0)
            hot_ref[:, (2 * tile + pair) * 256 : (2 * tile + pair) * 256 + 256] = hot.astype(BF)
    zero = jnp.zeros((16, 256), BF)
    for pair in range(2):
        for tile in range(3):
            at = (2 * tile + pair) * 256
            value = jnp.dot(fld_ref[...], hot_ref[:, at : at + 256], preferred_element_type=F32)
            value = jnp.concatenate([zero, value.astype(BF), zero], axis=0)
            for half in range(2):
                d0 = (2 * pair + half) * 64
                for m in range(BLOCKS):
                    g_ref[m, d0 : d0 + 64, tile * 128 : tile * 128 + 128] = value[
                        48 * m : 48 * m + 64, half * 128 : half * 128 + 128
                    ]


def spread(fld):
    return pl.pallas_call(
        spread_kernel,
        in_specs=[VM],
        out_specs=[VM] * 2,
        out_shape=[
            jax.ShapeDtypeStruct((BLOCKS, 256, LANES), BF),
            jax.ShapeDtypeStruct((COLS, 6 * 256), BF),
        ],
        compiler_params=params(12),
        cost_estimate=cost(2 * 512 * 512 * 1536, 4 << 20),
        name="spread",
    )(fld)


def halos(last, a_ref, b_ref, core_ref, x_ref, hot_ref, rim, left_ref, right_ref):
    band = lax.axis_index("band")
    a, b = a_ref[...], b_ref[...]
    b = jnp.where((band == 0) | (band == last), jnp.zeros_like(b), b)
    even = band % 2 == 0
    rows = jnp.concatenate([jnp.where(even, b, a), jnp.where(even, a, b)], axis=0)
    rim[...] = jnp.zeros_like(rim)
    for pair in range(2):
        for tile in range(3):
            at = (2 * tile + pair) * 256
            value = jnp.dot(rows, hot_ref[:, at : at + 256], preferred_element_type=F32).astype(BF)
            for half in range(2):
                d0 = (2 * pair + half) * 64
                lanes = slice(tile * 128, tile * 128 + 128)
                part = value[:, half * 128 : half * 128 + 128]
                rim[0, d0 : d0 + 16, lanes] = part[0:16]
                rim[1, d0 + 48 : d0 + 64, lanes] = part[16:32]
    even = lax.axis_index("lon") % 2 == 0
    core, x = core_ref[...].astype(F32), x_ref[...].astype(F32)
    right, left = jnp.where(even, core, x), jnp.where(even, x, core)
    hr = lax.broadcasted_iota(jnp.int32, (16, 256), 0)
    hl = lax.broadcasted_iota(jnp.int32, (16, 256), 1)
    for side, base, at, out in ((left, 2, 0, left_ref), (right, 0, SUB - 1, right_ref)):
        hot = ((hl % 128) == at) & (hr == hl // 128 + base)
        value = lax.dot_general(
            side.astype(BF),
            jnp.where(hot, 1.0, 0.0).astype(BF),
            (((0,), (0,)), ((), ())),
            preferred_element_type=F32,
        ).astype(BF)
        for m in range(BLOCKS):
            for half in range(2):
                out[m, half * 64 : half * 64 + 64] = value[
                    48 * m : 48 * m + 64, half * 128 : half * 128 + 128
                ]


def conv_kernel(
    last,
    g_ref,
    a_ref,
    b_ref,
    core_ref,
    x_ref,
    ws_ref,
    bs_ref,
    wm_ref,
    bm_ref,
    hot_ref,
    out_ref,
    rim,
    left_ref,
    right_ref,
    hs,
    ys,
    yb,
    sem,
):
    band = lax.axis_index("band")

    def stem(block, which, low, high):
        block_in = jnp.minimum(block, BLOCKS - 1)
        edge = jnp.where(block_in == 0, 0, jnp.where(block_in == BLOCKS - 1, 1, 2))
        x = g_ref[block_in] + rim[edge]
        first = jnp.concatenate([x[:128, :128] + left_ref[block_in], x[128:, :128]], axis=0)
        final = jnp.concatenate([x[:128, 256:], x[128:, 256:] + right_ref[block_in]], axis=0)
        x = jnp.concatenate([first, x[:, 128:256], final], axis=1)[:, :HROWS]
        for i in which:
            t = lax.dot_general(
                x,
                ws_ref[:, i * 256 : i * 256 + 256],
                (((0,), (0,)), ((), ())),
                preferred_element_type=F32,
            )
            t = t + bs_ref[...]
            h = t + t * jnp.tanh(t)
            if i == 0 and low is not None:
                h = h * low
            if i == STEP - 1 and high is not None:
                h = h * high
            hs[block % 2, i] = h.astype(BF)

    halos(last, a_ref, b_ref, core_ref, x_ref, hot_ref, rim, left_ref, right_ref)
    stem(0, range(STEP), jnp.where(band == 0, 0.0, 1.0), None)

    def copy(at, slot):
        return pltpu.make_async_copy(
            yb.at[slot], out_ref.at[pl.ds(6 * at - 2, 6)], sem.at[slot]
        )

    first = pltpu.make_async_copy(yb.at[0, pl.ds(2, 4)], out_ref.at[pl.ds(0, 4)], sem.at[0])

    def step(s, carry):
        slot = s % 2

        @pl.when(s == 2)
        def _():
            first.wait()

        @pl.when(s > 2)
        def _():
            copy(s - 2, slot).wait()

        rows = [(1 - slot, 4), (1 - slot, 5)] + [(slot, i) for i in range(STEP)]
        keep_last = jnp.where((s == BLOCKS - 2) & (band == last), 0.0, 1.0)

        def mix(t):
            for c in range(PAIRS // CHUNK):
                row0 = c * CHUNK

                def both(r):
                    return jnp.concatenate(
                        [hs[rows[2 * t + r]][row0 + k * SUB : row0 + k * SUB + CHUNK] for k in range(2)],
                        axis=1,
                    )

                h = [both(r) for r in range(4)]
                v = [h[0] - h[2], h[1] + h[2], h[2] - h[1], h[1] - h[3]]
                m = [jnp.dot(v[k], wm_ref[k], preferred_element_type=F32) for k in range(4)]
                plus, minus = m[1] + m[2], m[1] - m[2]
                for q, y in enumerate([plus + m[0], minus - m[3]]):
                    row = 2 * t + q
                    for par in range(2):
                        part = y[:, par * 128 : par * 128 + 128] + bm_ref[...]
                        for k in range(CHUNK // SUB):
                            to = pl.ds(2 * (c * CHUNK // SUB + k) + par, SUB, stride=PITCH)
                            ys[row, to, :] = part[k * SUB : k * SUB + SUB]
            for q in range(2):
                for a in range(SUB):
                    yb[slot, 2 * t + q, 2 * SUB * a : 2 * SUB * a + 2 * SUB] = ys[
                        2 * t + q, PITCH * a : PITCH * a + 2 * SUB
                    ].astype(BF)

        for t in range(STEP // 2):
            mix(t)
        stem(s + 1, range(STEP), None, keep_last)

        @pl.when(s == 0)
        def _():
            first.start()

        @pl.when(s > 0)
        def _():
            copy(s, slot).start()
        return carry

    lax.fori_loop(0, BLOCKS, step, 0)
    copy(BLOCKS - 2, (BLOCKS - 2) % 2).wait()
    copy(BLOCKS - 1, (BLOCKS - 1) % 2).wait()


def conv(n_band, g, a, b, core, x, ws, bs, wm, bm, hot):
    channels = bm.shape[-1]
    return pl.pallas_call(
        functools.partial(conv_kernel, n_band - 1),
        in_specs=[VM] * 10,
        out_specs=ANY,
        out_shape=jax.ShapeDtypeStruct((ROWS, COLS, channels), BF),
        scratch_shapes=[
            pltpu.VMEM((3, 256, LANES), BF),
            pltpu.VMEM((BLOCKS, 128, 128), BF),
            pltpu.VMEM((BLOCKS, 128, 128), BF),
            pltpu.VMEM((2, STEP, HROWS, 256), BF),
            pltpu.VMEM((STEP, SUB * PITCH, channels), F32),
            pltpu.VMEM((2, STEP, COLS, channels), BF),
            pltpu.SemaphoreType.DMA((2,)),
        ],
        compiler_params=params(20),
        cost_estimate=cost(2 * ROWS * COLS * 9 * 128 * 128, 12 << 20),
        name="conv",
    )(g, a, b, core, x, ws, bs, wm, bm, hot)


def on_device(source, routes, slot_weights, window, stem_weight, stem_bias, mix_weight, mix_bias):
    n_band = lax.axis_size("band")
    n_lon = lax.axis_size("lon")
    axes = ("band", "lon")

    def move(value, way, turn):
        return lax.ppermute(value, axes, swap(n_band, n_lon, way, turn))

    own, to_core, to_x, to_a, to_ax, to_b, to_bx = pack(routes.T, source)
    win = window.transpose(1, 0, 2)
    core = move(to_core, "", "core")
    bx, ax = move(to_bx, "b", "x"), move(to_ax, "a", "x")
    x_both, a_both, b_both, far = merge(core, to_x, to_a, to_b)
    x, a, b = move(x_both, "", "x"), move(a_both, "a", "stay"), move(b_both, "b", "stay")
    arrays = [x, a, ax, move(far, "a", "x_rim"), b, bx]
    near, early = near_part(n_band, win, own, core, x, slot_weights)
    fld, a_row, b_row = far_part(n_band, win, arrays, near, early, slot_weights)
    a_halo = move(a_row, "a", "stay")
    b_halo = move(b_row, "b", "stay")
    g, hot = spread(fld)
    a_halo, b_halo, g, hot = lax.optimization_barrier((a_halo, b_halo, g, hot))
    edge = edges(n_band, fld, a_halo, b_halo)
    core_edge = move(edge, "", "core")
    x_edge = move(edge, "", "x")
    ws, bs, wm = prep(stem_weight, stem_bias, mix_weight)
    return conv(
        n_band, g, a_halo, b_halo, core_edge, x_edge, ws, bs, wm, mix_bias[None], hot
    )


def solution(mesh):
    both = ("band", "lon")
    in_specs = (
        P(both, None, None),
        P(both, None),
        P(both, None, None, None, None),
        P(both, None, None),
        P(),
        P(),
        P(),
        P(),
    )
    return jax.shard_map(
        on_device, mesh=mesh, in_specs=in_specs, out_specs=P("band", "lon", None), check_vma=False
    )
```

```python
import functools

import jax
import jax.numpy as jnp
from jax import lax
from jax.experimental import pallas as pl
from jax.experimental.pallas import tpu as pltpu
from jax.sharding import PartitionSpec as P

ROWS = 64
COLS = 512
PAIRS = COLS // 2
SUB = 16
HROWS = PAIRS + SUB
PITCH = 2 * SUB + 1
LANES = 384
CHUNK = 256
NEAR, FAR = 3, 7
EARLY = 2
STEP = 6
BLOCKS = (ROWS + 2) // STEP
SCALE = 1.0 / 2.0
BF = jnp.bfloat16
F32 = jnp.float32
VM = pl.BlockSpec(memory_space=pltpu.VMEM)
SM = pl.BlockSpec(memory_space=pltpu.SMEM)
ANY = pl.BlockSpec(memory_space=pl.ANY)
HBM = pl.BlockSpec(memory_space=pltpu.HBM)


def params(mib):
    return pltpu.CompilerParams(vmem_limit_bytes=mib << 20)


def cost(flops, size):
    return pl.CostEstimate(flops=flops, bytes_accessed=size, transcendentals=0)


def swap(n_band, n_lon, way, turn):
    pairs = []
    for b in range(n_band):
        if way == "a":
            partner = b ^ 1
        elif way == "b":
            partner = b + 1 if b % 2 else b - 1
        else:
            partner = b
        for l in range(n_lon):
            target = {"stay": l, "core": l ^ 1, "x": n_lon - 1 - l, "x_rim": n_lon - 1 - l}[turn]
            if not 0 <= partner < n_band or (turn == "x_rim" and 2 <= b < n_band - 2):
                pairs.append((b * n_lon + l, b * n_lon + (l ^ 1)))
            else:
                pairs.append((b * n_lon + l, partner * n_lon + target))
    return pairs


def in_hbm(*arrays):
    return [pltpu.with_memory_space_constraint(a, pltpu.HBM) for a in arrays]


PARTS = ((0, 1), (1, 5), (6, 1), (7, 1), (8, 1), (9, 1), (10, 1))


def pack_kernel(routes_hbm, src_hbm, *refs):
    outs, (routes_ref, src_ref, buf, place, sem) = refs[:7], refs[7:]
    copies = [
        pltpu.make_async_copy(routes_hbm, routes_ref, sem.at[0]),
        pltpu.make_async_copy(src_hbm, src_ref, sem.at[1]),
    ]
    for copy in copies:
        copy.start()
    band, lon = lax.axis_index("band"), lax.axis_index("lon")
    a_dir = 1 - 2 * (band % 2)
    core_dl = 1 + 2 * (lon % 2)
    for q in range(12):
        db, dl = q // 4 - 1, q % 4
        if dl == 2:
            group = 5 if db == 0 else 4
        elif db == 0:
            group = 0 if dl == 0 else jnp.where(core_dl == dl, 1, 6)
        elif dl == 0:
            group = jnp.where(a_dir == db, 7, 9)
        else:
            group = jnp.where(core_dl == dl, jnp.where(a_dir == db, 2, 3), jnp.where(a_dir == db, 8, 10))
        place[q] = group * 32
    buf[...] = jnp.zeros_like(buf)
    for copy in copies:
        copy.wait()

    def one(j, carry):
        block = src_ref[j]
        for t in range(2):
            q = routes_ref[t, j]
            at = place[q]
            place[q] = at + 1
            buf[at] = block
        return carry

    lax.fori_loop(0, src_ref.shape[0], one, 0, unroll=8)
    for out, (begin, groups) in zip(outs, PARTS):
        out[...] = buf[begin * 32 : (begin + groups) * 32]


def pack(routes, source):
    fields, cells = source.shape[1:]
    shape = lambda n: jax.ShapeDtypeStruct((n, fields, cells), BF)
    return pl.pallas_call(
        pack_kernel,
        in_specs=[HBM, HBM],
        out_specs=[VM] * 7,
        out_shape=[shape(32 * groups) for _, groups in PARTS],
        scratch_shapes=[
            pltpu.SMEM(routes.shape, jnp.int32),
            pltpu.VMEM(source.shape, BF),
            pltpu.VMEM((352, fields, cells), BF),
            pltpu.SMEM((12,), jnp.int32),
            pltpu.SemaphoreType.DMA((2,)),
        ],
        compiler_params=params(16),
        cost_estimate=cost(0, 1 << 20),
        name="pack",
    )(*in_hbm(routes, source))


def merge_kernel(core_ref, x_ref, a_ref, b_ref, x_out, a_out, b_out, far_out):
    for out, mine, group in ((x_out, x_ref, 4), (a_out, a_ref, 1), (b_out, b_ref, 2)):
        out[0:32] = mine[...]
        out[32:64] = core_ref[group * 32 : group * 32 + 32]
    far_out[...] = core_ref[96:128]


def merge(core, x, a, b):
    shape = lambda n: jax.ShapeDtypeStruct((n,) + a.shape[1:], BF)
    return pl.pallas_call(
        merge_kernel,
        in_specs=[VM] * 4,
        out_specs=[VM] * 4,
        out_shape=[shape(64), shape(64), shape(64), shape(32)],
        compiler_params=params(8),
        cost_estimate=cost(0, 1 << 20),
        name="merge",
    )(core, x, a, b)


def prep_kernel(last, stem_ref, bias_ref, mix_ref, a_ref, b_ref, hot_ref, ws_ref, bs_ref, wm_ref, rim):
    band = lax.axis_index("band")
    a, b = a_ref[...], b_ref[...]
    b = jnp.where((band == 0) | (band == last), jnp.zeros_like(b), b)
    even = band % 2 == 0
    rows = jnp.concatenate([jnp.where(even, b, a), jnp.where(even, a, b)], axis=0)
    rim[...] = jnp.zeros_like(rim)
    for pair in range(2):
        for tile in range(3):
            at = (2 * tile + pair) * 256
            value = jnp.dot(rows, hot_ref[:, at : at + 256], preferred_element_type=F32).astype(BF)
            for half in range(2):
                d0 = (2 * pair + half) * 64
                lanes = slice(tile * 128, tile * 128 + 128)
                part = value[:, half * 128 : half * 128 + 128]
                rim[0, d0 : d0 + 16, lanes] = part[0:16]
                rim[1, d0 + 48 : d0 + 64, lanes] = part[16:32]

    for par in range(2):
        bs_ref[:, par * 128 : par * 128 + 128] = bias_ref[...] * SCALE
    zero8 = jnp.zeros((8, 128), F32)
    taps = [stem_ref[t].astype(F32) * SCALE for t in range(9)]
    for i in range(STEP):
        for par in range(2):
            rows = []
            for d in range(4):
                for row in range(8):
                    a, b = row - i, d - par
                    rows.append(taps[3 * a + b] if 0 <= a < 3 and 0 <= b < 3 else zero8)
            lane = (2 * i + par) * 128
            ws_ref[:, lane : lane + 128] = jnp.concatenate(rows, axis=0).astype(BF)
    zero = jnp.zeros((128, 128), BF)
    for b in range(3):
        w = [mix_ref[3 * a + b].astype(F32) for a in range(3)]
        mean = 0.5 * (w[0] + w[2])
        forms = [w[0], mean + 0.5 * w[1], mean - 0.5 * w[1], w[2]]
        for k in range(4):
            for par in range(2):
                d = b + par
                wm_ref[k, d * 128 : d * 128 + 128, par * 128 : par * 128 + 128] = forms[k].astype(BF)
    for k in range(4):
        wm_ref[k, 0:128, 128:256] = zero
        wm_ref[k, 384:512, 0:128] = zero


def prep(n_band, stem_weight, stem_bias, mix_weight, a, b, hot):
    return pl.pallas_call(
        functools.partial(prep_kernel, n_band - 1),
        in_specs=[VM] * 6,
        out_specs=[VM] * 4,
        out_shape=[
            jax.ShapeDtypeStruct((256, STEP * 256), BF),
            jax.ShapeDtypeStruct((1, 256), F32),
            jax.ShapeDtypeStruct((4, 512, 256), BF),
            jax.ShapeDtypeStruct((3, 256, LANES), BF),
        ],
        compiler_params=params(12),
        cost_estimate=cost(0, 2 << 20),
        name="prep",
    )(*in_hbm(stem_weight, stem_bias[None], mix_weight), a, b, hot)


def group_codes(last, codes_ref):
    band, lon = lax.axis_index("band"), lax.axis_index("lon")
    core_dl = jnp.where(lon % 2 == 0, 3, 1)
    x_dl = 4 - core_dl
    a_base = jnp.where(band % 2 == 0, 0, 8)
    b_base = 8 - a_base
    rim = (band == 0) | (band == last)
    codes = [4, 4 + core_dl, 4 + x_dl]
    codes += [a_base, a_base + core_dl]
    codes += [a_base + x_dl, jnp.where(band < (last + 1) // 2, 10, 2)]
    codes += [jnp.where(rim, 6, b_base), b_base + core_dl, b_base + x_dl]
    for g, code in enumerate(codes):
        codes_ref[g] = jnp.int32(code)


def add_groups(codes_ref, win_ref, w_ref, inc, acc, first, begin, count, ready=None):
    def group(i, carry):
        if ready is not None:
            ready(i)
        q = codes_ref[first + begin + i]
        for s in range(0, 32, 2):
            pair = jnp.dot(
                inc[begin + i, s : s + 2].reshape(16, 128),
                jnp.concatenate([w_ref[i, s], w_ref[i, s + 1]], axis=1),
                preferred_element_type=F32,
            )
            for k in range(2):
                part = pair[8 * k : 8 * k + 8, 128 * k : 128 * k + 128]
                w = win_ref[q, 0, s + k]
                place = (w % 4) * ROWS + w // 4
                acc[place] = acc[place] + part.astype(BF).astype(F32)
        return carry

    lax.fori_loop(0, count, group, 0)


def near_kernel(last, win_hbm, own_ref, core_ref, x_ref, w_hbm, acc, early_ref, w_ref, inc, codes_ref, win_ref, sem, early_sem, win_sem):
    window = pltpu.make_async_copy(win_hbm, win_ref, win_sem)
    window.start()
    group_codes(last, codes_ref)

    def copy(g):
        return pltpu.make_async_copy(w_hbm.at[0, codes_ref[g]], w_ref.at[g], sem.at[g])

    early = [
        pltpu.make_async_copy(w_hbm.at[0, codes_ref[NEAR + g]], early_ref.at[g], early_sem.at[g])
        for g in range(EARLY)
    ]
    for g in range(NEAR):
        copy(g).start()
    for transfer in early:
        transfer.start()
    acc[...] = jnp.zeros_like(acc)
    for g, array in enumerate((own_ref, core_ref, x_ref)):
        inc[g] = array[0:32]
    window.wait()
    add_groups(codes_ref, win_ref, w_ref, inc, acc, 0, 0, NEAR, lambda g: copy(g).wait())
    for transfer in early:
        transfer.wait()


def far_kernel(last, win_hbm, *refs):
    (x_in, a_in, ax_in, far_in, b_in, bx_in), refs = refs[:6], refs[6:]
    near_ref, early_ref, w_hbm, fld_ref, a_ref, b_ref = refs[:6]
    acc, w_ref, inc, codes_ref, win_ref, sem, win_sem = refs[6:]
    window = pltpu.make_async_copy(win_hbm, win_ref, win_sem)
    window.start()
    group_codes(last, codes_ref)

    def copy(g):
        return pltpu.make_async_copy(
            w_hbm.at[0, codes_ref[NEAR + EARLY + g]], w_ref.at[g], sem.at[g]
        )

    for g in range(FAR - EARLY):
        copy(g).start()
    acc[...] = near_ref[...]
    band = lax.axis_index("band")
    rim = (band == 0) | (band == last)
    blocks = [a_in[0:32], a_in[32:64], ax_in[...], far_in[...]]
    blocks += [jnp.where(rim, x_in[32:64], b_in[0:32]), b_in[32:64], bx_in[...]]
    for g, value in enumerate(blocks):
        inc[g] = value
    window.wait()
    add_groups(codes_ref, win_ref, early_ref, inc, acc, NEAR, 0, EARLY)
    add_groups(
        codes_ref, win_ref, w_ref, inc, acc, NEAR, EARLY, FAR - EARLY, lambda g: copy(g).wait()
    )
    for cb in range(4):
        rows = acc[cb * ROWS : (cb + 1) * ROWS].reshape(ROWS * 8, 128)
        fld_ref[:, cb * 128 : cb * 128 + 128] = rows.astype(BF)
    even = lax.axis_index("band") % 2 == 0
    top, bottom = fld_ref[0:16], fld_ref[ROWS * 8 - 16 : ROWS * 8]
    a_ref[...] = jnp.where(even, bottom, top)
    b_ref[...] = jnp.where(even, top, bottom)


def near_part(n_band, win, own, core, x, weights):
    group = weights.shape[2:]
    return pl.pallas_call(
        functools.partial(near_kernel, n_band - 1),
        in_specs=[HBM] + [VM] * 3 + [HBM],
        out_specs=[VM] * 2,
        out_shape=[
            jax.ShapeDtypeStruct((ROWS * 4, 8, 128), F32),
            jax.ShapeDtypeStruct((EARLY,) + group, BF),
        ],
        scratch_shapes=[
            pltpu.VMEM((NEAR,) + group, BF),
            pltpu.VMEM((NEAR, 32, 8, 128), BF),
            pltpu.SMEM((NEAR + FAR,), jnp.int32),
            pltpu.SMEM(win.shape, jnp.int32),
            pltpu.SemaphoreType.DMA((NEAR,)),
            pltpu.SemaphoreType.DMA((EARLY,)),
            pltpu.SemaphoreType.DMA,
        ],
        compiler_params=params(14),
        cost_estimate=cost(96 * 2 * 8 * 128 * 128, 12 << 20),
        name="near",
    )(*in_hbm(win), own, core, x, *in_hbm(weights))


def far_part(n_band, win, arrays, near, early, weights):
    group = weights.shape[2:]
    return pl.pallas_call(
        functools.partial(far_kernel, n_band - 1),
        in_specs=[HBM] + [VM] * 8 + [HBM],
        out_specs=[VM] * 3,
        out_shape=[
            jax.ShapeDtypeStruct((ROWS * 8, COLS), BF),
            jax.ShapeDtypeStruct((16, COLS), BF),
            jax.ShapeDtypeStruct((16, COLS), BF),
        ],
        scratch_shapes=[
            pltpu.VMEM((ROWS * 4, 8, 128), F32),
            pltpu.VMEM((FAR - EARLY,) + group, BF),
            pltpu.VMEM((FAR, 32, 8, 128), BF),
            pltpu.SMEM((NEAR + FAR,), jnp.int32),
            pltpu.SMEM(win.shape, jnp.int32),
            pltpu.SemaphoreType.DMA((FAR - EARLY,)),
            pltpu.SemaphoreType.DMA,
        ],
        compiler_params=params(14),
        cost_estimate=cost(224 * 2 * 8 * 128 * 128, 8 << 20),
        name="far",
    )(*in_hbm(win), *arrays, near, early, *in_hbm(weights))


def edge_kernel(last, fld_ref, a_ref, b_ref, edge_ref):
    band = lax.axis_index("band")
    a, b = a_ref[...], b_ref[...]
    b = jnp.where((band == 0) | (band == last), jnp.zeros_like(b), b)
    even = band % 2 == 0
    north, south = jnp.where(even, b, a), jnp.where(even, a, b)
    ends = []
    for lanes in (slice(0, 128), slice(COLS - 128, COLS)):
        ends.append(jnp.concatenate([north[:, lanes], fld_ref[:, lanes], south[:, lanes]], axis=0))
    rank = lax.broadcasted_iota(jnp.int32, (16, 256), 0)
    col = lax.broadcasted_iota(jnp.int32, (16, 256), 1)
    pick = ((rank < 2) & (col == rank)) | ((rank >= 2) & (rank < 4) & (col == 252 + rank))
    edge_ref[...] = lax.dot_general(
        jnp.where(pick, 1.0, 0.0).astype(BF),
        jnp.concatenate(ends, axis=1),
        (((1,), (1,)), ((), ())),
        preferred_element_type=F32,
    ).astype(BF)


def edges(n_band, fld, a, b):
    return pl.pallas_call(
        functools.partial(edge_kernel, n_band - 1),
        in_specs=[VM, VM, VM],
        out_specs=VM,
        out_shape=jax.ShapeDtypeStruct((16, (ROWS + 4) * 8), BF),
        compiler_params=params(8),
        cost_estimate=cost(0, 1 << 20),
        name="edges",
    )(fld, a, b)


def spread_kernel(fld_ref, g_ref, hot_ref):
    c = lax.broadcasted_iota(jnp.int32, (COLS, 256), 0)
    lane = lax.broadcasted_iota(jnp.int32, (COLS, 256), 1)
    for tile in range(3):
        n = lane % 128 + tile * 128
        j = jnp.where(n < PAIRS, SUB * (n % SUB) + n // SUB, SUB * (n - PAIRS + 1))
        gap = jnp.where(n < HROWS, c - 2 * j - lane // 128, -COLS)
        for pair in range(2):
            hot = jnp.where(gap == 2 * pair - 2, 1.0, 0.0)
            hot_ref[:, (2 * tile + pair) * 256 : (2 * tile + pair) * 256 + 256] = hot.astype(BF)
    zero = jnp.zeros((16, 256), BF)
    for pair in range(2):
        for tile in range(3):
            at = (2 * tile + pair) * 256
            value = jnp.dot(fld_ref[...], hot_ref[:, at : at + 256], preferred_element_type=F32)
            value = jnp.concatenate([zero, value.astype(BF), zero], axis=0)
            for half in range(2):
                d0 = (2 * pair + half) * 64
                for m in range(BLOCKS):
                    g_ref[m, d0 : d0 + 64, tile * 128 : tile * 128 + 128] = value[
                        48 * m : 48 * m + 64, half * 128 : half * 128 + 128
                    ]


def spread(fld):
    return pl.pallas_call(
        spread_kernel,
        in_specs=[VM],
        out_specs=[VM] * 2,
        out_shape=[
            jax.ShapeDtypeStruct((BLOCKS, 256, LANES), BF),
            jax.ShapeDtypeStruct((COLS, 6 * 256), BF),
        ],
        compiler_params=params(12),
        cost_estimate=cost(2 * 512 * 512 * 1536, 4 << 20),
        name="spread",
    )(fld)


def halos(core_ref, x_ref, left_ref, right_ref):
    even = lax.axis_index("lon") % 2 == 0
    core, x = core_ref[...].astype(F32), x_ref[...].astype(F32)
    right, left = jnp.where(even, core, x), jnp.where(even, x, core)
    hr = lax.broadcasted_iota(jnp.int32, (16, 256), 0)
    hl = lax.broadcasted_iota(jnp.int32, (16, 256), 1)
    for side, base, at, out in ((left, 2, 0, left_ref), (right, 0, SUB - 1, right_ref)):
        hot = ((hl % 128) == at) & (hr == hl // 128 + base)
        value = lax.dot_general(
            side.astype(BF),
            jnp.where(hot, 1.0, 0.0).astype(BF),
            (((0,), (0,)), ((), ())),
            preferred_element_type=F32,
        ).astype(BF)
        for m in range(BLOCKS):
            for half in range(2):
                out[m, half * 64 : half * 64 + 64] = value[
                    48 * m : 48 * m + 64, half * 128 : half * 128 + 128
                ]


def conv_kernel(
    last,
    g_ref,
    core_ref,
    x_ref,
    ws_ref,
    bs_ref,
    wm_ref,
    bm_ref,
    rim,
    out_ref,
    left_ref,
    right_ref,
    hs,
    ys,
    yb,
    sem,
):
    band = lax.axis_index("band")

    def stem(block, which, low, high):
        block_in = jnp.minimum(block, BLOCKS - 1)
        edge = jnp.where(block_in == 0, 0, jnp.where(block_in == BLOCKS - 1, 1, 2))
        x = g_ref[block_in] + rim[edge]
        first = jnp.concatenate([x[:128, :128] + left_ref[block_in], x[128:, :128]], axis=0)
        final = jnp.concatenate([x[:128, 256:], x[128:, 256:] + right_ref[block_in]], axis=0)
        x = jnp.concatenate([first, x[:, 128:256], final], axis=1)[:, :HROWS]
        for i in which:
            t = lax.dot_general(
                x,
                ws_ref[:, i * 256 : i * 256 + 256],
                (((0,), (0,)), ((), ())),
                preferred_element_type=F32,
            )
            t = t + bs_ref[...]
            h = t + t * jnp.tanh(t)
            if i == 0 and low is not None:
                h = h * low
            if i == STEP - 1 and high is not None:
                h = h * high
            hs[block % 2, i] = h.astype(BF)

    halos(core_ref, x_ref, left_ref, right_ref)
    stem(0, range(STEP), jnp.where(band == 0, 0.0, 1.0), None)

    def copy(at, slot):
        return pltpu.make_async_copy(
            yb.at[slot], out_ref.at[pl.ds(6 * at - 2, 6)], sem.at[slot]
        )

    first = pltpu.make_async_copy(yb.at[0, pl.ds(2, 4)], out_ref.at[pl.ds(0, 4)], sem.at[0])

    def step(s, carry):
        slot = s % 2

        @pl.when(s == 2)
        def _():
            first.wait()

        @pl.when(s > 2)
        def _():
            copy(s - 2, slot).wait()

        rows = [(1 - slot, 4), (1 - slot, 5)] + [(slot, i) for i in range(STEP)]
        keep_last = jnp.where((s == BLOCKS - 2) & (band == last), 0.0, 1.0)

        def mix(t):
            for c in range(PAIRS // CHUNK):
                row0 = c * CHUNK

                def both(r):
                    return jnp.concatenate(
                        [hs[rows[2 * t + r]][row0 + k * SUB : row0 + k * SUB + CHUNK] for k in range(2)],
                        axis=1,
                    )

                h = [both(r) for r in range(4)]
                v = [h[0] - h[2], h[1] + h[2], h[2] - h[1], h[1] - h[3]]
                m = [jnp.dot(v[k], wm_ref[k], preferred_element_type=F32) for k in range(4)]
                m[1] = m[1] + jnp.concatenate([bm_ref[...], bm_ref[...]], axis=1)
                plus, minus = m[1] + m[2], m[1] - m[2]
                for q, y in enumerate([plus + m[0], minus - m[3]]):
                    row = 2 * t + q
                    for par in range(2):
                        part = y[:, par * 128 : par * 128 + 128]
                        for k in range(CHUNK // SUB):
                            to = pl.ds(2 * (c * CHUNK // SUB + k) + par, SUB, stride=PITCH)
                            ys[row, to, :] = part[k * SUB : k * SUB + SUB]
            for q in range(2):
                for a in range(SUB):
                    yb[slot, 2 * t + q, 2 * SUB * a : 2 * SUB * a + 2 * SUB] = ys[
                        2 * t + q, PITCH * a : PITCH * a + 2 * SUB
                    ].astype(BF)

        for t in range(STEP // 2):
            mix(t)
        stem(s + 1, range(STEP), None, keep_last)

        @pl.when(s == 0)
        def _():
            first.start()

        @pl.when(s > 0)
        def _():
            copy(s, slot).start()
        return carry

    lax.fori_loop(0, BLOCKS, step, 0)
    copy(BLOCKS - 2, (BLOCKS - 2) % 2).wait()
    copy(BLOCKS - 1, (BLOCKS - 1) % 2).wait()


def conv(n_band, g, core, x, ws, bs, wm, bm, rim):
    channels = bm.shape[-1]
    return pl.pallas_call(
        functools.partial(conv_kernel, n_band - 1),
        in_specs=[VM] * 8,
        out_specs=ANY,
        out_shape=jax.ShapeDtypeStruct((ROWS, COLS, channels), BF),
        scratch_shapes=[
            pltpu.VMEM((BLOCKS, 128, 128), BF),
            pltpu.VMEM((BLOCKS, 128, 128), BF),
            pltpu.VMEM((2, STEP, HROWS, 256), BF),
            pltpu.VMEM((STEP, SUB * PITCH, channels), F32),
            pltpu.VMEM((2, STEP, COLS, channels), BF),
            pltpu.SemaphoreType.DMA((2,)),
        ],
        compiler_params=params(20),
        cost_estimate=cost(2 * ROWS * COLS * 9 * 128 * 128, 12 << 20),
        name="conv",
    )(g, core, x, ws, bs, wm, bm, rim)


def on_device(source, routes, slot_weights, window, stem_weight, stem_bias, mix_weight, mix_bias):
    n_band = lax.axis_size("band")
    n_lon = lax.axis_size("lon")
    axes = ("band", "lon")

    def move(value, way, turn):
        return lax.ppermute(value, axes, swap(n_band, n_lon, way, turn))

    own, to_core, to_x, to_a, to_ax, to_b, to_bx = pack(routes.T, source)
    win = window.transpose(1, 0, 2)
    core = move(to_core, "", "core")
    bx, ax = move(to_bx, "b", "x"), move(to_ax, "a", "x")
    x_both, a_both, b_both, far = merge(core, to_x, to_a, to_b)
    x, a, b = move(x_both, "", "x"), move(a_both, "a", "stay"), move(b_both, "b", "stay")
    arrays = [x, a, ax, move(far, "a", "x_rim"), b, bx]
    near, early = near_part(n_band, win, own, core, x, slot_weights)
    fld, a_row, b_row = far_part(n_band, win, arrays, near, early, slot_weights)
    a_halo = move(a_row, "a", "stay")
    b_halo = move(b_row, "b", "stay")
    g, hot = spread(fld)
    a_halo, b_halo, g, hot = lax.optimization_barrier((a_halo, b_halo, g, hot))
    edge = edges(n_band, fld, a_halo, b_halo)
    core_edge = move(edge, "", "core")
    x_edge = move(edge, "", "x")
    ws, bs, wm, rim = prep(n_band, stem_weight, stem_bias, mix_weight, a_halo, b_halo, hot)
    return conv(n_band, g, core_edge, x_edge, ws, bs, wm, mix_bias[None], rim)


def solution(mesh):
    both = ("band", "lon")
    in_specs = (
        P(both, None, None),
        P(both, None),
        P(both, None, None, None, None),
        P(both, None, None),
        P(),
        P(),
        P(),
        P(),
    )
    return jax.shard_map(
        on_device, mesh=mesh, in_specs=in_specs, out_specs=P("band", "lon", None), check_vma=False
    )
```

```python
import functools

import jax
import jax.numpy as jnp
from jax import lax
from jax.experimental import pallas as pl
from jax.experimental.pallas import tpu as pltpu
from jax.sharding import PartitionSpec as P

ROWS = 64
COLS = 512
PAIRS = COLS // 2
SUB = 16
HROWS = PAIRS + SUB
PITCH = 2 * SUB + 1
LANES = 384
CHUNK = 256
NEAR, FAR = 3, 7
EARLY = 2
STEP = 6
BLOCKS = (ROWS + 2) // STEP
SCALE = 1.0 / 2.0
BF = jnp.bfloat16
F32 = jnp.float32
VM = pl.BlockSpec(memory_space=pltpu.VMEM)
SM = pl.BlockSpec(memory_space=pltpu.SMEM)
ANY = pl.BlockSpec(memory_space=pl.ANY)
HBM = pl.BlockSpec(memory_space=pltpu.HBM)


def params(mib):
    return pltpu.CompilerParams(vmem_limit_bytes=mib << 20)


def cost(flops, size):
    return pl.CostEstimate(flops=flops, bytes_accessed=size, transcendentals=0)


def swap(n_band, n_lon, way, turn):
    pairs = []
    for b in range(n_band):
        if way == "a":
            partner = b ^ 1
        elif way == "b":
            partner = b + 1 if b % 2 else b - 1
        else:
            partner = b
        for l in range(n_lon):
            target = {"stay": l, "core": l ^ 1, "x": n_lon - 1 - l, "x_rim": n_lon - 1 - l}[turn]
            if not 0 <= partner < n_band or (turn == "x_rim" and 2 <= b < n_band - 2):
                pairs.append((b * n_lon + l, b * n_lon + (l ^ 1)))
            else:
                pairs.append((b * n_lon + l, partner * n_lon + target))
    return pairs


def in_hbm(*arrays):
    return [pltpu.with_memory_space_constraint(a, pltpu.HBM) for a in arrays]


PARTS = ((0, 1), (1, 5), (6, 1), (7, 1), (8, 1), (9, 1), (10, 1))


def pack_kernel(routes_hbm, src_hbm, *refs):
    outs, (routes_ref, src_ref, buf, place, sem) = refs[:7], refs[7:]
    copies = [
        pltpu.make_async_copy(routes_hbm, routes_ref, sem.at[0]),
        pltpu.make_async_copy(src_hbm, src_ref, sem.at[1]),
    ]
    for copy in copies:
        copy.start()
    band, lon = lax.axis_index("band"), lax.axis_index("lon")
    a_dir = 1 - 2 * (band % 2)
    core_dl = 1 + 2 * (lon % 2)
    for q in range(12):
        db, dl = q // 4 - 1, q % 4
        if dl == 2:
            group = 5 if db == 0 else 4
        elif db == 0:
            group = 0 if dl == 0 else jnp.where(core_dl == dl, 1, 6)
        elif dl == 0:
            group = jnp.where(a_dir == db, 7, 9)
        else:
            group = jnp.where(core_dl == dl, jnp.where(a_dir == db, 2, 3), jnp.where(a_dir == db, 8, 10))
        place[q] = group * 32
    buf[...] = jnp.zeros_like(buf)
    for copy in copies:
        copy.wait()

    def one(j, carry):
        block = src_ref[j]
        for t in range(2):
            q = routes_ref[t, j]
            at = place[q]
            place[q] = at + 1
            buf[at] = block
        return carry

    lax.fori_loop(0, src_ref.shape[0], one, 0, unroll=8)
    for out, (begin, groups) in zip(outs, PARTS):
        out[...] = buf[begin * 32 : (begin + groups) * 32]


def pack(routes, source):
    fields, cells = source.shape[1:]
    shape = lambda n: jax.ShapeDtypeStruct((n, fields, cells), BF)
    return pl.pallas_call(
        pack_kernel,
        in_specs=[HBM, HBM],
        out_specs=[VM] * 7,
        out_shape=[shape(32 * groups) for _, groups in PARTS],
        scratch_shapes=[
            pltpu.SMEM(routes.shape, jnp.int32),
            pltpu.VMEM(source.shape, BF),
            pltpu.VMEM((352, fields, cells), BF),
            pltpu.SMEM((12,), jnp.int32),
            pltpu.SemaphoreType.DMA((2,)),
        ],
        compiler_params=params(16),
        cost_estimate=cost(0, 1 << 20),
        name="pack",
    )(*in_hbm(routes, source))


def merge_kernel(core_ref, x_ref, a_ref, b_ref, x_out, a_out, b_out, far_out):
    for out, mine, group in ((x_out, x_ref, 4), (a_out, a_ref, 1), (b_out, b_ref, 2)):
        out[0:32] = mine[...]
        out[32:64] = core_ref[group * 32 : group * 32 + 32]
    far_out[...] = core_ref[96:128]


def merge(core, x, a, b):
    shape = lambda n: jax.ShapeDtypeStruct((n,) + a.shape[1:], BF)
    return pl.pallas_call(
        merge_kernel,
        in_specs=[VM] * 4,
        out_specs=[VM] * 4,
        out_shape=[shape(64), shape(64), shape(64), shape(32)],
        compiler_params=params(8),
        cost_estimate=cost(0, 1 << 20),
        name="merge",
    )(core, x, a, b)


def prep_kernel(last, stem_ref, bias_ref, mix_ref, a_ref, b_ref, hot_ref, ws_ref, bs_ref, wm_ref, rim):
    band = lax.axis_index("band")
    a, b = a_ref[...], b_ref[...]
    b = jnp.where((band == 0) | (band == last), jnp.zeros_like(b), b)
    even = band % 2 == 0
    rows = jnp.concatenate([jnp.where(even, b, a), jnp.where(even, a, b)], axis=0)
    rim[...] = jnp.zeros_like(rim)
    for pair in range(2):
        for tile in range(3):
            at = (2 * tile + pair) * 256
            value = jnp.dot(rows, hot_ref[:, at : at + 256], preferred_element_type=F32).astype(BF)
            for half in range(2):
                d0 = (2 * pair + half) * 64
                lanes = slice(tile * 128, tile * 128 + 128)
                part = value[:, half * 128 : half * 128 + 128]
                rim[0, d0 : d0 + 16, lanes] = part[0:16]
                rim[1, d0 + 48 : d0 + 64, lanes] = part[16:32]

    for par in range(2):
        bs_ref[:, par * 128 : par * 128 + 128] = bias_ref[...] * SCALE
    zero8 = jnp.zeros((8, 128), F32)
    taps = [stem_ref[t].astype(F32) * SCALE for t in range(9)]
    for i in range(STEP):
        for par in range(2):
            rows = []
            for d in range(4):
                for row in range(8):
                    a, b = row - i, d - par
                    rows.append(taps[3 * a + b] if 0 <= a < 3 and 0 <= b < 3 else zero8)
            lane = (2 * i + par) * 128
            ws_ref[:, lane : lane + 128] = jnp.concatenate(rows, axis=0).astype(BF)
    zero = jnp.zeros((128, 128), BF)
    for b in range(3):
        w = [mix_ref[3 * a + b].astype(F32) for a in range(3)]
        mean = 0.5 * (w[0] + w[2])
        forms = [w[0], mean + 0.5 * w[1], mean - 0.5 * w[1], w[2]]
        for k in range(4):
            for par in range(2):
                d = b + par
                wm_ref[k, d * 128 : d * 128 + 128, par * 128 : par * 128 + 128] = forms[k].astype(BF)
    for k in range(4):
        wm_ref[k, 0:128, 128:256] = zero
        wm_ref[k, 384:512, 0:128] = zero


def prep(n_band, stem_weight, stem_bias, mix_weight, a, b, hot):
    return pl.pallas_call(
        functools.partial(prep_kernel, n_band - 1),
        in_specs=[VM] * 6,
        out_specs=[VM] * 4,
        out_shape=[
            jax.ShapeDtypeStruct((256, STEP * 256), BF),
            jax.ShapeDtypeStruct((1, 256), F32),
            jax.ShapeDtypeStruct((4, 512, 256), BF),
            jax.ShapeDtypeStruct((3, 256, LANES), BF),
        ],
        compiler_params=params(12),
        cost_estimate=cost(0, 2 << 20),
        name="prep",
    )(*in_hbm(stem_weight, stem_bias[None], mix_weight), a, b, hot)


def group_codes(last, codes_ref):
    band, lon = lax.axis_index("band"), lax.axis_index("lon")
    core_dl = jnp.where(lon % 2 == 0, 3, 1)
    x_dl = 4 - core_dl
    a_base = jnp.where(band % 2 == 0, 0, 8)
    b_base = 8 - a_base
    rim = (band == 0) | (band == last)
    codes = [4, 4 + core_dl, 4 + x_dl]
    codes += [a_base, a_base + core_dl]
    codes += [a_base + x_dl, jnp.where(band < (last + 1) // 2, 10, 2)]
    codes += [jnp.where(rim, 6, b_base), b_base + core_dl, b_base + x_dl]
    for g, code in enumerate(codes):
        codes_ref[g] = jnp.int32(code)


def add_groups(codes_ref, win_ref, w_ref, inc, acc, first, begin, count, ready=None):
    def group(i, carry):
        if ready is not None:
            ready(i)
        q = codes_ref[first + begin + i]
        for s in range(0, 32, 2):
            pair = jnp.dot(
                inc[begin + i, s : s + 2].reshape(16, 128),
                jnp.concatenate([w_ref[i, s], w_ref[i, s + 1]], axis=1),
                preferred_element_type=F32,
            )
            for k in range(2):
                part = pair[8 * k : 8 * k + 8, 128 * k : 128 * k + 128]
                w = win_ref[q, 0, s + k]
                place = (w % 4) * ROWS + w // 4
                acc[place] = acc[place] + part.astype(BF).astype(F32)
        return carry

    lax.fori_loop(0, count, group, 0)


def near_kernel(last, win_hbm, own_ref, core_ref, x_ref, w_hbm, acc, early_ref, w_ref, inc, codes_ref, win_ref, sem, early_sem, win_sem):
    window = pltpu.make_async_copy(win_hbm, win_ref, win_sem)
    window.start()
    group_codes(last, codes_ref)

    def copy(g):
        return pltpu.make_async_copy(w_hbm.at[0, codes_ref[g]], w_ref.at[g], sem.at[g])

    early = [
        pltpu.make_async_copy(w_hbm.at[0, codes_ref[NEAR + g]], early_ref.at[g], early_sem.at[g])
        for g in range(EARLY)
    ]
    for g in range(NEAR):
        copy(g).start()
    for transfer in early:
        transfer.start()
    acc[...] = jnp.zeros_like(acc)
    for g, array in enumerate((own_ref, core_ref, x_ref)):
        inc[g] = array[0:32]
    window.wait()
    add_groups(codes_ref, win_ref, w_ref, inc, acc, 0, 0, NEAR, lambda g: copy(g).wait())
    for transfer in early:
        transfer.wait()


def far_kernel(last, win_hbm, *refs):
    (x_in, a_in, ax_in, far_in, b_in, bx_in), refs = refs[:6], refs[6:]
    near_ref, early_ref, w_hbm, fld_ref, a_ref, b_ref = refs[:6]
    acc, w_ref, inc, codes_ref, win_ref, sem, win_sem = refs[6:]
    window = pltpu.make_async_copy(win_hbm, win_ref, win_sem)
    window.start()
    group_codes(last, codes_ref)

    def copy(g):
        return pltpu.make_async_copy(
            w_hbm.at[0, codes_ref[NEAR + EARLY + g]], w_ref.at[g], sem.at[g]
        )

    for g in range(FAR - EARLY):
        copy(g).start()
    acc[...] = near_ref[...]
    band = lax.axis_index("band")
    rim = (band == 0) | (band == last)
    blocks = [a_in[0:32], a_in[32:64], ax_in[...], far_in[...]]
    blocks += [jnp.where(rim, x_in[32:64], b_in[0:32]), b_in[32:64], bx_in[...]]
    for g, value in enumerate(blocks):
        inc[g] = value
    window.wait()
    add_groups(codes_ref, win_ref, early_ref, inc, acc, NEAR, 0, EARLY)
    add_groups(
        codes_ref, win_ref, w_ref, inc, acc, NEAR, EARLY, FAR - EARLY, lambda g: copy(g).wait()
    )
    for cb in range(4):
        rows = acc[cb * ROWS : (cb + 1) * ROWS].reshape(ROWS * 8, 128)
        fld_ref[:, cb * 128 : cb * 128 + 128] = rows.astype(BF)
    even = lax.axis_index("band") % 2 == 0
    top, bottom = fld_ref[0:16], fld_ref[ROWS * 8 - 16 : ROWS * 8]
    a_ref[...] = jnp.where(even, bottom, top)
    b_ref[...] = jnp.where(even, top, bottom)


def near_part(n_band, win, own, core, x, weights):
    group = weights.shape[2:]
    return pl.pallas_call(
        functools.partial(near_kernel, n_band - 1),
        in_specs=[HBM] + [VM] * 3 + [HBM],
        out_specs=[VM] * 2,
        out_shape=[
            jax.ShapeDtypeStruct((ROWS * 4, 8, 128), F32),
            jax.ShapeDtypeStruct((EARLY,) + group, BF),
        ],
        scratch_shapes=[
            pltpu.VMEM((NEAR,) + group, BF),
            pltpu.VMEM((NEAR, 32, 8, 128), BF),
            pltpu.SMEM((NEAR + FAR,), jnp.int32),
            pltpu.SMEM(win.shape, jnp.int32),
            pltpu.SemaphoreType.DMA((NEAR,)),
            pltpu.SemaphoreType.DMA((EARLY,)),
            pltpu.SemaphoreType.DMA,
        ],
        compiler_params=params(14),
        cost_estimate=cost(96 * 2 * 8 * 128 * 128, 12 << 20),
        name="near",
    )(*in_hbm(win), own, core, x, *in_hbm(weights))


def far_part(n_band, win, arrays, near, early, weights):
    group = weights.shape[2:]
    return pl.pallas_call(
        functools.partial(far_kernel, n_band - 1),
        in_specs=[HBM] + [VM] * 8 + [HBM],
        out_specs=[VM] * 3,
        out_shape=[
            jax.ShapeDtypeStruct((ROWS * 8, COLS), BF),
            jax.ShapeDtypeStruct((16, COLS), BF),
            jax.ShapeDtypeStruct((16, COLS), BF),
        ],
        scratch_shapes=[
            pltpu.VMEM((ROWS * 4, 8, 128), F32),
            pltpu.VMEM((FAR - EARLY,) + group, BF),
            pltpu.VMEM((FAR, 32, 8, 128), BF),
            pltpu.SMEM((NEAR + FAR,), jnp.int32),
            pltpu.SMEM(win.shape, jnp.int32),
            pltpu.SemaphoreType.DMA((FAR - EARLY,)),
            pltpu.SemaphoreType.DMA,
        ],
        compiler_params=params(14),
        cost_estimate=cost(224 * 2 * 8 * 128 * 128, 8 << 20),
        name="far",
    )(*in_hbm(win), *arrays, near, early, *in_hbm(weights))


def edge_kernel(last, fld_ref, a_ref, b_ref, edge_ref):
    band = lax.axis_index("band")
    a, b = a_ref[...], b_ref[...]
    b = jnp.where((band == 0) | (band == last), jnp.zeros_like(b), b)
    even = band % 2 == 0
    north, south = jnp.where(even, b, a), jnp.where(even, a, b)
    ends = []
    for lanes in (slice(0, 128), slice(COLS - 128, COLS)):
        ends.append(jnp.concatenate([north[:, lanes], fld_ref[:, lanes], south[:, lanes]], axis=0))
    rank = lax.broadcasted_iota(jnp.int32, (16, 256), 0)
    col = lax.broadcasted_iota(jnp.int32, (16, 256), 1)
    pick = ((rank < 2) & (col == rank)) | ((rank >= 2) & (rank < 4) & (col == 252 + rank))
    edge_ref[...] = lax.dot_general(
        jnp.where(pick, 1.0, 0.0).astype(BF),
        jnp.concatenate(ends, axis=1),
        (((1,), (1,)), ((), ())),
        preferred_element_type=F32,
    ).astype(BF)


def edges(n_band, fld, a, b):
    return pl.pallas_call(
        functools.partial(edge_kernel, n_band - 1),
        in_specs=[VM, VM, VM],
        out_specs=VM,
        out_shape=jax.ShapeDtypeStruct((16, (ROWS + 4) * 8), BF),
        compiler_params=params(8),
        cost_estimate=cost(0, 1 << 20),
        name="edges",
    )(fld, a, b)


def spread_kernel(fld_ref, g_ref, hot_ref):
    c = lax.broadcasted_iota(jnp.int32, (COLS, 256), 0)
    lane = lax.broadcasted_iota(jnp.int32, (COLS, 256), 1)
    for tile in range(3):
        n = lane % 128 + tile * 128
        j = jnp.where(n < PAIRS, SUB * (n % SUB) + n // SUB, SUB * (n - PAIRS + 1))
        gap = jnp.where(n < HROWS, c - 2 * j - lane // 128, -COLS)
        for pair in range(2):
            hot = jnp.where(gap == 2 * pair - 2, 1.0, 0.0)
            hot_ref[:, (2 * tile + pair) * 256 : (2 * tile + pair) * 256 + 256] = hot.astype(BF)
    zero = jnp.zeros((16, 256), BF)
    for pair in range(2):
        for tile in range(3):
            at = (2 * tile + pair) * 256
            value = jnp.dot(fld_ref[...], hot_ref[:, at : at + 256], preferred_element_type=F32)
            value = jnp.concatenate([zero, value.astype(BF), zero], axis=0)
            for half in range(2):
                d0 = (2 * pair + half) * 64
                for m in range(BLOCKS):
                    g_ref[m, d0 : d0 + 64, tile * 128 : tile * 128 + 128] = value[
                        48 * m : 48 * m + 64, half * 128 : half * 128 + 128
                    ]


def spread(fld):
    return pl.pallas_call(
        spread_kernel,
        in_specs=[VM],
        out_specs=[VM] * 2,
        out_shape=[
            jax.ShapeDtypeStruct((BLOCKS, 256, LANES), BF),
            jax.ShapeDtypeStruct((COLS, 6 * 256), BF),
        ],
        compiler_params=params(12),
        cost_estimate=cost(2 * 512 * 512 * 1536, 4 << 20),
        name="spread",
    )(fld)


def halos(core_ref, x_ref, left_ref, right_ref):
    even = lax.axis_index("lon") % 2 == 0
    core, x = core_ref[...].astype(F32), x_ref[...].astype(F32)
    right, left = jnp.where(even, core, x), jnp.where(even, x, core)
    hr = lax.broadcasted_iota(jnp.int32, (16, 256), 0)
    hl = lax.broadcasted_iota(jnp.int32, (16, 256), 1)
    for side, base, at, out in ((left, 2, 0, left_ref), (right, 0, SUB - 1, right_ref)):
        hot = ((hl % 128) == at) & (hr == hl // 128 + base)
        value = lax.dot_general(
            side.astype(BF),
            jnp.where(hot, 1.0, 0.0).astype(BF),
            (((0,), (0,)), ((), ())),
            preferred_element_type=F32,
        ).astype(BF)
        for m in range(BLOCKS):
            for half in range(2):
                out[m, half * 64 : half * 64 + 64] = value[
                    48 * m : 48 * m + 64, half * 128 : half * 128 + 128
                ]


def conv_kernel(
    last,
    g_ref,
    core_ref,
    x_ref,
    ws_ref,
    bs_ref,
    wm_ref,
    bm_ref,
    rim,
    out_ref,
    left_ref,
    right_ref,
    hs,
    ys,
    yb,
    sem,
):
    band = lax.axis_index("band")

    def stem(block, which, low, high):
        block_in = jnp.minimum(block, BLOCKS - 1)
        edge = jnp.where(block_in == 0, 0, jnp.where(block_in == BLOCKS - 1, 1, 2))
        x = g_ref[block_in] + rim[edge]
        first = jnp.concatenate([x[:128, :128] + left_ref[block_in], x[128:, :128]], axis=0)
        final = jnp.concatenate([x[:128, 256:], x[128:, 256:] + right_ref[block_in]], axis=0)
        x = jnp.concatenate([first, x[:, 128:256], final], axis=1)[:, :HROWS]
        for i in which:
            t = lax.dot_general(
                x,
                ws_ref[:, i * 256 : i * 256 + 256],
                (((0,), (0,)), ((), ())),
                preferred_element_type=F32,
            )
            t = t + bs_ref[...]
            h = t + t * jnp.tanh(t)
            if i == 0 and low is not None:
                h = h * low
            if i == STEP - 1 and high is not None:
                h = h * high
            hs[block % 2, i] = h.astype(BF)

    halos(core_ref, x_ref, left_ref, right_ref)
    stem(0, range(STEP), jnp.where(band == 0, 0.0, 1.0), None)

    def copy(at, slot):
        return pltpu.make_async_copy(
            yb.at[slot], out_ref.at[pl.ds(6 * at - 2, 6)], sem.at[slot]
        )

    first = pltpu.make_async_copy(yb.at[0, pl.ds(2, 4)], out_ref.at[pl.ds(0, 4)], sem.at[0])

    def step(s, carry):
        slot = s % 2

        @pl.when(s == 2)
        def _():
            first.wait()

        @pl.when(s > 2)
        def _():
            copy(s - 2, slot).wait()

        rows = [(1 - slot, 4), (1 - slot, 5)] + [(slot, i) for i in range(STEP)]
        keep_last = jnp.where((s == BLOCKS - 2) & (band == last), 0.0, 1.0)

        def mix(t):
            for c in range(PAIRS // CHUNK):
                row0 = c * CHUNK

                def both(r):
                    return jnp.concatenate(
                        [hs[rows[2 * t + r]][row0 + k * SUB : row0 + k * SUB + CHUNK] for k in range(2)],
                        axis=1,
                    )

                h = [both(r) for r in range(4)]
                v = [h[0] - h[2], h[1] + h[2], h[2] - h[1], h[1] - h[3]]
                m = [jnp.dot(v[k], wm_ref[k], preferred_element_type=F32) for k in range(4)]
                m[1] = m[1] + jnp.concatenate([bm_ref[...], bm_ref[...]], axis=1)
                plus, minus = m[1] + m[2], m[1] - m[2]
                for q, y in enumerate([plus + m[0], minus - m[3]]):
                    row = 2 * t + q
                    for par in range(2):
                        part = y[:, par * 128 : par * 128 + 128]
                        for k in range(CHUNK // SUB):
                            to = pl.ds(2 * (c * CHUNK // SUB + k) + par, SUB, stride=PITCH)
                            ys[row, to, :] = part[k * SUB : k * SUB + SUB]
            for q in range(2):
                for a in range(SUB):
                    yb[slot, 2 * t + q, 2 * SUB * a : 2 * SUB * a + 2 * SUB] = ys[
                        2 * t + q, PITCH * a : PITCH * a + 2 * SUB
                    ].astype(BF)

        for t in range(STEP // 2):
            mix(t)
        stem(s + 1, range(STEP), None, keep_last)

        @pl.when(s == 0)
        def _():
            first.start()

        @pl.when(s > 0)
        def _():
            copy(s, slot).start()
        return carry

    lax.fori_loop(0, BLOCKS, step, 0)
    copy(BLOCKS - 2, (BLOCKS - 2) % 2).wait()
    copy(BLOCKS - 1, (BLOCKS - 1) % 2).wait()


def conv(n_band, g, core, x, ws, bs, wm, bm, rim):
    channels = bm.shape[-1]
    return pl.pallas_call(
        functools.partial(conv_kernel, n_band - 1),
        in_specs=[VM] * 8,
        out_specs=ANY,
        out_shape=jax.ShapeDtypeStruct((ROWS, COLS, channels), BF),
        scratch_shapes=[
            pltpu.VMEM((BLOCKS, 128, 128), BF),
            pltpu.VMEM((BLOCKS, 128, 128), BF),
            pltpu.VMEM((2, STEP, HROWS, 256), BF),
            pltpu.VMEM((STEP, (SUB + 1) * PITCH + 7, channels), F32),
            pltpu.VMEM((2, STEP, COLS, channels), BF),
            pltpu.SemaphoreType.DMA((2,)),
        ],
        compiler_params=params(20),
        cost_estimate=cost(2 * ROWS * COLS * 9 * 128 * 128, 12 << 20),
        name="conv",
    )(g, core, x, ws, bs, wm, bm, rim)


def on_device(source, routes, slot_weights, window, stem_weight, stem_bias, mix_weight, mix_bias):
    n_band = lax.axis_size("band")
    n_lon = lax.axis_size("lon")
    axes = ("band", "lon")

    def move(value, way, turn):
        return lax.ppermute(value, axes, swap(n_band, n_lon, way, turn))

    own, to_core, to_x, to_a, to_ax, to_b, to_bx = pack(routes.T, source)
    win = window.transpose(1, 0, 2)
    core = move(to_core, "", "core")
    bx, ax = move(to_bx, "b", "x"), move(to_ax, "a", "x")
    x_both, a_both, b_both, far = merge(core, to_x, to_a, to_b)
    x, a, b = move(x_both, "", "x"), move(a_both, "a", "stay"), move(b_both, "b", "stay")
    arrays = [x, a, ax, move(far, "a", "x_rim"), b, bx]
    near, early = near_part(n_band, win, own, core, x, slot_weights)
    fld, a_row, b_row = far_part(n_band, win, arrays, near, early, slot_weights)
    a_halo = move(a_row, "a", "stay")
    b_halo = move(b_row, "b", "stay")
    g, hot = spread(fld)
    a_halo, b_halo, g, hot = lax.optimization_barrier((a_halo, b_halo, g, hot))
    edge = edges(n_band, fld, a_halo, b_halo)
    core_edge = move(edge, "", "core")
    x_edge = move(edge, "", "x")
    ws, bs, wm, rim = prep(n_band, stem_weight, stem_bias, mix_weight, a_halo, b_halo, hot)
    return conv(n_band, g, core_edge, x_edge, ws, bs, wm, mix_bias[None], rim)


def solution(mesh):
    both = ("band", "lon")
    in_specs = (
        P(both, None, None),
        P(both, None),
        P(both, None, None, None, None),
        P(both, None, None),
        P(),
        P(),
        P(),
        P(),
    )
    return jax.shard_map(
        on_device, mesh=mesh, in_specs=in_specs, out_specs=P("band", "lon", None), check_vma=False
    )
```

```python
import functools

import jax
import jax.numpy as jnp
from jax import lax
from jax.experimental import pallas as pl
from jax.experimental.pallas import tpu as pltpu
from jax.sharding import PartitionSpec as P

ROWS = 64
COLS = 512
PAIRS = COLS // 2
SUB = 16
HROWS = PAIRS + SUB
PITCH = 2 * SUB + 1
LANES = 384
CHUNK = 256
NEAR, FAR = 3, 7
EARLY = 2
STEP = 6
BLOCKS = (ROWS + 2) // STEP
SCALE = 1.0 / 2.0
BF = jnp.bfloat16
F32 = jnp.float32
VM = pl.BlockSpec(memory_space=pltpu.VMEM)
SM = pl.BlockSpec(memory_space=pltpu.SMEM)
ANY = pl.BlockSpec(memory_space=pl.ANY)
HBM = pl.BlockSpec(memory_space=pltpu.HBM)


def params(mib):
    return pltpu.CompilerParams(vmem_limit_bytes=mib << 20)


def cost(flops, size):
    return pl.CostEstimate(flops=flops, bytes_accessed=size, transcendentals=0)


def swap(n_band, n_lon, way, turn):
    pairs = []
    for b in range(n_band):
        if way == "a":
            partner = b ^ 1
        elif way == "b":
            partner = b + 1 if b % 2 else b - 1
        else:
            partner = b
        for l in range(n_lon):
            target = {"stay": l, "core": l ^ 1, "x": n_lon - 1 - l, "x_rim": n_lon - 1 - l}[turn]
            if not 0 <= partner < n_band or (turn == "x_rim" and 2 <= b < n_band - 2):
                pairs.append((b * n_lon + l, b * n_lon + (l ^ 1)))
            else:
                pairs.append((b * n_lon + l, partner * n_lon + target))
    return pairs


def in_hbm(*arrays):
    return [pltpu.with_memory_space_constraint(a, pltpu.HBM) for a in arrays]


PARTS = ((0, 1), (1, 5), (6, 1), (7, 1), (8, 1), (9, 1), (10, 1))


def pack_kernel(routes_hbm, src_hbm, *refs):
    outs, (routes_ref, src_ref, buf, place, sem) = refs[:7], refs[7:]
    copies = [
        pltpu.make_async_copy(routes_hbm, routes_ref, sem.at[0]),
        pltpu.make_async_copy(src_hbm, src_ref, sem.at[1]),
    ]
    for copy in copies:
        copy.start()
    band, lon = lax.axis_index("band"), lax.axis_index("lon")
    a_dir = 1 - 2 * (band % 2)
    core_dl = 1 + 2 * (lon % 2)
    for q in range(12):
        db, dl = q // 4 - 1, q % 4
        if dl == 2:
            group = 5 if db == 0 else 4
        elif db == 0:
            group = 0 if dl == 0 else jnp.where(core_dl == dl, 1, 6)
        elif dl == 0:
            group = jnp.where(a_dir == db, 7, 9)
        else:
            group = jnp.where(core_dl == dl, jnp.where(a_dir == db, 2, 3), jnp.where(a_dir == db, 8, 10))
        place[q] = group * 32
    buf[...] = jnp.zeros_like(buf)
    for copy in copies:
        copy.wait()

    def one(j, carry):
        block = src_ref[j]
        for t in range(2):
            q = routes_ref[t, j]
            at = place[q]
            place[q] = at + 1
            buf[at] = block
        return carry

    lax.fori_loop(0, src_ref.shape[0], one, 0, unroll=32)
    for out, (begin, groups) in zip(outs, PARTS):
        out[...] = buf[begin * 32 : (begin + groups) * 32]


def pack(routes, source):
    fields, cells = source.shape[1:]
    shape = lambda n: jax.ShapeDtypeStruct((n, fields, cells), BF)
    return pl.pallas_call(
        pack_kernel,
        in_specs=[HBM, HBM],
        out_specs=[VM] * 7,
        out_shape=[shape(32 * groups) for _, groups in PARTS],
        scratch_shapes=[
            pltpu.SMEM(routes.shape, jnp.int32),
            pltpu.VMEM(source.shape, BF),
            pltpu.VMEM((352, fields, cells), BF),
            pltpu.SMEM((12,), jnp.int32),
            pltpu.SemaphoreType.DMA((2,)),
        ],
        compiler_params=params(16),
        cost_estimate=cost(0, 1 << 20),
        name="pack",
    )(*in_hbm(routes, source))


def merge_kernel(core_ref, x_ref, a_ref, b_ref, x_out, a_out, b_out, far_out):
    for out, mine, group in ((x_out, x_ref, 4), (a_out, a_ref, 1), (b_out, b_ref, 2)):
        out[0:32] = mine[...]
        out[32:64] = core_ref[group * 32 : group * 32 + 32]
    far_out[...] = core_ref[96:128]


def merge(core, x, a, b):
    shape = lambda n: jax.ShapeDtypeStruct((n,) + a.shape[1:], BF)
    return pl.pallas_call(
        merge_kernel,
        in_specs=[VM] * 4,
        out_specs=[VM] * 4,
        out_shape=[shape(64), shape(64), shape(64), shape(32)],
        compiler_params=params(8),
        cost_estimate=cost(0, 1 << 20),
        name="merge",
    )(core, x, a, b)


def prep_kernel(last, stem_ref, bias_ref, mix_ref, a_ref, b_ref, hot_ref, ws_ref, bs_ref, wm_ref, rim):
    band = lax.axis_index("band")
    a, b = a_ref[...], b_ref[...]
    b = jnp.where((band == 0) | (band == last), jnp.zeros_like(b), b)
    even = band % 2 == 0
    rows = jnp.concatenate([jnp.where(even, b, a), jnp.where(even, a, b)], axis=0)
    rim[...] = jnp.zeros_like(rim)
    for pair in range(2):
        for tile in range(3):
            at = (2 * tile + pair) * 256
            value = jnp.dot(rows, hot_ref[:, at : at + 256], preferred_element_type=F32).astype(BF)
            for half in range(2):
                d0 = (2 * pair + half) * 64
                lanes = slice(tile * 128, tile * 128 + 128)
                part = value[:, half * 128 : half * 128 + 128]
                rim[0, d0 : d0 + 16, lanes] = part[0:16]
                rim[1, d0 + 48 : d0 + 64, lanes] = part[16:32]

    for par in range(2):
        bs_ref[:, par * 128 : par * 128 + 128] = bias_ref[...] * SCALE
    zero8 = jnp.zeros((8, 128), F32)
    taps = [stem_ref[t].astype(F32) * SCALE for t in range(9)]
    for i in range(STEP):
        for par in range(2):
            rows = []
            for d in range(4):
                for row in range(8):
                    a, b = row - i, d - par
                    rows.append(taps[3 * a + b] if 0 <= a < 3 and 0 <= b < 3 else zero8)
            lane = (2 * i + par) * 128
            ws_ref[:, lane : lane + 128] = jnp.concatenate(rows, axis=0).astype(BF)
    zero = jnp.zeros((128, 128), BF)
    for b in range(3):
        w = [mix_ref[3 * a + b].astype(F32) for a in range(3)]
        mean = 0.5 * (w[0] + w[2])
        forms = [w[0], mean + 0.5 * w[1], mean - 0.5 * w[1], w[2]]
        for k in range(4):
            for par in range(2):
                d = b + par
                wm_ref[k, d * 128 : d * 128 + 128, par * 128 : par * 128 + 128] = forms[k].astype(BF)
    for k in range(4):
        wm_ref[k, 0:128, 128:256] = zero
        wm_ref[k, 384:512, 0:128] = zero


def prep(n_band, stem_weight, stem_bias, mix_weight, a, b, hot):
    return pl.pallas_call(
        functools.partial(prep_kernel, n_band - 1),
        in_specs=[VM] * 6,
        out_specs=[VM] * 4,
        out_shape=[
            jax.ShapeDtypeStruct((256, STEP * 256), BF),
            jax.ShapeDtypeStruct((1, 256), F32),
            jax.ShapeDtypeStruct((4, 512, 256), BF),
            jax.ShapeDtypeStruct((3, 256, LANES), BF),
        ],
        compiler_params=params(12),
        cost_estimate=cost(0, 2 << 20),
        name="prep",
    )(*in_hbm(stem_weight, stem_bias[None], mix_weight), a, b, hot)


def group_codes(last, codes_ref):
    band, lon = lax.axis_index("band"), lax.axis_index("lon")
    core_dl = jnp.where(lon % 2 == 0, 3, 1)
    x_dl = 4 - core_dl
    a_base = jnp.where(band % 2 == 0, 0, 8)
    b_base = 8 - a_base
    rim = (band == 0) | (band == last)
    codes = [4, 4 + core_dl, 4 + x_dl]
    codes += [a_base, a_base + core_dl]
    codes += [a_base + x_dl, jnp.where(band < (last + 1) // 2, 10, 2)]
    codes += [jnp.where(rim, 6, b_base), b_base + core_dl, b_base + x_dl]
    for g, code in enumerate(codes):
        codes_ref[g] = jnp.int32(code)


def add_groups(codes_ref, win_ref, w_ref, inc, acc, first, begin, count, ready=None):
    def group(i, carry):
        if ready is not None:
            ready(i)
        q = codes_ref[first + begin + i]
        for s in range(0, 32, 2):
            pair = jnp.dot(
                inc[begin + i, s : s + 2].reshape(16, 128),
                jnp.concatenate([w_ref[i, s], w_ref[i, s + 1]], axis=1),
                preferred_element_type=F32,
            )
            for k in range(2):
                part = pair[8 * k : 8 * k + 8, 128 * k : 128 * k + 128]
                w = win_ref[q, 0, s + k]
                place = (w % 4) * ROWS + w // 4
                acc[place] = acc[place] + part.astype(BF).astype(F32)
        return carry

    lax.fori_loop(0, count, group, 0)


def near_kernel(last, win_hbm, own_ref, core_ref, x_ref, w_hbm, acc, early_ref, w_ref, inc, codes_ref, win_ref, sem, early_sem, win_sem):
    window = pltpu.make_async_copy(win_hbm, win_ref, win_sem)
    window.start()
    group_codes(last, codes_ref)

    def copy(g):
        return pltpu.make_async_copy(w_hbm.at[0, codes_ref[g]], w_ref.at[g], sem.at[g])

    early = [
        pltpu.make_async_copy(w_hbm.at[0, codes_ref[NEAR + g]], early_ref.at[g], early_sem.at[g])
        for g in range(EARLY)
    ]
    for g in range(NEAR):
        copy(g).start()
    for transfer in early:
        transfer.start()
    acc[...] = jnp.zeros_like(acc)
    for g, array in enumerate((own_ref, core_ref, x_ref)):
        inc[g] = array[0:32]
    window.wait()
    add_groups(codes_ref, win_ref, w_ref, inc, acc, 0, 0, NEAR, lambda g: copy(g).wait())
    for transfer in early:
        transfer.wait()


def far_kernel(last, win_hbm, *refs):
    (x_in, a_in, ax_in, far_in, b_in, bx_in), refs = refs[:6], refs[6:]
    near_ref, early_ref, w_hbm, fld_ref, a_ref, b_ref = refs[:6]
    acc, w_ref, inc, codes_ref, win_ref, sem, win_sem = refs[6:]
    window = pltpu.make_async_copy(win_hbm, win_ref, win_sem)
    window.start()
    group_codes(last, codes_ref)

    def copy(g):
        return pltpu.make_async_copy(
            w_hbm.at[0, codes_ref[NEAR + EARLY + g]], w_ref.at[g], sem.at[g]
        )

    for g in range(FAR - EARLY):
        copy(g).start()
    acc[...] = near_ref[...]
    band = lax.axis_index("band")
    rim = (band == 0) | (band == last)
    blocks = [a_in[0:32], a_in[32:64], ax_in[...], far_in[...]]
    blocks += [jnp.where(rim, x_in[32:64], b_in[0:32]), b_in[32:64], bx_in[...]]
    for g, value in enumerate(blocks):
        inc[g] = value
    window.wait()
    add_groups(codes_ref, win_ref, early_ref, inc, acc, NEAR, 0, EARLY)
    add_groups(
        codes_ref, win_ref, w_ref, inc, acc, NEAR, EARLY, FAR - EARLY, lambda g: copy(g).wait()
    )
    for cb in range(4):
        rows = acc[cb * ROWS : (cb + 1) * ROWS].reshape(ROWS * 8, 128)
        fld_ref[:, cb * 128 : cb * 128 + 128] = rows.astype(BF)
    even = lax.axis_index("band") % 2 == 0
    top, bottom = fld_ref[0:16], fld_ref[ROWS * 8 - 16 : ROWS * 8]
    a_ref[...] = jnp.where(even, bottom, top)
    b_ref[...] = jnp.where(even, top, bottom)


def near_part(n_band, win, own, core, x, weights):
    group = weights.shape[2:]
    return pl.pallas_call(
        functools.partial(near_kernel, n_band - 1),
        in_specs=[HBM] + [VM] * 3 + [HBM],
        out_specs=[VM] * 2,
        out_shape=[
            jax.ShapeDtypeStruct((ROWS * 4, 8, 128), F32),
            jax.ShapeDtypeStruct((EARLY,) + group, BF),
        ],
        scratch_shapes=[
            pltpu.VMEM((NEAR,) + group, BF),
            pltpu.VMEM((NEAR, 32, 8, 128), BF),
            pltpu.SMEM((NEAR + FAR,), jnp.int32),
            pltpu.SMEM(win.shape, jnp.int32),
            pltpu.SemaphoreType.DMA((NEAR,)),
            pltpu.SemaphoreType.DMA((EARLY,)),
            pltpu.SemaphoreType.DMA,
        ],
        compiler_params=params(14),
        cost_estimate=cost(96 * 2 * 8 * 128 * 128, 12 << 20),
        name="near",
    )(*in_hbm(win), own, core, x, *in_hbm(weights))


def far_part(n_band, win, arrays, near, early, weights):
    group = weights.shape[2:]
    return pl.pallas_call(
        functools.partial(far_kernel, n_band - 1),
        in_specs=[HBM] + [VM] * 8 + [HBM],
        out_specs=[VM] * 3,
        out_shape=[
            jax.ShapeDtypeStruct((ROWS * 8, COLS), BF),
            jax.ShapeDtypeStruct((16, COLS), BF),
            jax.ShapeDtypeStruct((16, COLS), BF),
        ],
        scratch_shapes=[
            pltpu.VMEM((ROWS * 4, 8, 128), F32),
            pltpu.VMEM((FAR - EARLY,) + group, BF),
            pltpu.VMEM((FAR, 32, 8, 128), BF),
            pltpu.SMEM((NEAR + FAR,), jnp.int32),
            pltpu.SMEM(win.shape, jnp.int32),
            pltpu.SemaphoreType.DMA((FAR - EARLY,)),
            pltpu.SemaphoreType.DMA,
        ],
        compiler_params=params(14),
        cost_estimate=cost(224 * 2 * 8 * 128 * 128, 8 << 20),
        name="far",
    )(*in_hbm(win), *arrays, near, early, *in_hbm(weights))


def edge_kernel(last, fld_ref, a_ref, b_ref, edge_ref):
    band = lax.axis_index("band")
    a, b = a_ref[...], b_ref[...]
    b = jnp.where((band == 0) | (band == last), jnp.zeros_like(b), b)
    even = band % 2 == 0
    north, south = jnp.where(even, b, a), jnp.where(even, a, b)
    ends = []
    for lanes in (slice(0, 128), slice(COLS - 128, COLS)):
        ends.append(jnp.concatenate([north[:, lanes], fld_ref[:, lanes], south[:, lanes]], axis=0))
    rank = lax.broadcasted_iota(jnp.int32, (16, 256), 0)
    col = lax.broadcasted_iota(jnp.int32, (16, 256), 1)
    pick = ((rank < 2) & (col == rank)) | ((rank >= 2) & (rank < 4) & (col == 252 + rank))
    edge_ref[...] = lax.dot_general(
        jnp.where(pick, 1.0, 0.0).astype(BF),
        jnp.concatenate(ends, axis=1),
        (((1,), (1,)), ((), ())),
        preferred_element_type=F32,
    ).astype(BF)


def edges(n_band, fld, a, b):
    return pl.pallas_call(
        functools.partial(edge_kernel, n_band - 1),
        in_specs=[VM, VM, VM],
        out_specs=VM,
        out_shape=jax.ShapeDtypeStruct((16, (ROWS + 4) * 8), BF),
        compiler_params=params(8),
        cost_estimate=cost(0, 1 << 20),
        name="edges",
    )(fld, a, b)


def spread_kernel(fld_ref, g_ref, hot_ref):
    c = lax.broadcasted_iota(jnp.int32, (COLS, 256), 0)
    lane = lax.broadcasted_iota(jnp.int32, (COLS, 256), 1)
    for tile in range(3):
        n = lane % 128 + tile * 128
        j = jnp.where(n < PAIRS, SUB * (n % SUB) + n // SUB, SUB * (n - PAIRS + 1))
        gap = jnp.where(n < HROWS, c - 2 * j - lane // 128, -COLS)
        for pair in range(2):
            hot = jnp.where(gap == 2 * pair - 2, 1.0, 0.0)
            hot_ref[:, (2 * tile + pair) * 256 : (2 * tile + pair) * 256 + 256] = hot.astype(BF)
    zero = jnp.zeros((16, 256), BF)
    for pair in range(2):
        for tile in range(3):
            at = (2 * tile + pair) * 256
            value = jnp.dot(fld_ref[...], hot_ref[:, at : at + 256], preferred_element_type=F32)
            value = jnp.concatenate([zero, value.astype(BF), zero], axis=0)
            for half in range(2):
                d0 = (2 * pair + half) * 64
                for m in range(BLOCKS):
                    g_ref[m, d0 : d0 + 64, tile * 128 : tile * 128 + 128] = value[
                        48 * m : 48 * m + 64, half * 128 : half * 128 + 128
                    ]


def spread(fld):
    return pl.pallas_call(
        spread_kernel,
        in_specs=[VM],
        out_specs=[VM] * 2,
        out_shape=[
            jax.ShapeDtypeStruct((BLOCKS, 256, LANES), BF),
            jax.ShapeDtypeStruct((COLS, 6 * 256), BF),
        ],
        compiler_params=params(12),
        cost_estimate=cost(2 * 512 * 512 * 1536, 4 << 20),
        name="spread",
    )(fld)


def halos(core_ref, x_ref, left_ref, right_ref):
    even = lax.axis_index("lon") % 2 == 0
    core, x = core_ref[...].astype(F32), x_ref[...].astype(F32)
    right, left = jnp.where(even, core, x), jnp.where(even, x, core)
    hr = lax.broadcasted_iota(jnp.int32, (16, 256), 0)
    hl = lax.broadcasted_iota(jnp.int32, (16, 256), 1)
    for side, base, at, out in ((left, 2, 0, left_ref), (right, 0, SUB - 1, right_ref)):
        hot = ((hl % 128) == at) & (hr == hl // 128 + base)
        value = lax.dot_general(
            side.astype(BF),
            jnp.where(hot, 1.0, 0.0).astype(BF),
            (((0,), (0,)), ((), ())),
            preferred_element_type=F32,
        ).astype(BF)
        for m in range(BLOCKS):
            for half in range(2):
                out[m, half * 64 : half * 64 + 64] = value[
                    48 * m : 48 * m + 64, half * 128 : half * 128 + 128
                ]


def conv_kernel(
    last,
    g_ref,
    core_ref,
    x_ref,
    ws_ref,
    bs_ref,
    wm_ref,
    bm_ref,
    rim,
    out_ref,
    left_ref,
    right_ref,
    hs,
    ys,
    yb,
    sem,
):
    band = lax.axis_index("band")

    def stem(block, which, low, high):
        block_in = jnp.minimum(block, BLOCKS - 1)
        edge = jnp.where(block_in == 0, 0, jnp.where(block_in == BLOCKS - 1, 1, 2))
        x = g_ref[block_in] + rim[edge]
        first = jnp.concatenate([x[:128, :128] + left_ref[block_in], x[128:, :128]], axis=0)
        final = jnp.concatenate([x[:128, 256:], x[128:, 256:] + right_ref[block_in]], axis=0)
        x = jnp.concatenate([first, x[:, 128:256], final], axis=1)[:, :HROWS]
        for i in which:
            t = lax.dot_general(
                x,
                ws_ref[:, i * 256 : i * 256 + 256],
                (((0,), (0,)), ((), ())),
                preferred_element_type=F32,
            )
            t = t + bs_ref[...]
            h = t + t * jnp.tanh(t)
            if i == 0 and low is not None:
                h = h * low
            if i == STEP - 1 and high is not None:
                h = h * high
            hs[block % 2, i] = h.astype(BF)

    halos(core_ref, x_ref, left_ref, right_ref)
    stem(0, range(STEP), jnp.where(band == 0, 0.0, 1.0), None)

    def copy(at, slot):
        return pltpu.make_async_copy(
            yb.at[slot], out_ref.at[pl.ds(6 * at - 2, 6)], sem.at[slot]
        )

    first = pltpu.make_async_copy(yb.at[0, pl.ds(2, 4)], out_ref.at[pl.ds(0, 4)], sem.at[0])

    def step(s, carry):
        slot = s % 2

        @pl.when(s == 2)
        def _():
            first.wait()

        @pl.when(s > 2)
        def _():
            copy(s - 2, slot).wait()

        rows = [(1 - slot, 4), (1 - slot, 5)] + [(slot, i) for i in range(STEP)]
        keep_last = jnp.where((s == BLOCKS - 2) & (band == last), 0.0, 1.0)

        def mix(t):
            for c in range(PAIRS // CHUNK):
                row0 = c * CHUNK

                def both(r):
                    return jnp.concatenate(
                        [hs[rows[2 * t + r]][row0 + k * SUB : row0 + k * SUB + CHUNK] for k in range(2)],
                        axis=1,
                    )

                h = [both(r) for r in range(4)]
                v = [h[0] - h[2], h[1] + h[2], h[2] - h[1], h[1] - h[3]]
                m = [jnp.dot(v[k], wm_ref[k], preferred_element_type=F32) for k in range(4)]
                m[1] = m[1] + jnp.concatenate([bm_ref[...], bm_ref[...]], axis=1)
                plus, minus = m[1] + m[2], m[1] - m[2]
                for q, y in enumerate([plus + m[0], minus - m[3]]):
                    row = 2 * t + q
                    for par in range(2):
                        part = y[:, par * 128 : par * 128 + 128]
                        for k in range(CHUNK // SUB):
                            to = pl.ds(2 * (c * CHUNK // SUB + k) + par, SUB, stride=PITCH)
                            ys[row, to, :] = part[k * SUB : k * SUB + SUB]
            for q in range(2):
                for a in range(SUB):
                    yb[slot, 2 * t + q, 2 * SUB * a : 2 * SUB * a + 2 * SUB] = ys[
                        2 * t + q, PITCH * a : PITCH * a + 2 * SUB
                    ].astype(BF)

        for t in range(STEP // 2):
            mix(t)
        stem(s + 1, range(STEP), None, keep_last)

        @pl.when(s == 0)
        def _():
            first.start()

        @pl.when(s > 0)
        def _():
            copy(s, slot).start()
        return carry

    lax.fori_loop(0, BLOCKS, step, 0)
    copy(BLOCKS - 2, (BLOCKS - 2) % 2).wait()
    copy(BLOCKS - 1, (BLOCKS - 1) % 2).wait()


def conv(n_band, g, core, x, ws, bs, wm, bm, rim):
    channels = bm.shape[-1]
    return pl.pallas_call(
        functools.partial(conv_kernel, n_band - 1),
        in_specs=[VM] * 8,
        out_specs=ANY,
        out_shape=jax.ShapeDtypeStruct((ROWS, COLS, channels), BF),
        scratch_shapes=[
            pltpu.VMEM((BLOCKS, 128, 128), BF),
            pltpu.VMEM((BLOCKS, 128, 128), BF),
            pltpu.VMEM((2, STEP, HROWS, 256), BF),
            pltpu.VMEM((STEP, (SUB + 1) * PITCH + 7, channels), F32),
            pltpu.VMEM((2, STEP, COLS, channels), BF),
            pltpu.SemaphoreType.DMA((2,)),
        ],
        compiler_params=params(20),
        cost_estimate=cost(2 * ROWS * COLS * 9 * 128 * 128, 12 << 20),
        name="conv",
    )(g, core, x, ws, bs, wm, bm, rim)


def on_device(source, routes, slot_weights, window, stem_weight, stem_bias, mix_weight, mix_bias):
    n_band = lax.axis_size("band")
    n_lon = lax.axis_size("lon")
    axes = ("band", "lon")

    def move(value, way, turn):
        return lax.ppermute(value, axes, swap(n_band, n_lon, way, turn))

    own, to_core, to_x, to_a, to_ax, to_b, to_bx = pack(routes.T, source)
    win = window.transpose(1, 0, 2)
    core = move(to_core, "", "core")
    bx, ax = move(to_bx, "b", "x"), move(to_ax, "a", "x")
    x_both, a_both, b_both, far = merge(core, to_x, to_a, to_b)
    x, a, b = move(x_both, "", "x"), move(a_both, "a", "stay"), move(b_both, "b", "stay")
    arrays = [x, a, ax, move(far, "a", "x_rim"), b, bx]
    near, early = near_part(n_band, win, own, core, x, slot_weights)
    fld, a_row, b_row = far_part(n_band, win, arrays, near, early, slot_weights)
    a_halo = move(a_row, "a", "stay")
    b_halo = move(b_row, "b", "stay")
    g, hot = spread(fld)
    a_halo, b_halo, g, hot = lax.optimization_barrier((a_halo, b_halo, g, hot))
    edge = edges(n_band, fld, a_halo, b_halo)
    core_edge = move(edge, "", "core")
    x_edge = move(edge, "", "x")
    ws, bs, wm, rim = prep(n_band, stem_weight, stem_bias, mix_weight, a_halo, b_halo, hot)
    return conv(n_band, g, core_edge, x_edge, ws, bs, wm, mix_bias[None], rim)


def solution(mesh):
    both = ("band", "lon")
    in_specs = (
        P(both, None, None),
        P(both, None),
        P(both, None, None, None, None),
        P(both, None, None),
        P(),
        P(),
        P(),
        P(),
    )
    return jax.shard_map(
        on_device, mesh=mesh, in_specs=in_specs, out_specs=P("band", "lon", None), check_vma=False
    )
```
